256 devices in a mesh: ha: 16 (over y, x_lo, core), wa: 8 (over z), dp: 2 (over x_hi).
Axes of the slice: x: 4 (x_hi: 2, x_lo: 2; x = x_hi * 2 + x_lo), y: 4, z: 8, core: 2. Of those that a mesh axis runs over, the one named last changes fastest.
Arguments:
- tokens: bfloat16 [8, 224, 56, 384], P('dp', 'ha', 'wa'), may hold values from -6 to 6
- grad_out: bfloat16 [8, 224, 56, 384], P('dp', 'ha', 'wa'), may hold values from -6 to 6
- gain_first: float32 [384], replicated, may hold values from 0.5 to 1.5
- gain_second: float32 [384], replicated, may hold values from 0.5 to 1.5
- w_qkv: bfloat16 [1152, 384], replicated, may hold values from -0.3125 to 0.3125
- w_proj: bfloat16 [384, 384], replicated, may hold values from -0.3125 to 0.3125
- w_up: bfloat16 [1536, 384], replicated, may hold values from -0.3125 to 0.3125
- w_down: bfloat16 [384, 1536], replicated, may hold values from -0.15625 to 0.15625
Outputs:
- grad_tokens: bfloat16 [8, 224, 56, 384], P('dp', 'ha', 'wa')
- grad_qkv: float32 [1152, 384], P('ha', 'wa')
- grad_proj: float32 [384, 384], P('ha', 'wa')
- grad_up: float32 [1536, 384], P('ha', 'wa')
- grad_down: float32 [384, 1536], P('ha', 'wa')
- grad_gain_first: float32 [384], replicated
- grad_gain_second: float32 [384], replicated
The draws below stay inside these ranges and needn't reach their ends.
All inputs are finite; a program needn't handle non-finite values.
Results may differ from the reference program's by a relative error of at most 0.033.
Values may be sent and summed in bfloat16 or wider, within the bound.
No kernel may reach another device: no remote copies, remote signals or barrier semaphores. Data moves between devices by JAX's collectives and lax.ppermute only.
A program may use at most 64 MiB of HBM per device.

```python
import jax
import jax.numpy as jnp
from jax import lax

C = 384
HEADS = 12
FF = 1536
GRID = 7
CROPS = 8
HEIGHT = 224
WIDTH = 56


def strengthened(array, stream_key, source, target, blocks, factor):
    owner, partner = [(jnp.arange(array.shape[dim]) // (array.shape[dim] // blocks)).reshape([-1 if axis == dim else 1 for axis in range(array.ndim)]) for dim in (source, target)]
    chosen = jax.random.permutation(stream_key, blocks)[partner]
    strong = (owner == chosen) | (owner == (partner + blocks // 2) % blocks)
    return jnp.where(strong, factor * array, array)


def level_of(key, dims, pieces, smallest, top_value):
    def one(dim, blocks):
        draws = jax.random.uniform(jax.random.fold_in(jax.random.fold_in(key, 6), dim), (blocks,), jnp.float32, smallest / len(pieces), top_value / len(pieces))
        return jnp.repeat(jnp.exp(draws), dims[dim] // blocks).reshape((-1,) + (1,) * (len(dims) - dim - 1))

    factor_of = one(*pieces[0])
    for cut in pieces[1:]:
        factor_of = factor_of * one(*cut)
    return factor_of


def centred(key, dims, spread, bound, cuts=(), dtype=jnp.bfloat16):
    factor_of = level_of(key, dims, cuts, -0.22, 0.18) if cuts else 1.0
    values = jax.random.normal(key, dims, jnp.float32) * spread * factor_of
    return jnp.minimum(jnp.maximum(values, -bound), bound).astype(dtype)


def heavy_noise(stream_key, dims, deviation, reach, pieces, heavy, held_as=jnp.bfloat16):
    entries = deviation * jax.random.normal(stream_key, dims, jnp.float32)
    if pieces:
        entries = entries * level_of(stream_key, dims, pieces, -0.22, 0.18)
    return jnp.clip(strengthened(entries, jax.random.fold_in(stream_key, 3), *heavy), -reach, reach).astype(held_as)


def setup_inputs(seed: int = 0) -> dict:
    keys = jax.random.split(jax.random.key(seed), 9)
    return {
        "tokens": centred(keys[0], (CROPS, HEIGHT, WIDTH, C), 1.0, 6.0, ((0, 2), (1, 16), (2, 8))),
        "grad_out": heavy_noise(keys[1], (CROPS, HEIGHT, WIDTH, C), 1.0, 6.0, ((0, 2), (1, 16), (2, 8)), (1, 3, 16, 2.0)),
        "gain_first": jnp.clip(1.0 + 0.1 * jax.random.normal(keys[2], (C,), jnp.float32), 0.5, 1.5),
        "gain_second": jnp.clip(1.0 + 0.1 * jax.random.normal(keys[3], (C,), jnp.float32), 0.5, 1.5),
        "w_qkv": centred(keys[4], (3 * C, C), C ** -0.5, 0.3125),
        "w_proj": centred(keys[5], (C, C), C ** -0.5, 0.3125),
        "w_up": centred(keys[6], (FF, C), C ** -0.5, 0.3125),
        "w_down": centred(keys[7], (C, FF), FF ** -0.5, 0.15625),
    }


EPSILON = 1e-05

def contract(form, left, right):
    return jnp.einsum(form, left.astype(jnp.float32), right.astype(jnp.float32))

def norm_forward(values, gain):
    values_f = values.astype(jnp.float32)
    centered = values_f - lax.optimization_barrier(jnp.mean(values_f, axis=-1, keepdims=True))
    inv_std = lax.rsqrt(lax.optimization_barrier(jnp.mean(centered * centered, axis=-1, keepdims=True)) + EPSILON)
    normal_hat = centered * inv_std
    return ((normal_hat * gain).astype(jnp.bfloat16), normal_hat, inv_std)

def norm_backward(grad_norm, normal_hat, inv_std, gain):
    grad_float = grad_norm.astype(jnp.float32)
    grad_hat = grad_float * gain
    first_mean = lax.optimization_barrier(jnp.mean(grad_hat, axis=-1, keepdims=True))
    second_mean = lax.optimization_barrier(jnp.mean(grad_hat * normal_hat, axis=-1, keepdims=True))
    return (inv_std * (grad_hat - first_mean - normal_hat * second_mean), lax.optimization_barrier(jnp.sum(grad_float * normal_hat, axis=0)))

def linear(activations, weight):
    return jnp.dot(activations, weight.T, preferred_element_type=jnp.float32)

def linear_back(gradient, weight):
    return jnp.dot(gradient, weight, preferred_element_type=jnp.float32)

def weight_grad(gradient, activations):
    return jnp.dot(gradient.T, activations, preferred_element_type=jnp.float32)

def split_heads(qkv_rows):
    token_count, triple = qkv_rows.shape
    return qkv_rows.reshape(token_count // (GRID * GRID), GRID * GRID, 3, HEADS, triple // (3 * HEADS))

def attention_forward(normed, w_qkv):
    token_count, channels = normed.shape
    qkv_rows = linear(normed, w_qkv).astype(jnp.bfloat16)
    heads_view = split_heads(qkv_rows)
    scale = (channels // HEADS) ** (-0.5)
    scores = contract('gqhd,gkhd->ghqk', heads_view[:, :, 0], heads_view[:, :, 1]) * scale
    expo_scores = jnp.exp(scores)
    probs_float = expo_scores / lax.optimization_barrier(jnp.sum(expo_scores, axis=-1, keepdims=True))
    probs_round = probs_float.astype(jnp.bfloat16)
    mixed = contract('ghqk,gkhd->gqhd', probs_round, heads_view[:, :, 2])
    return (qkv_rows, probs_float, probs_round, mixed.astype(jnp.bfloat16).reshape(token_count, channels))

def attention_backward(grad_resid, normed, qkv_rows, probs_float, probs_round, mixed, w_qkv, w_proj):
    token_count, channels = grad_resid.shape
    grad_mixed = linear_back(grad_resid, w_proj).astype(jnp.bfloat16)
    heads_view = split_heads(qkv_rows)
    scale = (channels // HEADS) ** (-0.5)
    grad_heads = grad_mixed.reshape(token_count // (GRID * GRID), GRID * GRID, HEADS, channels // HEADS)
    grad_probs = contract('gqhd,gkhd->ghqk', grad_heads, heads_view[:, :, 2])
    grad_value = contract('ghqk,gqhd->gkhd', probs_round, grad_heads)
    centre = lax.optimization_barrier(jnp.sum(grad_probs * probs_float, axis=-1, keepdims=True))
    grad_scores = (probs_float * (grad_probs - centre) * scale).astype(jnp.bfloat16)
    grad_query = contract('ghqk,gkhd->gqhd', grad_scores, heads_view[:, :, 1])
    grad_key = contract('ghqk,gqhd->gkhd', grad_scores, heads_view[:, :, 0])
    grad_rows = jnp.stack([grad_query, grad_key, grad_value], axis=2).astype(jnp.bfloat16).reshape(token_count, 3 * channels)
    grad_normed = linear_back(grad_rows, w_qkv).astype(jnp.bfloat16)
    return (grad_normed, weight_grad(grad_rows, normed), weight_grad(grad_resid, mixed))

def mlp_backward(resid, grad_out, gain_second, w_up, w_down):
    normed, normal_hat, inv_std = norm_forward(resid, gain_second)
    hidden = linear(normed, w_up)
    activated, gelu_back = jax.vjp(jax.nn.gelu, hidden)
    activated = activated.astype(jnp.bfloat16)
    grad_act = linear_back(grad_out, w_down)
    grad_hidden = gelu_back(grad_act)[0].astype(jnp.bfloat16)
    grad_normed = linear_back(grad_hidden, w_up)
    grad_float, grad_gain = norm_backward(grad_normed, normal_hat, inv_std, gain_second)
    grad_resid = (grad_out.astype(jnp.float32) + grad_float).astype(jnp.bfloat16)
    return (grad_resid, weight_grad(grad_hidden, normed), weight_grad(grad_out, activated), grad_gain)

def block_backward(tokens, grad_out, gain_first, gain_second, w_qkv, w_proj, w_up, w_down):
    normed, normal_hat, inv_std = norm_forward(tokens, gain_first)
    qkv_rows, probs_float, probs_round, mixed = attention_forward(normed, w_qkv)
    branch = linear(mixed, w_proj).astype(jnp.bfloat16)
    resid = (tokens.astype(jnp.float32) + branch.astype(jnp.float32)).astype(jnp.bfloat16)
    grad_resid, grad_up, grad_down, gain_two = mlp_backward(resid, grad_out, gain_second, w_up, w_down)
    grad_normed, grad_qkv, grad_proj = attention_backward(grad_resid, normed, qkv_rows, probs_float, probs_round, mixed, w_qkv, w_proj)
    grad_float, gain_one = norm_backward(grad_normed, normal_hat, inv_std, gain_first)
    grad_tokens = (grad_resid.astype(jnp.float32) + grad_float).astype(jnp.bfloat16)
    return (grad_tokens, (grad_qkv, grad_proj, grad_up, grad_down, gain_one, gain_two))

def reference(tokens, grad_out, gain_first, gain_second, w_qkv, w_proj, w_up, w_down):
    spacing_h = HEIGHT // GRID
    spacing_w = WIDTH // GRID

    def to_grid(crop):
        return crop.reshape(GRID, spacing_h, GRID, spacing_w, C).transpose(1, 3, 0, 2, 4).reshape(-1, C)

    def one_crop(members):
        crop_tok, crop_grad = members
        grad_grid, partial_value = block_backward(to_grid(crop_tok), to_grid(crop_grad), gain_first, gain_second, w_qkv, w_proj, w_up, w_down)
        restored = grad_grid.reshape(spacing_h, spacing_w, GRID, GRID, C).transpose(2, 0, 3, 1, 4).reshape(HEIGHT, WIDTH, C)
        return (restored, partial_value)
    grad_tokens, partials = lax.map(one_crop, (tokens, grad_out))
    factor = (CROPS * HEIGHT * WIDTH) ** (-0.5)
    totals = [lax.optimization_barrier(jnp.sum(member, axis=0)) * factor for member in partials]
    return (grad_tokens, totals[0], totals[1], totals[2], totals[3], totals[4], totals[5])
```

```python
import functools

import jax
import jax.numpy as jnp
from jax import lax
from jax.experimental import pallas as pl
from jax.experimental.pallas import tpu as pltpu
from jax.sharding import Mesh, PartitionSpec as P

HEADS = 12
GRID = 7
EPSILON = 1e-05
SLOTS = 128
ROWS = 64
LINES = 14
QUAD = 4
F32 = jnp.float32
BF16 = jnp.bfloat16
HA = ("y", "xl", "core")


def dot(left, right):
    return jnp.dot(left, right, preferred_element_type=F32)


def dot_nt(left, right):
    return lax.dot_general(left, right, (((1,), (1,)), ((), ())), preferred_element_type=F32)


def dot_tn(left, right):
    return lax.dot_general(left, right, (((0,), (0,)), ((), ())), preferred_element_type=F32)


def iota(shape, dim):
    return lax.broadcasted_iota(jnp.int32, shape, dim)


def position():
    rows = (lax.axis_index("y") * 2 + lax.axis_index("xl")) * 2 + lax.axis_index("core")
    return rows, lax.axis_index("wa")


def group_match(slot, member):
    row, col = position()
    parity, local = member >> 6, member & 63
    band_row = (local * 37) >> 8
    band_col = local - GRID * band_row
    offset_row = row + 16 * parity + 32 * band_row - LINES * (slot >> 3)
    offset_col = col + 8 * band_col - GRID * (slot & 7)
    hit = jnp.logical_and(offset_row >= 0, offset_row < LINES)
    hit = jnp.logical_and(hit, jnp.logical_and(offset_col >= 0, offset_col < GRID))
    return jnp.logical_and(hit, local < GRID * GRID)


def owner_slot(line, column):
    row, col = position()
    return ((LINES * row + line) & 15) * 8 + ((GRID * col + column) & 7)


def one_hot(hit):
    return jnp.where(hit, 1.0, 0.0).astype(BF16)


def norm_parts(values):
    centered = values - jnp.mean(values, axis=-1, keepdims=True)
    inv_std = lax.rsqrt(jnp.mean(centered * centered, axis=-1, keepdims=True) + EPSILON)
    return centered * inv_std, inv_std


def norm_back(grad, normal_hat, inv_std, gain):
    grad_hat = grad * gain
    first = jnp.mean(grad_hat, axis=-1, keepdims=True)
    second = jnp.mean(grad_hat * normal_hat, axis=-1, keepdims=True)
    return inv_std * (grad_hat - first - normal_hat * second)


def head_mask(shape):
    return (iota(shape, 0) >> 6) == (iota(shape, 1) >> 5)


def spread(values, mask):
    tiled = jnp.concatenate([values] * QUAD, axis=0)
    return jnp.where(mask, tiled, jnp.zeros_like(tiled))


def gather_heads(values):
    lanes = iota((ROWS, 128), 1) >> 5
    total = jnp.where(lanes == 0, values[:ROWS], 0.0)
    for head in range(1, QUAD):
        total = total + jnp.where(lanes == head, values[head * ROWS : (head + 1) * ROWS], 0.0)
    return total


def probabilities(key, query_spread, scale):
    scores = dot_nt(key, query_spread) * scale
    expo = jnp.where(iota(scores.shape, 0) < GRID * GRID, jnp.exp(scores), 0.0)
    return expo * (1.0 / jnp.sum(expo, axis=0, keepdims=True))


def load_every(ref, start, step):
    parts = [ref[part, pl.ds(start, SLOTS, stride=step), :] for part in range(3)]
    return jnp.concatenate(parts, axis=1).astype(BF16)


def store_every(ref, start, step, values):
    for part in range(3):
        ref[part, pl.ds(start, SLOTS, stride=step), :] = values[:, part * 128 : (part + 1) * 128]


def send_kernel(tokens_hbm, grad_hbm, out_ref, tokens_ref, grad_ref, sems):
    copies = [
        pltpu.make_async_copy(tokens_hbm, tokens_ref, sems.at[0]),
        pltpu.make_async_copy(grad_hbm, grad_ref, sems.at[1]),
    ]
    for copy in copies:
        copy.start()
    for copy in copies:
        copy.wait()
    for line in range(16):
        for column in range(8):
            slot = owner_slot(line, column)
            if line < LINES and column < GRID:
                unit = jnp.concatenate(
                    [tokens_ref[line, column].astype(F32), grad_ref[line, column].astype(F32)], axis=0
                ).astype(BF16)
            else:
                unit = jnp.zeros((8, 384), BF16)
            out_ref[slot] = unit


def return_kernel(recv_ref, out_ref):
    for line in range(LINES):
        for column in range(GRID):
            out_ref[line, column] = recv_ref[owner_slot(line, column)]


def gelu_parts(hidden, grad):
    inner = 0.7978845608028654
    square = hidden * hidden
    tanh = jnp.tanh(inner * (hidden + 0.044715 * (hidden * square)))
    half = 0.5 * (1.0 + tanh)
    slope = half + 0.5 * hidden * (1.0 - tanh * tanh) * (
        inner * (1.0 + 3 * 0.044715 * square)
    )
    return hidden * half, grad * slope


def forward_kernel(
    recv_ref, gain_one, w_qkv, w_proj,
    x_ref, qkv_ref, mixed_ref, resid_ref, grad_ref, arrived, normed,
):
    for part in range(3):
        arrived[part] = recv_ref[:, part * 128 : (part + 1) * 128].astype(F32)
    match = one_hot(group_match(iota((SLOTS, SLOTS), 1), iota((SLOTS, SLOTS), 0)))
    for crop in range(4):
        rows = pl.ds(crop * SLOTS, SLOTS)
        x = dot(match, load_every(arrived, crop, 8))
        x_ref[rows, :] = x.astype(BF16)
        normal_hat, _ = norm_parts(x)
        normed[rows, :] = (normal_hat * gain_one[...]).astype(BF16)
        grad_ref[rows, :] = dot(match, load_every(arrived, crop + 4, 8)).astype(BF16)
    for part in range(3):
        cols = pl.ds(part * 384, 384)
        qkv_ref[:, cols] = dot_nt(normed[...], w_qkv[cols, :]).astype(BF16)
    mask = head_mask((QUAD * ROWS, 128))
    scale = 32.0 ** -0.5

    @pl.loop(0, 4)
    def _(pair):
        units = unit_places(pair)
        query = [spread(qkv_ref[rows, pl.ds(lane, 128)], mask) for rows, lane in units]
        probs = [
            probabilities(qkv_ref[rows, pl.ds(384 + lane, 128)], query[n], scale).astype(BF16)
            for n, (rows, lane) in enumerate(units)
        ]
        mixed = [
            dot_tn(probs[n], qkv_ref[rows, pl.ds(768 + lane, 128)])
            for n, (rows, lane) in enumerate(units)
        ]
        for n, (rows, lane) in enumerate(units):
            mixed_ref[rows, pl.ds(lane, 128)] = gather_heads(mixed[n]).astype(BF16)

    for crop in range(4):
        rows = pl.ds(crop * SLOTS, SLOTS)
        branch = dot_nt(mixed_ref[rows, :], w_proj[...]).astype(BF16)
        resid_ref[rows, :] = (x_ref[rows, :].astype(F32) + branch.astype(F32)).astype(BF16)


def unit_places(pair):
    places = []
    for half in range(2):
        rows = pl.ds(pl.multiple_of(pair * 2 * ROWS + half * ROWS, ROWS), ROWS)
        places.extend((rows, quad * 128) for quad in range(3))
    return places


def mlp_kernel(
    grad_out, resid, gain_two, w_up, w_down,
    resid_grad_ref, keep_ref, send_ref, gain_ref,
    normed, hidden_grad, grad_turned, up_total, down_total, back, piece_rows,
):
    for crop in range(4):
        rows = pl.ds(crop * SLOTS, SLOTS)
        normal_hat, _ = norm_parts(resid[rows, :].astype(F32))
        normed[rows, :] = (normal_hat * gain_two[...]).astype(BF16)
        grad_turned[:, rows] = grad_out[rows, :].astype(F32).T.astype(BF16)
    back[...] = jnp.zeros_like(back)

    @pl.loop(0, 4)
    def _(chunk):
        cols = pl.ds(pl.multiple_of(chunk * 384, 384), 384)
        hidden = dot_nt(normed[...], w_up[cols, :])
        grad_act = dot(grad_out[...], w_down[:, cols])
        activated, grad_hidden = gelu_parts(hidden, grad_act)
        hidden_grad[...] = grad_hidden.astype(BF16)
        down_total[:, cols] = dot(grad_turned[...], activated.astype(BF16))
        up_total[cols, :] = dot_tn(hidden_grad[...], normed[...])
        back[...] += dot(hidden_grad[...], w_up[cols, :])

    for ref, side in piece_sides(keep_ref, send_ref):
        for piece in range(8):
            owner = 2 * piece + side
            piece_rows[:96, :] = up_total[pl.ds(pl.multiple_of(owner * 96, 8), 96), :]
            for part in range(4):
                piece_rows[96 + 24 * part : 120 + 24 * part, :] = down_total[
                    pl.ds(pl.multiple_of(owner * 24, 8), 24), part * 384 : (part + 1) * 384
                ]
            ref[piece] = piece_rows[...].astype(BF16)
    gain = jnp.zeros((1, 384), F32)
    for crop in range(4):
        rows = pl.ds(crop * SLOTS, SLOTS)
        normal_hat, inv_std = norm_parts(resid[rows, :].astype(F32))
        grad = back[rows, :]
        gain = gain + jnp.sum(grad * normal_hat, axis=0, keepdims=True)
        resid_grad_ref[rows, :] = (
            grad_out[rows, :].astype(F32) + norm_back(grad, normal_hat, inv_std, gain_two[...])
        ).astype(BF16)
    gain_ref[...] = gain


def piece_sides(keep_ref, send_ref):
    core = lax.axis_index("core")
    return (keep_ref, core), (send_ref, 1 - core)


def attention_kernel(
    x_ref, qkv_ref, resid_grad_ref, gain_one, w_qkv, w_proj,
    out_ref, rows_grad, normed_ref, gain_ref, grad_mixed, slots,
):
    grad_mixed[...] = dot(resid_grad_ref[...], w_proj[...]).astype(BF16)
    mask = head_mask((QUAD * ROWS, 128))
    scale = 32.0 ** -0.5

    @pl.loop(0, 4)
    def _(pair):
        units = unit_places(pair)
        count = range(len(units))
        query = [spread(qkv_ref[rows, pl.ds(lane, 128)], mask) for rows, lane in units]
        grad = [spread(grad_mixed[rows, pl.ds(lane, 128)], mask) for rows, lane in units]
        key = [qkv_ref[rows, pl.ds(384 + lane, 128)] for rows, lane in units]
        probs = [probabilities(key[n], query[n], scale) for n in count]
        grad_probs = [
            dot_nt(qkv_ref[rows, pl.ds(768 + lane, 128)], grad[n])
            for n, (rows, lane) in enumerate(units)
        ]
        grad_scores = []
        for n in count:
            centre = jnp.sum(grad_probs[n] * probs[n], axis=0, keepdims=True)
            grad_scores.append((probs[n] * (grad_probs[n] - centre) * scale).astype(BF16))
        for n, (rows, lane) in enumerate(units):
            rows_grad[rows, pl.ds(768 + lane, 128)] = dot(probs[n].astype(BF16), grad[n]).astype(BF16)
            rows_grad[rows, pl.ds(384 + lane, 128)] = dot(grad_scores[n], query[n]).astype(BF16)
            rows_grad[rows, pl.ds(lane, 128)] = gather_heads(
                dot_tn(grad_scores[n], key[n])
            ).astype(BF16)

    match = one_hot(group_match(iota((SLOTS, SLOTS), 0), iota((SLOTS, SLOTS), 1)))
    gain = jnp.zeros((1, 384), F32)
    for crop in range(4):
        rows = pl.ds(crop * SLOTS, SLOTS)
        grad = dot(rows_grad[rows, :], w_qkv[...]).astype(BF16).astype(F32)
        normal_hat, inv_std = norm_parts(x_ref[rows, :].astype(F32))
        normed_ref[rows, :] = (normal_hat * gain_one[...]).astype(BF16)
        gain = gain + jnp.sum(grad * normal_hat, axis=0, keepdims=True)
        grad_x = resid_grad_ref[rows, :].astype(F32) + norm_back(
            grad, normal_hat, inv_std, gain_one[...]
        )
        store_every(slots, crop, 4, dot(match, grad_x.astype(BF16)))
    for slot in range(SLOTS):
        for part in range(3):
            out_ref[slot, :, part * 128 : (part + 1) * 128] = slots[
                part, slot * 4 : slot * 4 + 4, :
            ].astype(BF16)
    gain_ref[...] = gain


def weight_kernel(
    rows_grad, normed, resid_grad, mixed, first, second, keep_ref, send_ref,
    qkv_total, proj_total, piece_rows,
):
    for part in range(3):
        cols = pl.ds(part * 384, 384)
        qkv_total[cols, :] = dot_tn(rows_grad[:, cols], normed[...])
    proj_total[...] = dot_tn(resid_grad[...], mixed[...])
    piece_rows[96:, :] = jnp.zeros((16, 384), F32)
    piece_rows[96:97, :] = first[...]
    piece_rows[97:98, :] = second[...]
    for ref, side in piece_sides(keep_ref, send_ref):
        for piece in range(8):
            owner = 2 * piece + side
            piece_rows[:72, :] = qkv_total[pl.ds(pl.multiple_of(owner * 72, 8), 72), :]
            piece_rows[72:96, :] = proj_total[pl.ds(pl.multiple_of(owner * 24, 8), 24), :]
            ref[piece] = piece_rows[...].astype(BF16)


def core_kernel(early_keep, early_recv, late_keep, late_recv, *outs):
    row = lax.axis_index("y")
    for step in range(4):
        place = (row + step) & 3
        for col in range(2):
            piece = place * 2 + col
            outs[step][col, :192] = (
                early_keep[piece].astype(F32) + early_recv[piece].astype(F32)
            ).astype(BF16)
            outs[step][col, 192:] = (
                late_keep[piece].astype(F32) + late_recv[piece].astype(F32)
            ).astype(BF16)


def pack_columns(rows, col):
    low = pltpu.roll(rows[:48], (384 - 48 * col) % 384, 1)[:, :128]
    high = pltpu.roll(rows[48:96], (384 + 64 - 48 * col) % 384, 1)[:, :128]
    return jnp.where(iota((48, 128), 1) < 64, low, high)


def pack_kernel(own, one, two, three, out_ref, gains):
    row = lax.axis_index("y")
    for step, ref in enumerate((own, one, two, three)):
        gains[(row - step) & 3] = ref[0, 288:].astype(F32)
    gain = (gains[0] + gains[1]) + (gains[2] + gains[3])
    gain_rows = [
        gain[which : which + 1, part * 128 : (part + 1) * 128]
        for which in range(2)
        for part in range(3)
    ]
    gain_rows.append(jnp.zeros((2, 128), F32))
    for side in range(2):
        total = own[side, :288].astype(F32) + one[side, :288].astype(F32)
        total = total + (two[side, :288].astype(F32) + three[side, :288].astype(F32))
        for col in range(8):
            start = 96 + 24 * (col // 2)
            block = total[start : start + 24]
            if col % 2:
                block = pltpu.roll(block, 192, 1)
            out_ref[side * 8 + col] = jnp.concatenate(
                [pack_columns(total[:96], col), block[:, :128], block[:, 128:256]]
                + [pack_columns(total[192:], col)] + gain_rows,
                axis=0,
            ).astype(BF16)


def block_sum(recv_ref, out_ref):
    total = recv_ref[0].astype(F32)
    for place in range(1, 16):
        total = total + recv_ref[place].astype(F32)
    out_ref[...] = total.astype(BF16)


def unpack_columns(packed):
    low = packed[:, :48]
    high = pltpu.roll(packed, 64, 1)[:, :48]
    wide = jnp.concatenate([low, high], axis=0)
    wide = jnp.concatenate([wide, jnp.zeros((96, 80), F32)], axis=1)
    wide = jnp.concatenate([wide, jnp.zeros((32, 128), F32)], axis=0)
    return wide.T[:48]


def final_weights(
    own_ref, other_ref,
    qkv_ref, proj_ref, up_ref, down_ref, first_ref, second_ref, factor,
):
    total = (own_ref[...].astype(F32) + other_ref[...].astype(F32)) * factor
    early, late = total[:96], total[96:]
    up_ref[...] = unpack_columns(early[:48])[:, :96]
    down_ref[:, :128] = early[48:72]
    down_ref[:, 128:] = early[72:96, :64]
    qkv_ref[...] = unpack_columns(late[:48])[:, :72]
    proj_ref[...] = pltpu.roll(late[:48], 64, 1)[24:48, :48]
    for part in range(3):
        lane = pl.ds(part * 128, 128)
        first_ref[lane] = late[48 + part]
        second_ref[lane] = late[51 + part]


def call(kernel, outs, scratch=(), flops=0, nbytes=0, space=pltpu.VMEM):
    vmem = pl.BlockSpec(memory_space=pltpu.VMEM)
    scratch = [pltpu.VMEM(*item) if isinstance(item, tuple) else item for item in scratch]

    def run(*args):
        return pl.pallas_call(
            kernel,
            out_shape=[jax.ShapeDtypeStruct(shape, dtype) for shape, dtype in outs],
            in_specs=[pl.BlockSpec(memory_space=space)] * len(args),
            out_specs=[vmem] * len(outs),
            scratch_shapes=scratch,
            compiler_params=pltpu.CompilerParams(vmem_limit_bytes=24 << 20),
            cost_estimate=pl.CostEstimate(flops=flops, bytes_accessed=nbytes, transcendentals=0),
        )(*args)

    return run


def exchange(values, axes):
    return lax.all_to_all(values, axes, split_axis=0, concat_axis=0, tiled=True)


def swap(values, axis):
    return lax.ppermute(values, axis, [(0, 1), (1, 0)])


def body(tokens, grad_out, gain_first, gain_second, w_qkv, w_proj, w_up, w_down):
    gain_one, gain_two = gain_first.reshape(1, 384), gain_second.reshape(1, 384)
    factor = (8 * 224 * 56) ** -0.5
    tile = pltpu.VMEM((LINES, GRID, 4, 384), BF16)
    (sent,) = call(
        send_kernel,
        [((SLOTS, 8, 384), BF16)],
        [tile, tile, pltpu.SemaphoreType.DMA((2,))],
        nbytes=2 * 10**6,
        space=pltpu.HBM,
    )(
        tokens.transpose(1, 2, 0, 3), grad_out.transpose(1, 2, 0, 3)
    )
    arrived = exchange(sent, HA + ("wa",)).reshape(SLOTS * 8, 384)
    rows = ((512, 384), BF16)
    x, qkv, mixed, resid, grad_rows = call(
        forward_kernel,
        [rows, ((512, 1152), BF16), rows, rows, rows],
        [((3, 1024, 128), F32), rows],
        flops=10**9, nbytes=4 * 10**6,
    )(arrived, gain_one, w_qkv, w_proj)
    resid_grad, early_keep, early_send, gain_sum_two = call(
        mlp_kernel,
        [rows, ((8, 192, 384), BF16), ((8, 192, 384), BF16), ((1, 384), F32)],
        [
            rows, rows, ((384, 512), BF16), ((1536, 384), F32), ((384, 1536), F32),
            ((512, 384), F32), ((192, 384), F32),
        ],
        flops=3 * 10**9, nbytes=6 * 10**6,
    )(grad_rows, resid, gain_two, w_up, w_down)
    slots, rows_grad, normed, gain_sum_one = call(
        attention_kernel,
        [((SLOTS, 4, 384), BF16), ((512, 1152), BF16), rows, ((1, 384), F32)],
        [rows, ((3, 512, 128), F32)],
        flops=6 * 10**9, nbytes=20 * 10**6,
    )(x, qkv, resid_grad, gain_one, w_qkv, w_proj)
    returned = exchange(slots, HA + ("wa",))
    late_keep, late_send = call(
        weight_kernel,
        [((8, 112, 384), BF16), ((8, 112, 384), BF16)],
        [((1152, 384), F32), ((384, 384), F32), ((112, 384), F32)],
        flops=10**9, nbytes=5 * 10**6,
    )(rows_grad, normed, resid_grad, mixed, gain_sum_one, gain_sum_two)
    piece = ((2, 304, 384), BF16)
    own, *others = call(core_kernel, [piece] * 4, nbytes=10**7)(
        early_keep, swap(early_send, "core"), late_keep, swap(late_send, "core")
    )
    arrived = [
        lax.ppermute(values, "y", [(place, (place + step) % 4) for place in range(4)])
        for step, values in zip((1, 2, 3), others)
    ]
    (blocks,) = call(
        pack_kernel, [((16, 152, 128), BF16)], [((4, 16, 384), F32)], nbytes=3 * 10**6
    )(own, *arrived)
    blocks, returned = lax.optimization_barrier((blocks, returned))
    (total,) = call(block_sum, [((152, 128), BF16)], nbytes=10**6)(exchange(blocks, ("xl", "wa")))
    other = swap(total, "dp")
    grad_qkv, grad_proj, grad_up, grad_down, first, second = call(
        functools.partial(final_weights, factor=factor),
        [
            ((48, 72), F32), ((24, 48), F32), ((48, 96), F32), ((24, 192), F32),
            ((384,), F32), ((384,), F32),
        ],
        nbytes=10**6,
    )(total, other)
    (grad_tile,) = call(return_kernel, [((LINES, GRID, 4, 384), BF16)], nbytes=10**6)(returned)
    return (
        grad_tile.transpose(2, 0, 1, 3), grad_qkv.T, grad_proj, grad_up.T, grad_down, first, second,
    )


def solution(mesh):
    fine = Mesh(mesh.devices.reshape(4, 2, 2, 8, 2), HA + ("wa", "dp"))
    tile = P("dp", HA, "wa", None)
    block = P(HA, "wa")
    return jax.shard_map(
        body,
        mesh=fine,
        in_specs=(tile, tile, P(), P(), P(), P(), P(), P()),
        out_specs=(tile, block, block, block, block, P(), P()),
        check_vma=False,
    )
```

```python
import functools

import jax
import jax.numpy as jnp
from jax import lax
from jax.experimental import pallas as pl
from jax.experimental.pallas import tpu as pltpu
from jax.sharding import Mesh, PartitionSpec as P

HEADS = 12
GRID = 7
EPSILON = 1e-05
SLOTS = 128
ROWS = 64
LINES = 14
QUAD = 4
F32 = jnp.float32
BF16 = jnp.bfloat16
HA = ("y", "xl", "core")


def dot(left, right):
    return jnp.dot(left, right, preferred_element_type=F32)


def dot_nt(left, right):
    return lax.dot_general(left, right, (((1,), (1,)), ((), ())), preferred_element_type=F32)


def dot_tn(left, right):
    return lax.dot_general(left, right, (((0,), (0,)), ((), ())), preferred_element_type=F32)


def iota(shape, dim):
    return lax.broadcasted_iota(jnp.int32, shape, dim)


def position():
    rows = (lax.axis_index("y") * 2 + lax.axis_index("xl")) * 2 + lax.axis_index("core")
    return rows, lax.axis_index("wa")


def group_match(slot, member):
    row, col = position()
    parity, local = member >> 6, member & 63
    band_row = (local * 37) >> 8
    band_col = local - GRID * band_row
    offset_row = row + 16 * parity + 32 * band_row - LINES * (slot >> 3)
    offset_col = col + 8 * band_col - GRID * (slot & 7)
    hit = jnp.logical_and(offset_row >= 0, offset_row < LINES)
    hit = jnp.logical_and(hit, jnp.logical_and(offset_col >= 0, offset_col < GRID))
    return jnp.logical_and(hit, local < GRID * GRID)


def owner_slot(line, column):
    row, col = position()
    return ((LINES * row + line) & 15) * 8 + ((GRID * col + column) & 7)


def one_hot(hit):
    return jnp.where(hit, 1.0, 0.0).astype(BF16)


def norm_parts(values):
    centered = values - jnp.mean(values, axis=-1, keepdims=True)
    inv_std = lax.rsqrt(jnp.mean(centered * centered, axis=-1, keepdims=True) + EPSILON)
    return centered * inv_std, inv_std


def norm_back(grad, normal_hat, inv_std, gain):
    grad_hat = grad * gain
    first = jnp.mean(grad_hat, axis=-1, keepdims=True)
    second = jnp.mean(grad_hat * normal_hat, axis=-1, keepdims=True)
    return inv_std * (grad_hat - first - normal_hat * second)


def head_mask(shape):
    return (iota(shape, 0) >> 6) == (iota(shape, 1) >> 5)


def spread(values, mask):
    tiled = jnp.concatenate([values] * QUAD, axis=0)
    return jnp.where(mask, tiled, jnp.zeros_like(tiled))


def gather_heads(values):
    lanes = iota((ROWS, 128), 1) >> 5
    total = jnp.where(lanes == 0, values[:ROWS], 0.0)
    for head in range(1, QUAD):
        total = total + jnp.where(lanes == head, values[head * ROWS : (head + 1) * ROWS], 0.0)
    return total


def probabilities(key, query_spread, scale):
    scores = dot_nt(key, query_spread) * scale
    expo = jnp.where(iota(scores.shape, 0) < GRID * GRID, jnp.exp(scores), 0.0)
    return expo * (1.0 / jnp.sum(expo, axis=0, keepdims=True))


def load_every(ref, start, step):
    parts = [ref[part, pl.ds(start, SLOTS, stride=step), :] for part in range(3)]
    return jnp.concatenate(parts, axis=1).astype(BF16)


def send_kernel(tokens_hbm, grad_hbm, out_ref, tokens_ref, grad_ref, sems):
    copies = [
        pltpu.make_async_copy(tokens_hbm, tokens_ref, sems.at[0]),
        pltpu.make_async_copy(grad_hbm, grad_ref, sems.at[1]),
    ]
    for copy in copies:
        copy.start()
    for copy in copies:
        copy.wait()
    for line in range(16):
        for column in range(8):
            slot = owner_slot(line, column)
            if line < LINES and column < GRID:
                unit = jnp.concatenate(
                    [tokens_ref[line, column].astype(F32), grad_ref[line, column].astype(F32)], axis=0
                ).astype(BF16)
            else:
                unit = jnp.zeros((8, 384), BF16)
            out_ref[slot] = unit


def return_kernel(recv_ref, out_ref):
    for line in range(LINES):
        for column in range(GRID):
            unit = recv_ref[owner_slot(line, column), :16].astype(F32)
            for part in range(3):
                out_ref[line, column, :, part * 128 : (part + 1) * 128] = unit[
                    part * 4 : part * 4 + 4
                ].astype(BF16)


def gelu_parts(hidden, grad):
    inner = 0.7978845608028654
    square = hidden * hidden
    tanh = jnp.tanh(inner * (hidden + 0.044715 * (hidden * square)))
    half = 0.5 * (1.0 + tanh)
    slope = half + 0.5 * hidden * (1.0 - tanh * tanh) * (
        inner * (1.0 + 3 * 0.044715 * square)
    )
    return hidden * half, grad * slope


def forward_kernel(
    recv_ref, gain_one, w_qkv, w_proj,
    x_ref, qkv_ref, mixed_ref, resid_ref, grad_ref, arrived, normed,
):
    for part in range(3):
        arrived[part] = recv_ref[:, part * 128 : (part + 1) * 128].astype(F32)
    match = one_hot(group_match(iota((SLOTS, SLOTS), 1), iota((SLOTS, SLOTS), 0)))
    for crop in range(4):
        rows = pl.ds(crop * SLOTS, SLOTS)
        x = dot(match, load_every(arrived, crop, 8))
        x_ref[rows, :] = x.astype(BF16)
        normal_hat, _ = norm_parts(x)
        normed[rows, :] = (normal_hat * gain_one[...]).astype(BF16)
        grad_ref[rows, :] = dot(match, load_every(arrived, crop + 4, 8)).astype(BF16)
    for part in range(3):
        cols = pl.ds(part * 384, 384)
        qkv_ref[:, cols] = dot_nt(normed[...], w_qkv[cols, :]).astype(BF16)
    mask = head_mask((QUAD * ROWS, 128))
    scale = 32.0 ** -0.5

    @pl.loop(0, 4)
    def _(pair):
        units = unit_places(pair)
        query = [spread(qkv_ref[rows, pl.ds(lane, 128)], mask) for rows, lane in units]
        probs = [
            probabilities(qkv_ref[rows, pl.ds(384 + lane, 128)], query[n], scale).astype(BF16)
            for n, (rows, lane) in enumerate(units)
        ]
        mixed = [
            dot_tn(probs[n], qkv_ref[rows, pl.ds(768 + lane, 128)])
            for n, (rows, lane) in enumerate(units)
        ]
        for n, (rows, lane) in enumerate(units):
            mixed_ref[rows, pl.ds(lane, 128)] = gather_heads(mixed[n]).astype(BF16)

    for crop in range(4):
        rows = pl.ds(crop * SLOTS, SLOTS)
        branch = dot_nt(mixed_ref[rows, :], w_proj[...]).astype(BF16)
        resid_ref[rows, :] = (x_ref[rows, :].astype(F32) + branch.astype(F32)).astype(BF16)


def unit_places(pair):
    places = []
    for half in range(2):
        rows = pl.ds(pl.multiple_of(pair * 2 * ROWS + half * ROWS, ROWS), ROWS)
        places.extend((rows, quad * 128) for quad in range(3))
    return places


def mlp_kernel(
    grad_out, resid, gain_two, w_up, w_down,
    resid_grad_ref, keep_ref, send_ref, gain_ref,
    normed, hidden_grad, grad_turned, up_total, down_total, back, piece_rows,
):
    for crop in range(4):
        rows = pl.ds(crop * SLOTS, SLOTS)
        normal_hat, _ = norm_parts(resid[rows, :].astype(F32))
        normed[rows, :] = (normal_hat * gain_two[...]).astype(BF16)
        grad_turned[:, rows] = grad_out[rows, :].astype(F32).T.astype(BF16)
    back[...] = jnp.zeros_like(back)

    @pl.loop(0, 4)
    def _(chunk):
        cols = pl.ds(pl.multiple_of(chunk * 384, 384), 384)
        hidden = dot_nt(normed[...], w_up[cols, :])
        grad_act = dot(grad_out[...], w_down[:, cols])
        activated, grad_hidden = gelu_parts(hidden, grad_act)
        hidden_grad[...] = grad_hidden.astype(BF16)
        down_total[:, cols] = dot(grad_turned[...], activated.astype(BF16))
        up_total[cols, :] = dot_tn(hidden_grad[...], normed[...])
        back[...] += dot(hidden_grad[...], w_up[cols, :])

    for ref, side in piece_sides(keep_ref, send_ref):
        for piece in range(8):
            owner = 2 * piece + side
            piece_rows[:96, :] = up_total[pl.ds(pl.multiple_of(owner * 96, 8), 96), :]
            for part in range(4):
                piece_rows[96 + 24 * part : 120 + 24 * part, :] = down_total[
                    pl.ds(pl.multiple_of(owner * 24, 8), 24), part * 384 : (part + 1) * 384
                ]
            ref[piece] = piece_rows[...].astype(BF16)
    gain = jnp.zeros((1, 384), F32)
    for crop in range(4):
        rows = pl.ds(crop * SLOTS, SLOTS)
        normal_hat, inv_std = norm_parts(resid[rows, :].astype(F32))
        grad = back[rows, :]
        gain = gain + jnp.sum(grad * normal_hat, axis=0, keepdims=True)
        resid_grad_ref[rows, :] = (
            grad_out[rows, :].astype(F32) + norm_back(grad, normal_hat, inv_std, gain_two[...])
        ).astype(BF16)
    gain_ref[...] = gain


def piece_sides(keep_ref, send_ref):
    core = lax.axis_index("core")
    return (keep_ref, core), (send_ref, 1 - core)


def attention_kernel(
    x_ref, qkv_ref, resid_grad_ref, gain_one, w_qkv, w_proj,
    out_ref, rows_grad, normed_ref, gain_ref, grad_mixed, slots,
):
    grad_mixed[...] = dot(resid_grad_ref[...], w_proj[...]).astype(BF16)
    mask = head_mask((QUAD * ROWS, 128))
    scale = 32.0 ** -0.5

    @pl.loop(0, 4)
    def _(pair):
        units = unit_places(pair)
        count = range(len(units))
        query = [spread(qkv_ref[rows, pl.ds(lane, 128)], mask) for rows, lane in units]
        grad = [spread(grad_mixed[rows, pl.ds(lane, 128)], mask) for rows, lane in units]
        key = [qkv_ref[rows, pl.ds(384 + lane, 128)] for rows, lane in units]
        probs = [probabilities(key[n], query[n], scale) for n in count]
        grad_probs = [
            dot_nt(qkv_ref[rows, pl.ds(768 + lane, 128)], grad[n])
            for n, (rows, lane) in enumerate(units)
        ]
        grad_scores = []
        for n in count:
            centre = jnp.sum(grad_probs[n] * probs[n], axis=0, keepdims=True)
            grad_scores.append((probs[n] * (grad_probs[n] - centre) * scale).astype(BF16))
        for n, (rows, lane) in enumerate(units):
            rows_grad[rows, pl.ds(768 + lane, 128)] = dot(probs[n].astype(BF16), grad[n]).astype(BF16)
            rows_grad[rows, pl.ds(384 + lane, 128)] = dot(grad_scores[n], query[n]).astype(BF16)
            rows_grad[rows, pl.ds(lane, 128)] = gather_heads(
                dot_tn(grad_scores[n], key[n])
            ).astype(BF16)

    match = one_hot(group_match(iota((SLOTS, SLOTS), 0), iota((SLOTS, SLOTS), 1)))
    gain = jnp.zeros((1, 384), F32)
    for crop in range(4):
        rows = pl.ds(crop * SLOTS, SLOTS)
        grad = dot(rows_grad[rows, :], w_qkv[...]).astype(BF16).astype(F32)
        normal_hat, inv_std = norm_parts(x_ref[rows, :].astype(F32))
        normed_ref[rows, :] = (normal_hat * gain_one[...]).astype(BF16)
        gain = gain + jnp.sum(grad * normal_hat, axis=0, keepdims=True)
        grad_x = resid_grad_ref[rows, :].astype(F32) + norm_back(
            grad, normal_hat, inv_std, gain_one[...]
        )
        returned = dot(match, grad_x.astype(BF16))
        for part in range(3):
            slots[pl.ds(part * 4 + crop, SLOTS, stride=16), :] = returned[
                :, part * 128 : (part + 1) * 128
            ]
    for spare in range(12, 16):
        slots[pl.ds(spare, SLOTS, stride=16), :] = jnp.zeros((SLOTS, 128), F32)
    out_ref[...] = slots[...].astype(BF16)
    gain_ref[...] = gain


def weight_kernel(
    rows_grad, normed, resid_grad, mixed, first, second, keep_ref, send_ref, total, piece_rows,
):
    for part in range(3):
        grad = dot_tn(rows_grad[:, pl.ds(part * 384, 384)], normed[...])
        start, stop = part * 384, part * 384 + 384
        for owner in range(16):
            low, high = max(start, owner * 72), min(stop, owner * 72 + 72)
            if low < high:
                place = owner * 96 + low - owner * 72
                total[place : place + high - low, :] = grad[low - start : high - start]
    grad = dot_tn(resid_grad[...], mixed[...])
    for owner in range(16):
        total[owner * 96 + 72 : owner * 96 + 96, :] = grad[owner * 24 : owner * 24 + 24]
    for ref, side in piece_sides(keep_ref, send_ref):
        piece_rows[...] = jnp.zeros_like(piece_rows)
        for owner in range(16):
            for half in range(2):
                start = pl.multiple_of(owner * 96 + side * 48 + half * 24, 8)
                piece_rows[half, owner * 24 : owner * 24 + 24, :] = total[pl.ds(start, 24), :]
        piece_rows[0, 384:385, :] = jnp.where(side == 0, first[...], second[...])
        ref[...] = piece_rows[...].astype(BF16)


def column_spread(half):
    source, target = iota((384, 1024), 0), iota((384, 1024), 1)
    lane = (target & 127) - 64 * half
    hit = jnp.logical_and(source == (target >> 7) * 48 + lane, lane >= 0)
    return one_hot(jnp.logical_and(hit, lane < 48))


def out_kernel(keep_ref, recv_ref, slots_ref, out_ref):
    total = keep_ref[...].astype(F32) + recv_ref[...].astype(F32)
    packed = dot(total[0, :384].astype(BF16), column_spread(0))
    packed = packed + dot(total[1, :384].astype(BF16), column_spread(1))
    gain = jnp.concatenate(
        [jnp.zeros((12, 128), F32)]
        + [total[0, 384:385, part * 128 : (part + 1) * 128] for part in range(3)]
        + [jnp.zeros((1, 128), F32)],
        axis=0,
    )
    for row in range(16):
        for col in range(8):
            owner = row * 8 + col
            block = packed[row * 24 : row * 24 + 24, col * 128 : (col + 1) * 128]
            token = slots_ref[owner * 16 : owner * 16 + 16, :].astype(F32) + gain
            out_ref[owner, :16] = token.astype(BF16)
            out_ref[owner, 16:] = block.astype(BF16)


def pack_columns(rows, col):
    low = pltpu.roll(rows[:48], (384 - 48 * col) % 384, 1)[:, :128]
    high = pltpu.roll(rows[48:96], (384 + 64 - 48 * col) % 384, 1)[:, :128]
    return jnp.where(iota((48, 128), 1) < 64, low, high)


def core_kernel(keep_ref, recv_ref, own, near, back, far_low, far_high):
    row = lax.axis_index("y")

    def total(step, col):
        piece = ((row + step) & 3) * 2 + col
        return (keep_ref[piece].astype(F32) + recv_ref[piece].astype(F32)).astype(BF16)

    for ref, step in ((own, 0), (near, 1), (back, 3)):
        for col in range(2):
            ref[col] = total(step, col)
    far_low[...] = total(2, 0)
    far_high[...] = total(2, 1)


def ring_kernel(near, back, far_low, far_high, out_near, out_back):
    out_near[0] = (near[0].astype(F32) + far_low[...].astype(F32)).astype(BF16)
    out_near[1] = near[1]
    out_back[0] = back[0]
    out_back[1] = (back[1].astype(F32) + far_high[...].astype(F32)).astype(BF16)


def row_kernel(own, near, back, keep_ref, send_ref):
    col = lax.axis_index("xl")
    for ref, side in ((keep_ref, col), (send_ref, 1 - col)):
        total = own[side].astype(F32) + near[side].astype(F32) + back[side].astype(F32)
        ref[...] = total.astype(BF16)


def column_split(packed, keep_ref, send_ref, bit, count):
    own = (lax.axis_index("wa") >> bit) & 1
    for ref, side in ((keep_ref, own), (send_ref, 1 - own)):
        for piece in range(count):
            ref[piece] = packed(2 * piece + side).astype(BF16)


def early_pack(keep_ref, recv_ref, out_keep, out_send, packed):
    total = keep_ref[...].astype(F32) + recv_ref[...].astype(F32)
    for col in range(8):
        start = 96 + 24 * (col // 2)
        block = total[start : start + 24]
        if col % 2:
            block = pltpu.roll(block, 192, 1)
        packed[col, :48] = pack_columns(total[:96], col)
        packed[col, 48:72] = block[:, :128]
        packed[col, 72:] = block[:, 128:256]
    column_split(lambda piece: packed[piece], out_keep, out_send, 0, 4)


def early_halve(keep_ref, recv_ref, out_keep, out_send, bit, count):
    column_split(
        lambda piece: keep_ref[piece].astype(F32) + recv_ref[piece].astype(F32),
        out_keep, out_send, bit, count,
    )


def block_sum(early_keep, early_recv, recv_ref, out_ref):
    early = early_keep[0].astype(F32) + early_recv[0].astype(F32)
    out_ref[:96, :] = early.astype(BF16)
    gains = []
    for core in range(2):
        total = jnp.zeros((40, 128), F32)
        for plane in range(8):
            for col in range(8):
                total = total + recv_ref[(plane * 2 + core) * 8 + col].astype(F32)
        out_ref[96 + 24 * core : 120 + 24 * core, :] = total[16:].astype(BF16)
        gains.append(total[8:16])
    out_ref[144:, :] = jnp.concatenate(gains, axis=0).astype(BF16)


def unpack_columns(packed):
    low = packed[:, :48]
    high = pltpu.roll(packed, 64, 1)[:, :48]
    wide = jnp.concatenate([low, high], axis=0)
    wide = jnp.concatenate([wide, jnp.zeros((96, 80), F32)], axis=1)
    wide = jnp.concatenate([wide, jnp.zeros((32, 128), F32)], axis=0)
    return wide.T[:48]


def final_weights(
    own_ref, other_ref,
    qkv_ref, proj_ref, up_ref, down_ref, first_ref, second_ref, factor,
):
    total = (own_ref[...].astype(F32) + other_ref[...].astype(F32)) * factor
    up_ref[...] = unpack_columns(total[:48])[:, :96]
    down_ref[:, :128] = total[48:72]
    down_ref[:, 128:] = total[72:96, :64]
    late = total[96:144]
    high = pltpu.roll(late, 64, 1)
    proj_ref[...] = high[24:, :48]
    wide = jnp.concatenate([late[:24], high[:24], late[24:], jnp.zeros((56, 128), F32)], axis=0)
    qkv_ref[...] = wide.T[:48, :72]
    for part in range(3):
        lane = pl.ds(part * 128, 128)
        first_ref[lane] = total[148 + part]
        second_ref[lane] = total[156 + part]


def call(kernel, outs, scratch=(), flops=0, nbytes=0, space=pltpu.VMEM, limit=24):
    vmem = pl.BlockSpec(memory_space=pltpu.VMEM)
    scratch = [pltpu.VMEM(*item) if isinstance(item, tuple) else item for item in scratch]

    def run(*args):
        return pl.pallas_call(
            kernel,
            out_shape=[jax.ShapeDtypeStruct(shape, dtype) for shape, dtype in outs],
            in_specs=[pl.BlockSpec(memory_space=space)] * len(args),
            out_specs=[vmem] * len(outs),
            scratch_shapes=scratch,
            compiler_params=pltpu.CompilerParams(vmem_limit_bytes=limit << 20),
            cost_estimate=pl.CostEstimate(flops=flops, bytes_accessed=nbytes, transcendentals=0),
        )(*args)

    return run


def exchange(values, axes):
    return lax.all_to_all(values, axes, split_axis=0, concat_axis=0, tiled=True)


def swap(values, axis, size, bit):
    return lax.ppermute(values, axis, [(place, place ^ bit) for place in range(size)])


def shift(values, step):
    return lax.ppermute(values, "y", [(place, (place + step) % 4) for place in range(4)])


def early_ring(keep, arrived):
    part, half = ((2, 192, 384), BF16), ((192, 384), BF16)
    own, near, back, low, high = call(
        core_kernel, [part, part, part, half, half], nbytes=4 * 10**6
    )(keep, arrived)
    near, back = call(ring_kernel, [part, part], nbytes=3 * 10**6)(
        near, back, shift(low, 1), shift(high, 3)
    )
    return own, near, back


def early_sums(own, near, back):
    piece = ((192, 384), BF16)
    keep, send = call(row_kernel, [piece] * 2, nbytes=2 * 10**6)(own, shift(near, 1), shift(back, 3))
    keep, send = call(
        early_pack, [((4, 96, 128), BF16)] * 2, [((8, 96, 128), F32)], nbytes=10**6
    )(keep, swap(send, "xl", 2, 1))
    for bit, count in ((1, 2), (2, 1)):
        keep, send = call(
            functools.partial(early_halve, bit=bit, count=count),
            [((count, 96, 128), BF16)] * 2,
            nbytes=3 * 10**5,
        )(keep, swap(send, "wa", 8, bit))
    return keep, swap(send, "wa", 8, 4)


def body(tokens, grad_out, gain_first, gain_second, w_qkv, w_proj, w_up, w_down):
    gain_one, gain_two = gain_first.reshape(1, 384), gain_second.reshape(1, 384)
    factor = (8 * 224 * 56) ** -0.5
    tile = pltpu.VMEM((LINES, GRID, 4, 384), BF16)
    (sent,) = call(
        send_kernel,
        [((SLOTS, 8, 384), BF16)],
        [tile, tile, pltpu.SemaphoreType.DMA((2,))],
        nbytes=2 * 10**6,
        space=pl.ANY,
        limit=60,
    )(
        tokens.transpose(1, 2, 0, 3), grad_out.transpose(1, 2, 0, 3)
    )
    arrived = exchange(sent, HA + ("wa",)).reshape(SLOTS * 8, 384)
    rows = ((512, 384), BF16)
    x, qkv, mixed, resid, grad_rows = call(
        forward_kernel,
        [rows, ((512, 1152), BF16), rows, rows, rows],
        [((3, 1024, 128), F32), rows],
        flops=10**9, nbytes=4 * 10**6,
    )(arrived, gain_one, w_qkv, w_proj)
    resid_grad, early_keep, early_send, gain_sum_two = call(
        mlp_kernel,
        [rows, ((8, 192, 384), BF16), ((8, 192, 384), BF16), ((1, 384), F32)],
        [
            rows, rows, ((384, 512), BF16), ((1536, 384), F32), ((384, 1536), F32),
            ((512, 384), F32), ((192, 384), F32),
        ],
        flops=3 * 10**9, nbytes=6 * 10**6,
    )(grad_rows, resid, gain_two, w_up, w_down)
    early_arrived = swap(early_send, "core", 2, 1)
    slots, rows_grad, normed, gain_sum_one = call(
        attention_kernel,
        [((SLOTS * 16, 128), BF16), ((512, 1152), BF16), rows, ((1, 384), F32)],
        [rows, ((SLOTS * 16, 128), F32)],
        flops=6 * 10**9, nbytes=20 * 10**6,
    )(x, qkv, resid_grad, gain_one, w_qkv, w_proj)
    early_keep, rows_grad = lax.optimization_barrier((early_keep, rows_grad))
    own, near, back = early_ring(early_keep, early_arrived)
    late = ((2, 400, 384), BF16)
    late_keep, late_send = call(
        weight_kernel,
        [late, late],
        [((1536, 384), F32), ((2, 400, 384), F32)],
        flops=10**9, nbytes=5 * 10**6,
    )(rows_grad, normed, resid_grad, mixed, gain_sum_one, gain_sum_two)
    near, back, slots = lax.optimization_barrier((near, back, slots))
    (sent,) = call(out_kernel, [((SLOTS, 40, 128), BF16)], flops=10**9, nbytes=5 * 10**6)(
        late_keep, swap(late_send, "core", 2, 1), slots
    )
    returned = exchange(sent, HA + ("wa",))
    early = early_sums(own, near, back)
    (total,) = call(block_sum, [((160, 128), BF16)], nbytes=10**6)(*early, returned)
    other = lax.ppermute(total, "dp", [(0, 1), (1, 0)])
    grad_qkv, grad_proj, grad_up, grad_down, first, second = call(
        functools.partial(final_weights, factor=factor),
        [
            ((48, 72), F32), ((24, 48), F32), ((48, 96), F32), ((24, 192), F32),
            ((384,), F32), ((384,), F32),
        ],
        nbytes=10**6,
    )(total, other)
    (grad_tile,) = call(return_kernel, [((LINES, GRID, 4, 384), BF16)], nbytes=10**6)(returned)
    return (
        grad_tile.transpose(2, 0, 1, 3), grad_qkv.T, grad_proj, grad_up.T, grad_down, first, second,
    )


def solution(mesh):
    fine = Mesh(mesh.devices.reshape(4, 2, 2, 8, 2), HA + ("wa", "dp"))
    tile = P("dp", HA, "wa", None)
    block = P(HA, "wa")
    return jax.shard_map(
        body,
        mesh=fine,
        in_specs=(tile, tile, P(), P(), P(), P(), P(), P()),
        out_specs=(tile, block, block, block, block, P(), P()),
        check_vma=False,
    )
```

```python
import functools

import jax
import jax.numpy as jnp
from jax import lax
from jax.experimental import pallas as pl
from jax.experimental.pallas import tpu as pltpu
from jax.sharding import Mesh, PartitionSpec as P

HEADS = 12
GRID = 7
EPSILON = 1e-05
SLOTS = 128
ROWS = 64
LINES = 14
QUAD = 4
F32 = jnp.float32
BF16 = jnp.bfloat16
HA = ("y", "xl", "core")


def dot(left, right):
    return jnp.dot(left, right, preferred_element_type=F32)


def dot_nt(left, right):
    return lax.dot_general(left, right, (((1,), (1,)), ((), ())), preferred_element_type=F32)


def dot_tn(left, right):
    return lax.dot_general(left, right, (((0,), (0,)), ((), ())), preferred_element_type=F32)


def iota(shape, dim):
    return lax.broadcasted_iota(jnp.int32, shape, dim)


def position():
    rows = (lax.axis_index("y") * 2 + lax.axis_index("xl")) * 2 + lax.axis_index("core")
    return rows, lax.axis_index("wa")


def group_match(slot, member):
    row, col = position()
    parity, local = member >> 6, member & 63
    band_row = (local * 37) >> 8
    band_col = local - GRID * band_row
    offset_row = row + 16 * parity + 32 * band_row - LINES * (slot >> 3)
    offset_col = col + 8 * band_col - GRID * (slot & 7)
    hit = jnp.logical_and(offset_row >= 0, offset_row < LINES)
    hit = jnp.logical_and(hit, jnp.logical_and(offset_col >= 0, offset_col < GRID))
    return jnp.logical_and(hit, local < GRID * GRID)


def owner_slot(line, column):
    row, col = position()
    return ((LINES * row + line) & 15) * 8 + ((GRID * col + column) & 7)


def one_hot(hit):
    return jnp.where(hit, 1.0, 0.0).astype(BF16)


def norm_parts(values):
    centered = values - jnp.mean(values, axis=-1, keepdims=True)
    inv_std = lax.rsqrt(jnp.mean(centered * centered, axis=-1, keepdims=True) + EPSILON)
    return centered * inv_std, inv_std


def norm_back(grad, normal_hat, inv_std, gain):
    grad_hat = grad * gain
    first = jnp.mean(grad_hat, axis=-1, keepdims=True)
    second = jnp.mean(grad_hat * normal_hat, axis=-1, keepdims=True)
    return inv_std * (grad_hat - first - normal_hat * second)


def head_mask(shape):
    return (iota(shape, 0) >> 6) == (iota(shape, 1) >> 5)


def spread(values, mask):
    tiled = jnp.concatenate([values] * QUAD, axis=0)
    return jnp.where(mask, tiled, jnp.zeros_like(tiled))


def gather_heads(values):
    lanes = iota((ROWS, 128), 1) >> 5
    total = jnp.where(lanes == 0, values[:ROWS], 0.0)
    for head in range(1, QUAD):
        total = total + jnp.where(lanes == head, values[head * ROWS : (head + 1) * ROWS], 0.0)
    return total


def probabilities(key, query_spread, scale):
    scores = dot_nt(key, query_spread) * scale
    expo = jnp.where(iota(scores.shape, 0) < GRID * GRID, jnp.exp(scores), 0.0)
    return expo * (1.0 / jnp.sum(expo, axis=0, keepdims=True))


def load_every(ref, start, step):
    parts = [ref[part, pl.ds(start, SLOTS, stride=step), :] for part in range(3)]
    return jnp.concatenate(parts, axis=1).astype(BF16)


def store_every(ref, start, step, values):
    for part in range(3):
        ref[part, pl.ds(start, SLOTS, stride=step), :] = values[:, part * 128 : (part + 1) * 128]


def send_kernel(tokens_hbm, grad_hbm, out_ref, tokens_ref, grad_ref, sems):
    copies = [
        pltpu.make_async_copy(tokens_hbm, tokens_ref, sems.at[0]),
        pltpu.make_async_copy(grad_hbm, grad_ref, sems.at[1]),
    ]
    for copy in copies:
        copy.start()
    for copy in copies:
        copy.wait()
    for line in range(16):
        for column in range(8):
            slot = owner_slot(line, column)
            if line < LINES and column < GRID:
                unit = jnp.concatenate(
                    [tokens_ref[line, column].astype(F32), grad_ref[line, column].astype(F32)], axis=0
                ).astype(BF16)
            else:
                unit = jnp.zeros((8, 384), BF16)
            out_ref[slot] = unit


def return_kernel(recv_ref, out_ref):
    for line in range(LINES):
        for column in range(GRID):
            out_ref[line, column] = recv_ref[owner_slot(line, column)]


def gelu_parts(hidden, grad):
    inner = 0.7978845608028654
    square = hidden * hidden
    tanh = jnp.tanh(inner * (hidden + 0.044715 * (hidden * square)))
    half = 0.5 * (1.0 + tanh)
    slope = half + 0.5 * hidden * (1.0 - tanh * tanh) * (
        inner * (1.0 + 3 * 0.044715 * square)
    )
    return hidden * half, grad * slope


def forward_kernel(
    recv_ref, gain_one, w_qkv, w_proj,
    x_ref, qkv_ref, mixed_ref, resid_ref, grad_ref, arrived, normed,
):
    for part in range(3):
        arrived[part] = recv_ref[:, part * 128 : (part + 1) * 128].astype(F32)
    match = one_hot(group_match(iota((SLOTS, SLOTS), 1), iota((SLOTS, SLOTS), 0)))
    for crop in range(4):
        rows = pl.ds(crop * SLOTS, SLOTS)
        x = dot(match, load_every(arrived, crop, 8))
        x_ref[rows, :] = x.astype(BF16)
        normal_hat, _ = norm_parts(x)
        normed[rows, :] = (normal_hat * gain_one[...]).astype(BF16)
        grad_ref[rows, :] = dot(match, load_every(arrived, crop + 4, 8)).astype(BF16)
    for part in range(3):
        cols = pl.ds(part * 384, 384)
        qkv_ref[:, cols] = dot_nt(normed[...], w_qkv[cols, :]).astype(BF16)
    mask = head_mask((QUAD * ROWS, 128))
    scale = 32.0 ** -0.5

    @pl.loop(0, 4)
    def _(pair):
        units = unit_places(pair)
        query = [spread(qkv_ref[rows, pl.ds(lane, 128)], mask) for rows, lane in units]
        probs = [
            probabilities(qkv_ref[rows, pl.ds(384 + lane, 128)], query[n], scale).astype(BF16)
            for n, (rows, lane) in enumerate(units)
        ]
        mixed = [
            dot_tn(probs[n], qkv_ref[rows, pl.ds(768 + lane, 128)])
            for n, (rows, lane) in enumerate(units)
        ]
        for n, (rows, lane) in enumerate(units):
            mixed_ref[rows, pl.ds(lane, 128)] = gather_heads(mixed[n]).astype(BF16)

    for crop in range(4):
        rows = pl.ds(crop * SLOTS, SLOTS)
        branch = dot_nt(mixed_ref[rows, :], w_proj[...]).astype(BF16)
        resid_ref[rows, :] = (x_ref[rows, :].astype(F32) + branch.astype(F32)).astype(BF16)


def unit_places(pair):
    places = []
    for half in range(2):
        rows = pl.ds(pl.multiple_of(pair * 2 * ROWS + half * ROWS, ROWS), ROWS)
        places.extend((rows, quad * 128) for quad in range(3))
    return places


def mlp_kernel(
    grad_out, resid, gain_two, w_up, w_down,
    resid_grad_ref, keep_ref, send_ref, gain_ref,
    normed, hidden_grad, grad_turned, up_total, down_total, back, piece_rows,
):
    for crop in range(4):
        rows = pl.ds(crop * SLOTS, SLOTS)
        normal_hat, _ = norm_parts(resid[rows, :].astype(F32))
        normed[rows, :] = (normal_hat * gain_two[...]).astype(BF16)
        grad_turned[:, rows] = grad_out[rows, :].astype(F32).T.astype(BF16)
    for chunk in range(4):
        cols = pl.ds(chunk * 384, 384)
        hidden = dot_nt(normed[...], w_up[cols, :])
        grad_act = dot(grad_out[...], w_down[:, cols])
        activated, grad_hidden = gelu_parts(hidden, grad_act)
        hidden_grad[:, cols] = grad_hidden.astype(BF16)
        down_total[:, cols] = dot(grad_turned[...], activated.astype(BF16))
        up_total[cols, :] = dot_tn(hidden_grad[:, cols], normed[...])
    back[...] = dot(hidden_grad[...], w_up[...])

    for ref, side in piece_sides(keep_ref, send_ref):
        for piece in range(8):
            owner = 2 * piece + side
            piece_rows[:96, :] = up_total[pl.ds(pl.multiple_of(owner * 96, 8), 96), :]
            for part in range(4):
                piece_rows[96 + 24 * part : 120 + 24 * part, :] = down_total[
                    pl.ds(pl.multiple_of(owner * 24, 8), 24), part * 384 : (part + 1) * 384
                ]
            ref[piece] = piece_rows[...].astype(BF16)
    gain = jnp.zeros((1, 384), F32)
    for crop in range(4):
        rows = pl.ds(crop * SLOTS, SLOTS)
        normal_hat, inv_std = norm_parts(resid[rows, :].astype(F32))
        grad = back[rows, :]
        gain = gain + jnp.sum(grad * normal_hat, axis=0, keepdims=True)
        resid_grad_ref[rows, :] = (
            grad_out[rows, :].astype(F32) + norm_back(grad, normal_hat, inv_std, gain_two[...])
        ).astype(BF16)
    gain_ref[...] = gain


def piece_sides(keep_ref, send_ref):
    core = lax.axis_index("core")
    return (keep_ref, core), (send_ref, 1 - core)


def attention_kernel(
    x_ref, qkv_ref, resid_grad_ref, gain_one, w_qkv, w_proj,
    out_ref, rows_grad, normed_ref, gain_ref, grad_mixed, slots,
):
    grad_mixed[...] = dot(resid_grad_ref[...], w_proj[...]).astype(BF16)
    mask = head_mask((QUAD * ROWS, 128))
    scale = 32.0 ** -0.5

    @pl.loop(0, 4)
    def _(pair):
        units = unit_places(pair)
        count = range(len(units))
        query = [spread(qkv_ref[rows, pl.ds(lane, 128)], mask) for rows, lane in units]
        grad = [spread(grad_mixed[rows, pl.ds(lane, 128)], mask) for rows, lane in units]
        key = [qkv_ref[rows, pl.ds(384 + lane, 128)] for rows, lane in units]
        probs = [probabilities(key[n], query[n], scale) for n in count]
        grad_probs = [
            dot_nt(qkv_ref[rows, pl.ds(768 + lane, 128)], grad[n])
            for n, (rows, lane) in enumerate(units)
        ]
        grad_scores = []
        for n in count:
            centre = jnp.sum(grad_probs[n] * probs[n], axis=0, keepdims=True)
            grad_scores.append((probs[n] * (grad_probs[n] - centre) * scale).astype(BF16))
        for n, (rows, lane) in enumerate(units):
            rows_grad[rows, pl.ds(768 + lane, 128)] = dot(probs[n].astype(BF16), grad[n]).astype(BF16)
            rows_grad[rows, pl.ds(384 + lane, 128)] = dot(grad_scores[n], query[n]).astype(BF16)
            rows_grad[rows, pl.ds(lane, 128)] = gather_heads(
                dot_tn(grad_scores[n], key[n])
            ).astype(BF16)

    match = one_hot(group_match(iota((SLOTS, SLOTS), 0), iota((SLOTS, SLOTS), 1)))
    gain = jnp.zeros((1, 384), F32)
    for crop in range(4):
        rows = pl.ds(crop * SLOTS, SLOTS)
        grad = dot(rows_grad[rows, :], w_qkv[...]).astype(BF16).astype(F32)
        normal_hat, inv_std = norm_parts(x_ref[rows, :].astype(F32))
        normed_ref[rows, :] = (normal_hat * gain_one[...]).astype(BF16)
        gain = gain + jnp.sum(grad * normal_hat, axis=0, keepdims=True)
        grad_x = resid_grad_ref[rows, :].astype(F32) + norm_back(
            grad, normal_hat, inv_std, gain_one[...]
        )
        store_every(slots, crop, 4, dot(match, grad_x.astype(BF16)))
    for slot in range(SLOTS):
        for part in range(3):
            out_ref[slot, :, part * 128 : (part + 1) * 128] = slots[
                part, slot * 4 : slot * 4 + 4, :
            ].astype(BF16)
    gain_ref[...] = gain


def weight_kernel(
    rows_grad, normed, resid_grad, mixed, first, second, keep_ref, send_ref,
    qkv_total, proj_total, piece_rows,
):
    for part in range(3):
        cols = pl.ds(part * 384, 384)
        qkv_total[cols, :] = dot_tn(rows_grad[:, cols], normed[...])
    proj_total[...] = dot_tn(resid_grad[...], mixed[...])
    piece_rows[96:, :] = jnp.zeros((16, 384), F32)
    piece_rows[96:97, :] = first[...]
    piece_rows[97:98, :] = second[...]
    for ref, side in piece_sides(keep_ref, send_ref):
        for piece in range(8):
            owner = 2 * piece + side
            piece_rows[:72, :] = qkv_total[pl.ds(pl.multiple_of(owner * 72, 8), 72), :]
            piece_rows[72:96, :] = proj_total[pl.ds(pl.multiple_of(owner * 24, 8), 24), :]
            ref[piece] = piece_rows[...].astype(BF16)


def core_kernel(
    early_keep, early_recv, late_keep, late_recv, own, near, back, far_low, far_high,
):
    row = lax.axis_index("y")

    def put(ref, step, col):
        piece = ((row + step) & 3) * 2 + col
        early = early_keep[piece].astype(F32) + early_recv[piece].astype(F32)
        late = late_keep[piece].astype(F32) + late_recv[piece].astype(F32)
        ref[:192] = early.astype(BF16)
        if step == 2:
            late = jnp.concatenate([late[:96], pltpu.roll(late[96:], 2, 0)], axis=0)
        ref[192:] = late.astype(BF16)

    for ref, step in ((own, 0), (near, 1), (back, 3)):
        for col in range(2):
            put(ref.at[col], step, col)
    put(far_low, 2, 0)
    put(far_high, 2, 1)


def ring_kernel(near, back, far_low, far_high, out_near, out_back):
    out_near[0] = (near[0].astype(F32) + far_low[...].astype(F32)).astype(BF16)
    out_near[1] = near[1]
    out_back[0] = back[0]
    out_back[1] = (back[1].astype(F32) + far_high[...].astype(F32)).astype(BF16)


def row_kernel(own, near, back, keep_ref, send_ref, gains):
    row, col = lax.axis_index("y"), lax.axis_index("xl")
    first, second, third = (ref[0, 288:].astype(F32) for ref in (own, near, back))
    gains[row] = first
    gains[(row + 3) & 3] = second
    gains[(row + 1) & 3] = third
    gains[(row + 2) & 3] = pltpu.roll(second, 14, 0)
    gain = ((gains[0] + gains[1]) + (gains[2] + gains[3])).astype(BF16)
    for ref, side in ((keep_ref, col), (send_ref, 1 - col)):
        total = own[side, :288].astype(F32) + near[side, :288].astype(F32)
        ref[:288] = (total + back[side, :288].astype(F32)).astype(BF16)
        ref[288:] = gain


def pack_columns(rows, col):
    low = pltpu.roll(rows[:48], (384 - 48 * col) % 384, 1)[:, :128]
    high = pltpu.roll(rows[48:96], (384 + 64 - 48 * col) % 384, 1)[:, :128]
    return jnp.where(iota((48, 128), 1) < 64, low, high)


def pack_kernel(keep_ref, recv_ref, out_ref):
    total = keep_ref[...].astype(F32) + recv_ref[...].astype(F32)
    gain_rows = [
        total[288 + which : 289 + which, part * 128 : (part + 1) * 128]
        for which in range(2)
        for part in range(3)
    ]
    gain_rows.append(jnp.zeros((2, 128), F32))
    for col in range(8):
        start = 96 + 24 * (col // 2)
        block = total[start : start + 24]
        if col % 2:
            block = pltpu.roll(block, 192, 1)
        out_ref[col] = jnp.concatenate(
            [pack_columns(total[:96], col), block[:, :128], block[:, 128:256]]
            + [pack_columns(total[192:288], col)] + gain_rows,
            axis=0,
        ).astype(BF16)


def block_sum(recv_ref, out_ref):
    total = recv_ref[0].astype(F32)
    for place in range(1, 8):
        total = total + recv_ref[place].astype(F32)
    out_ref[...] = total.astype(BF16)


def unpack_columns(packed):
    low = packed[:, :48]
    high = pltpu.roll(packed, 64, 1)[:, :48]
    wide = jnp.concatenate([low, high], axis=0)
    wide = jnp.concatenate([wide, jnp.zeros((96, 80), F32)], axis=1)
    wide = jnp.concatenate([wide, jnp.zeros((32, 128), F32)], axis=0)
    return wide.T[:48]


def final_weights(
    own_ref, other_ref,
    qkv_ref, proj_ref, up_ref, down_ref, first_ref, second_ref, factor,
):
    total = (own_ref[...].astype(F32) + other_ref[...].astype(F32)) * factor
    early, late = total[:96], total[96:]
    up_ref[...] = unpack_columns(early[:48])[:, :96]
    down_ref[:, :128] = early[48:72]
    down_ref[:, 128:] = early[72:96, :64]
    qkv_ref[...] = unpack_columns(late[:48])[:, :72]
    proj_ref[...] = pltpu.roll(late[:48], 64, 1)[24:48, :48]
    for part in range(3):
        lane = pl.ds(part * 128, 128)
        first_ref[lane] = late[48 + part]
        second_ref[lane] = late[51 + part]


def call(kernel, outs, scratch=(), flops=0, nbytes=0, space=pltpu.VMEM, limit=16):
    vmem = pl.BlockSpec(memory_space=pltpu.VMEM)
    scratch = [pltpu.VMEM(*item) if isinstance(item, tuple) else item for item in scratch]

    def run(*args):
        return pl.pallas_call(
            kernel,
            out_shape=[jax.ShapeDtypeStruct(shape, dtype) for shape, dtype in outs],
            in_specs=[pl.BlockSpec(memory_space=space)] * len(args),
            out_specs=[vmem] * len(outs),
            scratch_shapes=scratch,
            compiler_params=pltpu.CompilerParams(vmem_limit_bytes=limit << 20),
            cost_estimate=pl.CostEstimate(flops=flops, bytes_accessed=nbytes, transcendentals=0),
        )(*args)

    return run


def exchange(values, axes):
    return lax.all_to_all(values, axes, split_axis=0, concat_axis=0, tiled=True)


def swap(values, axis):
    return lax.ppermute(values, axis, [(0, 1), (1, 0)])


def shift(values, step):
    return lax.ppermute(values, "y", [(place, (place + step) % 4) for place in range(4)])


def body(tokens, grad_out, gain_first, gain_second, w_qkv, w_proj, w_up, w_down):
    gain_one, gain_two = gain_first.reshape(1, 384), gain_second.reshape(1, 384)
    factor = (8 * 224 * 56) ** -0.5
    tile = pltpu.VMEM((LINES, GRID, 4, 384), BF16)
    (sent,) = call(
        send_kernel,
        [((SLOTS, 8, 384), BF16)],
        [tile, tile, pltpu.SemaphoreType.DMA((2,))],
        nbytes=2 * 10**6,
        space=pl.ANY,
        limit=60,
    )(
        tokens.transpose(1, 2, 0, 3), grad_out.transpose(1, 2, 0, 3)
    )
    arrived = exchange(sent, HA + ("wa",)).reshape(SLOTS * 8, 384)
    rows = ((512, 384), BF16)
    x, qkv, mixed, resid, grad_rows = call(
        forward_kernel,
        [rows, ((512, 1152), BF16), rows, rows, rows],
        [((3, 1024, 128), F32), rows],
        flops=10**9, nbytes=4 * 10**6,
    )(arrived, gain_one, w_qkv, w_proj)
    resid_grad, early_keep, early_send, gain_sum_two = call(
        mlp_kernel,
        [rows, ((8, 192, 384), BF16), ((8, 192, 384), BF16), ((1, 384), F32)],
        [
            rows, ((512, 1536), BF16), ((384, 512), BF16), ((1536, 384), F32), ((384, 1536), F32),
            ((512, 384), F32), ((192, 384), F32),
        ],
        flops=3 * 10**9, nbytes=6 * 10**6,
    )(grad_rows, resid, gain_two, w_up, w_down)
    slots, rows_grad, normed, gain_sum_one = call(
        attention_kernel,
        [((SLOTS, 4, 384), BF16), ((512, 1152), BF16), rows, ((1, 384), F32)],
        [rows, ((3, 512, 128), F32)],
        flops=6 * 10**9, nbytes=20 * 10**6,
    )(x, qkv, resid_grad, gain_one, w_qkv, w_proj)
    late_keep, late_send = call(
        weight_kernel,
        [((8, 112, 384), BF16), ((8, 112, 384), BF16)],
        [((1152, 384), F32), ((384, 384), F32), ((112, 384), F32)],
        flops=10**9, nbytes=5 * 10**6,
    )(rows_grad, normed, resid_grad, mixed, gain_sum_one, gain_sum_two)
    whole, half = ((2, 304, 384), BF16), ((304, 384), BF16)
    own, near, back, low, high = call(core_kernel, [whole, whole, whole, half, half], nbytes=10**7)(
        early_keep, swap(early_send, "core"), late_keep, swap(late_send, "core")
    )
    slots, low, high = lax.optimization_barrier((slots, low, high))
    returned = exchange(slots, HA + ("wa",))
    near, back = call(ring_kernel, [whole, whole], nbytes=4 * 10**6)(
        near, back, shift(low, 1), shift(high, 3)
    )
    keep, send = call(row_kernel, [half, half], [((4, 16, 384), F32)], nbytes=3 * 10**6)(
        own, shift(near, 1), shift(back, 3)
    )
    (blocks,) = call(pack_kernel, [((8, 152, 128), BF16)], nbytes=10**6)(keep, swap(send, "xl"))
    blocks, returned = lax.optimization_barrier((blocks, returned))
    (total,) = call(block_sum, [((152, 128), BF16)], nbytes=10**6)(exchange(blocks, "wa"))
    other = swap(total, "dp")
    grad_qkv, grad_proj, grad_up, grad_down, first, second = call(
        functools.partial(final_weights, factor=factor),
        [
            ((48, 72), F32), ((24, 48), F32), ((48, 96), F32), ((24, 192), F32),
            ((384,), F32), ((384,), F32),
        ],
        nbytes=10**6,
    )(total, other)
    (grad_tile,) = call(return_kernel, [((LINES, GRID, 4, 384), BF16)], nbytes=10**6)(returned)
    return (
        grad_tile.transpose(2, 0, 1, 3), grad_qkv.T, grad_proj, grad_up.T, grad_down, first, second,
    )


def solution(mesh):
    fine = Mesh(mesh.devices.reshape(4, 2, 2, 8, 2), HA + ("wa", "dp"))
    tile = P("dp", HA, "wa", None)
    block = P(HA, "wa")
    return jax.shard_map(
        body,
        mesh=fine,
        in_specs=(tile, tile, P(), P(), P(), P(), P(), P()),
        out_specs=(tile, block, block, block, block, P(), P()),
        check_vma=False,
    )
```

```python
import functools

import jax
import jax.numpy as jnp
from jax import lax
from jax.experimental import pallas as pl
from jax.experimental.pallas import tpu as pltpu
from jax.sharding import Mesh, PartitionSpec as P

HEADS = 12
GRID = 7
EPSILON = 1e-05
SLOTS = 128
ROWS = 64
LINES = 14
QUAD = 4
F32 = jnp.float32
BF16 = jnp.bfloat16
HA = ("y", "xl", "core")


def dot(left, right):
    return jnp.dot(left, right, preferred_element_type=F32)


def dot_nt(left, right):
    return lax.dot_general(left, right, (((1,), (1,)), ((), ())), preferred_element_type=F32)


def dot_tn(left, right):
    return lax.dot_general(left, right, (((0,), (0,)), ((), ())), preferred_element_type=F32)


def iota(shape, dim):
    return lax.broadcasted_iota(jnp.int32, shape, dim)


def position():
    rows = (lax.axis_index("y") * 2 + lax.axis_index("xl")) * 2 + lax.axis_index("core")
    return rows, lax.axis_index("wa")


def group_match(slot, member):
    row, col = position()
    parity, local = member >> 6, member & 63
    band_row = (local * 37) >> 8
    band_col = local - GRID * band_row
    offset_row = row + 16 * parity + 32 * band_row - LINES * (slot >> 3)
    offset_col = col + 8 * band_col - GRID * (slot & 7)
    hit = jnp.logical_and(offset_row >= 0, offset_row < LINES)
    hit = jnp.logical_and(hit, jnp.logical_and(offset_col >= 0, offset_col < GRID))
    return jnp.logical_and(hit, local < GRID * GRID)


def owner_slot(line, column):
    row, col = position()
    return ((LINES * row + line) & 15) * 8 + ((GRID * col + column) & 7)


def one_hot(hit):
    return jnp.where(hit, 1.0, 0.0).astype(BF16)


def norm_parts(values):
    centered = values - jnp.mean(values, axis=-1, keepdims=True)
    inv_std = lax.rsqrt(jnp.mean(centered * centered, axis=-1, keepdims=True) + EPSILON)
    return centered * inv_std, inv_std


def norm_back(grad, normal_hat, inv_std, gain):
    grad_hat = grad * gain
    first = jnp.mean(grad_hat, axis=-1, keepdims=True)
    second = jnp.mean(grad_hat * normal_hat, axis=-1, keepdims=True)
    return inv_std * (grad_hat - first - normal_hat * second)


def head_mask(shape):
    return (iota(shape, 0) >> 6) == (iota(shape, 1) >> 5)


def spread(values, mask):
    tiled = jnp.concatenate([values] * QUAD, axis=0)
    return jnp.where(mask, tiled, jnp.zeros_like(tiled))


def gather_heads(values):
    lanes = iota((ROWS, 128), 1) >> 5
    total = jnp.where(lanes == 0, values[:ROWS], 0.0)
    for head in range(1, QUAD):
        total = total + jnp.where(lanes == head, values[head * ROWS : (head + 1) * ROWS], 0.0)
    return total


def probabilities(key, query_spread, scale):
    scores = dot_nt(key, query_spread) * scale
    expo = jnp.where(iota(scores.shape, 0) < GRID * GRID, jnp.exp(scores), 0.0)
    return expo * (1.0 / jnp.sum(expo, axis=0, keepdims=True))


def load_every(ref, start, step):
    parts = [ref[part, pl.ds(start, SLOTS, stride=step), :] for part in range(3)]
    return jnp.concatenate(parts, axis=1).astype(BF16)


def send_kernel(tokens_hbm, grad_hbm, out_ref, tokens_ref, grad_ref, sems):
    copies = [
        pltpu.make_async_copy(tokens_hbm, tokens_ref, sems.at[0]),
        pltpu.make_async_copy(grad_hbm, grad_ref, sems.at[1]),
    ]
    for copy in copies:
        copy.start()
    for copy in copies:
        copy.wait()
    for line in range(16):
        for column in range(8):
            slot = owner_slot(line, column)
            if line < LINES and column < GRID:
                unit = jnp.concatenate(
                    [tokens_ref[line, column].astype(F32), grad_ref[line, column].astype(F32)], axis=0
                ).astype(BF16)
            else:
                unit = jnp.zeros((8, 384), BF16)
            out_ref[slot] = unit


def return_kernel(recv_ref, out_ref):
    for line in range(LINES):
        for column in range(GRID):
            slot = owner_slot(line, column)
            for part in range(3):
                out_ref[line, column, :, part * 128 : (part + 1) * 128] = recv_ref[slot, part]


def gelu_parts(hidden, grad):
    inner, cubic = 0.7978845608028654, 0.7978845608028654 * 0.044715
    square = hidden * hidden
    part = 0.5 * jnp.tanh(hidden * (inner + cubic * square)) + 0.5
    twice = hidden * (2 * inner + 6 * cubic * square)
    slope = part * (1.0 + (1.0 - part) * twice)
    return hidden * part, grad * slope


def forward_kernel(
    recv_ref, gain_one, w_qkv, w_proj,
    x_ref, qkv_ref, mixed_ref, resid_ref, grad_ref, arrived, normed,
):
    for part in range(3):
        arrived[part] = recv_ref[:, part * 128 : (part + 1) * 128].astype(F32)
    match = one_hot(group_match(iota((SLOTS, SLOTS), 1), iota((SLOTS, SLOTS), 0)))
    for crop in range(4):
        rows = pl.ds(crop * SLOTS, SLOTS)
        x = dot(match, load_every(arrived, crop, 8))
        x_ref[rows, :] = x.astype(BF16)
        normal_hat, _ = norm_parts(x)
        normed[rows, :] = (normal_hat * gain_one[...]).astype(BF16)
        grad_ref[rows, :] = dot(match, load_every(arrived, crop + 4, 8)).astype(BF16)
    for part in range(3):
        cols = pl.ds(part * 384, 384)
        qkv_ref[:, cols] = dot_nt(normed[...], w_qkv[cols, :]).astype(BF16)
    mask = head_mask((QUAD * ROWS, 128))
    scale = 32.0 ** -0.5

    @pl.loop(0, 4)
    def _(pair):
        units = unit_places(pair)
        query = [spread(qkv_ref[rows, pl.ds(lane, 128)], mask) for rows, lane in units]
        probs = [
            probabilities(qkv_ref[rows, pl.ds(384 + lane, 128)], query[n], scale).astype(BF16)
            for n, (rows, lane) in enumerate(units)
        ]
        mixed = [
            dot_tn(probs[n], qkv_ref[rows, pl.ds(768 + lane, 128)])
            for n, (rows, lane) in enumerate(units)
        ]
        for n, (rows, lane) in enumerate(units):
            mixed_ref[rows, pl.ds(lane, 128)] = gather_heads(mixed[n]).astype(BF16)

    for crop in range(4):
        rows = pl.ds(crop * SLOTS, SLOTS)
        branch = dot_nt(mixed_ref[rows, :], w_proj[...]).astype(BF16)
        resid_ref[rows, :] = (x_ref[rows, :].astype(F32) + branch.astype(F32)).astype(BF16)


def unit_places(pair):
    places = []
    for half in range(2):
        rows = pl.ds(pl.multiple_of(pair * 2 * ROWS + half * ROWS, ROWS), ROWS)
        places.extend((rows, quad * 128) for quad in range(3))
    return places


def mlp_kernel(
    grad_out, resid, gain_two, w_up, w_down,
    resid_grad_ref, keep_ref, send_ref, gain_ref,
    normed, hidden_grad, grad_turned, up_total, down_total, back, piece_rows,
):
    for crop in range(4):
        rows = pl.ds(crop * SLOTS, SLOTS)
        normal_hat, _ = norm_parts(resid[rows, :].astype(F32))
        normed[rows, :] = (normal_hat * gain_two[...]).astype(BF16)
        grad_turned[:, rows] = grad_out[rows, :].astype(F32).T.astype(BF16)
    for chunk in range(4):
        cols = pl.ds(chunk * 384, 384)
        hidden = dot_nt(normed[...], w_up[cols, :])
        grad_act = dot(grad_out[...], w_down[:, cols])
        activated, grad_hidden = gelu_parts(hidden, grad_act)
        hidden_grad[:, cols] = grad_hidden.astype(BF16)
        down_total[:, cols] = dot(grad_turned[...], activated.astype(BF16))
        up_total[cols, :] = dot_tn(hidden_grad[:, cols], normed[...])
    back[...] = dot(hidden_grad[...], w_up[...])

    for ref, side in piece_sides(keep_ref, send_ref):
        for piece in range(8):
            owner = 2 * piece + side
            piece_rows[:96, :] = up_total[pl.ds(pl.multiple_of(owner * 96, 8), 96), :]
            for part in range(4):
                piece_rows[96 + 24 * part : 120 + 24 * part, :] = down_total[
                    pl.ds(pl.multiple_of(owner * 24, 8), 24), part * 384 : (part + 1) * 384
                ]
            ref[piece] = piece_rows[...].astype(BF16)
    gain = jnp.zeros((1, 384), F32)
    for crop in range(4):
        rows = pl.ds(crop * SLOTS, SLOTS)
        normal_hat, inv_std = norm_parts(resid[rows, :].astype(F32))
        grad = back[rows, :]
        gain = gain + jnp.sum(grad * normal_hat, axis=0, keepdims=True)
        resid_grad_ref[rows, :] = (
            grad_out[rows, :].astype(F32) + norm_back(grad, normal_hat, inv_std, gain_two[...])
        ).astype(BF16)
    gain_ref[...] = gain


def piece_sides(keep_ref, send_ref):
    core = lax.axis_index("core")
    return (keep_ref, core), (send_ref, 1 - core)


def attention_kernel(
    x_ref, qkv_ref, resid_grad_ref, gain_one, w_qkv, w_proj,
    out_ref, rows_grad, normed_ref, gain_ref, grad_mixed, slots,
):
    grad_mixed[...] = dot(resid_grad_ref[...], w_proj[...]).astype(BF16)
    mask = head_mask((QUAD * ROWS, 128))
    scale = 32.0 ** -0.5

    @pl.loop(0, 4)
    def _(pair):
        units = unit_places(pair)
        count = range(len(units))
        query = [spread(qkv_ref[rows, pl.ds(lane, 128)], mask) for rows, lane in units]
        grad = [spread(grad_mixed[rows, pl.ds(lane, 128)], mask) for rows, lane in units]
        key = [qkv_ref[rows, pl.ds(384 + lane, 128)] for rows, lane in units]
        probs = [probabilities(key[n], query[n], scale) for n in count]
        grad_probs = [
            dot_nt(qkv_ref[rows, pl.ds(768 + lane, 128)], grad[n])
            for n, (rows, lane) in enumerate(units)
        ]
        grad_scores = []
        for n in count:
            centre = jnp.sum(grad_probs[n] * probs[n], axis=0, keepdims=True)
            grad_scores.append((probs[n] * (grad_probs[n] - centre) * scale).astype(BF16))
        for n, (rows, lane) in enumerate(units):
            rows_grad[rows, pl.ds(768 + lane, 128)] = dot(probs[n].astype(BF16), grad[n]).astype(BF16)
            rows_grad[rows, pl.ds(384 + lane, 128)] = dot(grad_scores[n], query[n]).astype(BF16)
            rows_grad[rows, pl.ds(lane, 128)] = gather_heads(
                dot_tn(grad_scores[n], key[n])
            ).astype(BF16)

    match = one_hot(group_match(iota((SLOTS, SLOTS), 0), iota((SLOTS, SLOTS), 1)))
    gain = jnp.zeros((1, 384), F32)
    for crop in range(4):
        rows = pl.ds(crop * SLOTS, SLOTS)
        grad = dot(rows_grad[rows, :], w_qkv[...]).astype(BF16).astype(F32)
        normal_hat, inv_std = norm_parts(x_ref[rows, :].astype(F32))
        normed_ref[rows, :] = (normal_hat * gain_one[...]).astype(BF16)
        gain = gain + jnp.sum(grad * normal_hat, axis=0, keepdims=True)
        grad_x = resid_grad_ref[rows, :].astype(F32) + norm_back(
            grad, normal_hat, inv_std, gain_one[...]
        )
        returned = dot(match, grad_x.astype(BF16))
        for part in range(3):
            slots[pl.ds(part * 4 + crop, SLOTS, stride=12), :] = returned[
                :, part * 128 : (part + 1) * 128
            ]
    for slot in range(SLOTS):
        for part in range(3):
            start = slot * 12 + part * 4
            out_ref[slot, part] = slots[start : start + 4, :].astype(BF16)
    gain_ref[...] = gain


def weight_kernel(
    rows_grad, normed, resid_grad, mixed, first, second, keep_ref, send_ref,
    qkv_total, proj_total, piece_rows,
):
    for part in range(3):
        cols = pl.ds(part * 384, 384)
        qkv_total[cols, :] = dot_tn(rows_grad[:, cols], normed[...])
    proj_total[...] = dot_tn(resid_grad[...], mixed[...])
    piece_rows[96:, :] = jnp.zeros((16, 384), F32)
    piece_rows[96:97, :] = first[...]
    piece_rows[97:98, :] = second[...]
    for ref, side in piece_sides(keep_ref, send_ref):
        for piece in range(8):
            owner = 2 * piece + side
            piece_rows[:72, :] = qkv_total[pl.ds(pl.multiple_of(owner * 72, 8), 72), :]
            piece_rows[72:96, :] = proj_total[pl.ds(pl.multiple_of(owner * 24, 8), 24), :]
            ref[piece] = piece_rows[...].astype(BF16)


def core_kernel(
    early_keep, early_recv, late_keep, late_recv, own, near, back, far_low, far_high,
):
    row = lax.axis_index("y")

    def put(ref, step, col):
        piece = ((row + step) & 3) * 2 + col
        early = early_keep[piece].astype(F32) + early_recv[piece].astype(F32)
        late = late_keep[piece].astype(F32) + late_recv[piece].astype(F32)
        ref[:192] = early.astype(BF16)
        if step == 2:
            late = jnp.concatenate([late[:96], pltpu.roll(late[96:], 2, 0)], axis=0)
        ref[192:] = late.astype(BF16)

    for ref, step in ((own, 0), (near, 1), (back, 3)):
        for col in range(2):
            put(ref.at[col], step, col)
    put(far_low, 2, 0)
    put(far_high, 2, 1)


def ring_kernel(near, back, far_low, far_high, out_near, out_back):
    out_near[0] = (near[0].astype(F32) + far_low[...].astype(F32)).astype(BF16)
    out_near[1] = near[1]
    out_back[0] = back[0]
    out_back[1] = (back[1].astype(F32) + far_high[...].astype(F32)).astype(BF16)


def row_kernel(own, near, back, keep_ref, send_ref, gains):
    row, col = lax.axis_index("y"), lax.axis_index("xl")
    first, second, third = (ref[0, 288:].astype(F32) for ref in (own, near, back))
    gains[row] = first
    gains[(row + 3) & 3] = second
    gains[(row + 1) & 3] = third
    gains[(row + 2) & 3] = pltpu.roll(second, 14, 0)
    gain = ((gains[0] + gains[1]) + (gains[2] + gains[3])).astype(BF16)
    for ref, side in ((keep_ref, col), (send_ref, 1 - col)):
        total = own[side, :288].astype(F32) + near[side, :288].astype(F32)
        ref[:288] = (total + back[side, :288].astype(F32)).astype(BF16)
        ref[288:] = gain


def pack_columns(rows, col):
    low = pltpu.roll(rows[:48], (384 - 48 * col) % 384, 1)[:, :128]
    high = pltpu.roll(rows[48:96], (384 + 64 - 48 * col) % 384, 1)[:, :128]
    return jnp.where(iota((48, 128), 1) < 64, low, high)


def pack_kernel(keep_ref, recv_ref, out_ref):
    total = keep_ref[...].astype(F32) + recv_ref[...].astype(F32)
    gain_rows = [
        total[288 + which : 289 + which, part * 128 : (part + 1) * 128]
        for which in range(2)
        for part in range(3)
    ]
    gain_rows.append(jnp.zeros((2, 128), F32))
    for col in range(8):
        start = 96 + 24 * (col // 2)
        block = total[start : start + 24]
        if col % 2:
            block = pltpu.roll(block, 192, 1)
        out_ref[col] = jnp.concatenate(
            [pack_columns(total[:96], col), block[:, :128], block[:, 128:256]]
            + [pack_columns(total[192:288], col)] + gain_rows,
            axis=0,
        ).astype(BF16)


def block_sum(recv_ref, out_ref):
    total = recv_ref[0].astype(F32)
    for place in range(1, 8):
        total = total + recv_ref[place].astype(F32)
    out_ref[...] = total.astype(BF16)


def unpack_columns(packed):
    low = packed[:, :48]
    high = pltpu.roll(packed, 64, 1)[:, :48]
    wide = jnp.concatenate([low, high], axis=0)
    wide = jnp.concatenate([wide, jnp.zeros((96, 80), F32)], axis=1)
    wide = jnp.concatenate([wide, jnp.zeros((32, 128), F32)], axis=0)
    return wide.T[:48]


def final_weights(
    own_ref, other_ref,
    qkv_ref, proj_ref, up_ref, down_ref, first_ref, second_ref, factor,
):
    total = (own_ref[...].astype(F32) + other_ref[...].astype(F32)) * factor
    early, late = total[:96], total[96:]
    up_ref[...] = unpack_columns(early[:48])[:, :96]
    down_ref[:, :128] = early[48:72]
    down_ref[:, 128:] = early[72:96, :64]
    qkv_ref[...] = unpack_columns(late[:48])[:, :72]
    proj_ref[...] = pltpu.roll(late[:48], 64, 1)[24:48, :48]
    for part in range(3):
        lane = pl.ds(part * 128, 128)
        first_ref[lane] = late[48 + part]
        second_ref[lane] = late[51 + part]


def call(kernel, outs, scratch=(), flops=0, nbytes=0, space=pltpu.VMEM, limit=16):
    vmem = pl.BlockSpec(memory_space=pltpu.VMEM)
    scratch = [pltpu.VMEM(*item) if isinstance(item, tuple) else item for item in scratch]

    def run(*args):
        return pl.pallas_call(
            kernel,
            out_shape=[jax.ShapeDtypeStruct(shape, dtype) for shape, dtype in outs],
            in_specs=[pl.BlockSpec(memory_space=space)] * len(args),
            out_specs=[vmem] * len(outs),
            scratch_shapes=scratch,
            compiler_params=pltpu.CompilerParams(vmem_limit_bytes=limit << 20),
            cost_estimate=pl.CostEstimate(flops=flops, bytes_accessed=nbytes, transcendentals=0),
        )(*args)

    return run


def exchange(values, axes):
    return lax.all_to_all(values, axes, split_axis=0, concat_axis=0, tiled=True)


def swap(values, axis):
    return lax.ppermute(values, axis, [(0, 1), (1, 0)])


def shift(values, step):
    return lax.ppermute(values, "y", [(place, (place + step) % 4) for place in range(4)])


def body(tokens, grad_out, gain_first, gain_second, w_qkv, w_proj, w_up, w_down):
    gain_one, gain_two = gain_first.reshape(1, 384), gain_second.reshape(1, 384)
    factor = (8 * 224 * 56) ** -0.5
    tile = pltpu.VMEM((LINES, GRID, 4, 384), BF16)
    (sent,) = call(
        send_kernel,
        [((SLOTS, 8, 384), BF16)],
        [tile, tile, pltpu.SemaphoreType.DMA((2,))],
        nbytes=2 * 10**6,
        space=pl.ANY,
        limit=60,
    )(
        tokens.transpose(1, 2, 0, 3), grad_out.transpose(1, 2, 0, 3)
    )
    arrived = exchange(sent, HA + ("wa",)).reshape(SLOTS * 8, 384)
    rows = ((512, 384), BF16)
    x, qkv, mixed, resid, grad_rows = call(
        forward_kernel,
        [rows, ((512, 1152), BF16), rows, rows, rows],
        [((3, 1024, 128), F32), rows],
        flops=10**9, nbytes=4 * 10**6,
    )(arrived, gain_one, w_qkv, w_proj)
    resid_grad, early_keep, early_send, gain_sum_two = call(
        mlp_kernel,
        [rows, ((8, 192, 384), BF16), ((8, 192, 384), BF16), ((1, 384), F32)],
        [
            rows, ((512, 1536), BF16), ((384, 512), BF16), ((1536, 384), F32), ((384, 1536), F32),
            ((512, 384), F32), ((192, 384), F32),
        ],
        flops=3 * 10**9, nbytes=6 * 10**6,
    )(grad_rows, resid, gain_two, w_up, w_down)
    slots, rows_grad, normed, gain_sum_one = call(
        attention_kernel,
        [((SLOTS, 3, 4, 128), BF16), ((512, 1152), BF16), rows, ((1, 384), F32)],
        [rows, ((SLOTS * 12, 128), F32)],
        flops=6 * 10**9, nbytes=20 * 10**6,
    )(x, qkv, resid_grad, gain_one, w_qkv, w_proj)
    late_keep, late_send = call(
        weight_kernel,
        [((8, 112, 384), BF16), ((8, 112, 384), BF16)],
        [((1152, 384), F32), ((384, 384), F32), ((112, 384), F32)],
        flops=10**9, nbytes=5 * 10**6,
    )(rows_grad, normed, resid_grad, mixed, gain_sum_one, gain_sum_two)
    whole, half = ((2, 304, 384), BF16), ((304, 384), BF16)
    own, near, back, low, high = call(core_kernel, [whole, whole, whole, half, half], nbytes=10**7)(
        early_keep, swap(early_send, "core"), late_keep, swap(late_send, "core")
    )
    near, back = call(ring_kernel, [whole, whole], nbytes=4 * 10**6)(
        near, back, shift(low, 1), shift(high, 3)
    )
    slots, near, back = lax.optimization_barrier((slots, near, back))
    returned = exchange(slots, HA + ("wa",))
    keep, send = call(row_kernel, [half, half], [((4, 16, 384), F32)], nbytes=3 * 10**6)(
        own, shift(near, 1), shift(back, 3)
    )
    (blocks,) = call(pack_kernel, [((8, 152, 128), BF16)], nbytes=10**6)(keep, swap(send, "xl"))
    blocks, returned = lax.optimization_barrier((blocks, returned))
    (total,) = call(block_sum, [((152, 128), BF16)], nbytes=10**6)(exchange(blocks, "wa"))
    other = swap(total, "dp")
    grad_qkv, grad_proj, grad_up, grad_down, first, second = call(
        functools.partial(final_weights, factor=factor),
        [
            ((48, 72), F32), ((24, 48), F32), ((48, 96), F32), ((24, 192), F32),
            ((384,), F32), ((384,), F32),
        ],
        nbytes=10**6,
    )(total, other)
    (grad_tile,) = call(return_kernel, [((LINES, GRID, 4, 384), BF16)], nbytes=10**6)(returned)
    return (
        grad_tile.transpose(2, 0, 1, 3), grad_qkv.T, grad_proj, grad_up.T, grad_down, first, second,
    )


def solution(mesh):
    fine = Mesh(mesh.devices.reshape(4, 2, 2, 8, 2), HA + ("wa", "dp"))
    tile = P("dp", HA, "wa", None)
    block = P(HA, "wa")
    return jax.shard_map(
        body,
        mesh=fine,
        in_specs=(tile, tile, P(), P(), P(), P(), P(), P()),
        out_specs=(tile, block, block, block, block, P(), P()),
        check_vma=False,
    )
```

```python
import functools

import jax
import jax.numpy as jnp
from jax import lax
from jax.experimental import pallas as pl
from jax.experimental.pallas import tpu as pltpu
from jax.sharding import Mesh, PartitionSpec as P

HEADS = 12
GRID = 7
EPSILON = 1e-05
SLOTS = 128
ROWS = 64
LINES = 14
QUAD = 4
F32 = jnp.float32
BF16 = jnp.bfloat16
HA = ("y", "xl", "core")


def dot(left, right):
    return jnp.dot(left, right, preferred_element_type=F32)


def dot_nt(left, right):
    return lax.dot_general(left, right, (((1,), (1,)), ((), ())), preferred_element_type=F32)


def dot_tn(left, right):
    return lax.dot_general(left, right, (((0,), (0,)), ((), ())), preferred_element_type=F32)


def iota(shape, dim):
    return lax.broadcasted_iota(jnp.int32, shape, dim)


def position():
    rows = (lax.axis_index("y") * 2 + lax.axis_index("xl")) * 2 + lax.axis_index("core")
    return rows, lax.axis_index("wa")


def group_match(slot, member):
    row, col = position()
    parity, local = member >> 6, member & 63
    band_row = (local * 37) >> 8
    band_col = local - GRID * band_row
    offset_row = row + 16 * parity + 32 * band_row - LINES * (slot >> 3)
    offset_col = col + 8 * band_col - GRID * (slot & 7)
    hit = jnp.logical_and(offset_row >= 0, offset_row < LINES)
    hit = jnp.logical_and(hit, jnp.logical_and(offset_col >= 0, offset_col < GRID))
    return jnp.logical_and(hit, local < GRID * GRID)


def owner_slot(line, column):
    row, col = position()
    return ((LINES * row + line) & 15) * 8 + ((GRID * col + column) & 7)


def one_hot(hit):
    return jnp.where(hit, 1.0, 0.0).astype(BF16)


def norm_parts(values):
    centered = values - jnp.mean(values, axis=-1, keepdims=True)
    inv_std = lax.rsqrt(jnp.mean(centered * centered, axis=-1, keepdims=True) + EPSILON)
    return centered * inv_std, inv_std


def norm_back(grad, normal_hat, inv_std, gain):
    grad_hat = grad * gain
    first = jnp.mean(grad_hat, axis=-1, keepdims=True)
    second = jnp.mean(grad_hat * normal_hat, axis=-1, keepdims=True)
    return inv_std * (grad_hat - first - normal_hat * second)


def head_mask(shape):
    return (iota(shape, 0) >> 6) == (iota(shape, 1) >> 5)


def spread(values, mask):
    tiled = jnp.concatenate([values] * QUAD, axis=0)
    return jnp.where(mask, tiled, jnp.zeros_like(tiled))


def gather_heads(values):
    lanes = iota((ROWS, 128), 1) >> 5
    total = jnp.where(lanes == 0, values[:ROWS], 0.0)
    for head in range(1, QUAD):
        total = total + jnp.where(lanes == head, values[head * ROWS : (head + 1) * ROWS], 0.0)
    return total


def probabilities(key, query_spread, scale):
    scores = dot_nt(key, query_spread) * scale
    expo = jnp.where(iota(scores.shape, 0) < GRID * GRID, jnp.exp(scores), 0.0)
    return expo * (1.0 / jnp.sum(expo, axis=0, keepdims=True))


def load_every(ref, start, step):
    parts = [ref[part, pl.ds(start, SLOTS, stride=step), :] for part in range(3)]
    return jnp.concatenate(parts, axis=1).astype(BF16)


def send_kernel(tokens_hbm, grad_hbm, out_ref, tokens_ref, grad_ref, sems):
    copies = [
        pltpu.make_async_copy(tokens_hbm, tokens_ref, sems.at[0]),
        pltpu.make_async_copy(grad_hbm, grad_ref, sems.at[1]),
    ]
    for copy in copies:
        copy.start()
    for copy in copies:
        copy.wait()
    for line in range(16):
        for column in range(8):
            slot = owner_slot(line, column)
            if line < LINES and column < GRID:
                unit = jnp.concatenate(
                    [tokens_ref[line, column].astype(F32), grad_ref[line, column].astype(F32)], axis=0
                ).astype(BF16)
            else:
                unit = jnp.zeros((8, 384), BF16)
            out_ref[slot] = unit


def return_kernel(recv_ref, out_ref):
    for line in range(LINES):
        for column in range(GRID):
            slot = owner_slot(line, column)
            for part in range(3):
                out_ref[line, column, :, part * 128 : (part + 1) * 128] = recv_ref[slot, part]


def gelu_parts(hidden, grad):
    inner, cubic = 0.7978845608028654, 0.7978845608028654 * 0.044715
    square = hidden * hidden
    part = 0.5 * jnp.tanh(hidden * (inner + cubic * square)) + 0.5
    twice = hidden * (2 * inner + 6 * cubic * square)
    slope = part * (1.0 + (1.0 - part) * twice)
    return hidden * part, grad * slope


def forward_kernel(
    recv_ref, gain_one, w_qkv, w_proj,
    x_ref, qkv_ref, mixed_ref, resid_ref, grad_ref, arrived, normed,
):
    for part in range(3):
        arrived[part] = recv_ref[:, part * 128 : (part + 1) * 128].astype(F32)
    match = one_hot(group_match(iota((SLOTS, SLOTS), 1), iota((SLOTS, SLOTS), 0)))
    for crop in range(4):
        rows = pl.ds(crop * SLOTS, SLOTS)
        x = dot(match, load_every(arrived, crop, 8))
        x_ref[rows, :] = x.astype(BF16)
        normal_hat, _ = norm_parts(x)
        normed[rows, :] = (normal_hat * gain_one[...]).astype(BF16)
        grad_ref[rows, :] = dot(match, load_every(arrived, crop + 4, 8)).astype(BF16)
    for part in range(3):
        cols = pl.ds(part * 384, 384)
        qkv_ref[:, cols] = dot_nt(normed[...], w_qkv[cols, :]).astype(BF16)
    mask = head_mask((QUAD * ROWS, 128))
    scale = 32.0 ** -0.5

    @pl.loop(0, 2)
    def _(part):
        units = unit_places(part)
        query = [spread(qkv_ref[rows, pl.ds(lane, 128)], mask) for rows, lane in units]
        probs = [
            probabilities(qkv_ref[rows, pl.ds(384 + lane, 128)], query[n], scale).astype(BF16)
            for n, (rows, lane) in enumerate(units)
        ]
        mixed = [
            dot_tn(probs[n], qkv_ref[rows, pl.ds(768 + lane, 128)])
            for n, (rows, lane) in enumerate(units)
        ]
        for n, (rows, lane) in enumerate(units):
            mixed_ref[rows, pl.ds(lane, 128)] = gather_heads(mixed[n]).astype(BF16)

    for crop in range(4):
        rows = pl.ds(crop * SLOTS, SLOTS)
        branch = dot_nt(mixed_ref[rows, :], w_proj[...]).astype(BF16)
        resid_ref[rows, :] = (x_ref[rows, :].astype(F32) + branch.astype(F32)).astype(BF16)


def unit_places(part):
    places = []
    for group in range(4):
        rows = pl.ds(pl.multiple_of((part * 4 + group) * ROWS, ROWS), ROWS)
        places.extend((rows, quad * 128) for quad in range(3))
    return places


def mlp_kernel(
    grad_out, resid, gain_two, w_up, w_down,
    resid_grad_ref, keep_ref, send_ref, gain_ref,
    normed, hidden_grad, grad_turned, up_total, down_total, back, piece_rows,
):
    for crop in range(4):
        rows = pl.ds(crop * SLOTS, SLOTS)
        normal_hat, _ = norm_parts(resid[rows, :].astype(F32))
        normed[rows, :] = (normal_hat * gain_two[...]).astype(BF16)
        grad_turned[:, rows] = grad_out[rows, :].astype(F32).T.astype(BF16)
    for chunk in range(4):
        cols = pl.ds(chunk * 384, 384)
        hidden = dot_nt(normed[...], w_up[cols, :])
        grad_act = dot(grad_out[...], w_down[:, cols])
        activated, grad_hidden = gelu_parts(hidden, grad_act)
        hidden_grad[:, cols] = grad_hidden.astype(BF16)
        down_total[:, cols] = dot(grad_turned[...], activated.astype(BF16))
        up_total[cols, :] = dot_tn(hidden_grad[:, cols], normed[...])
    back[...] = dot(hidden_grad[...], w_up[...])

    for ref, side in piece_sides(keep_ref, send_ref):
        for piece in range(8):
            owner = 2 * piece + side
            piece_rows[:96, :] = up_total[pl.ds(pl.multiple_of(owner * 96, 8), 96), :]
            for part in range(4):
                piece_rows[96 + 24 * part : 120 + 24 * part, :] = down_total[
                    pl.ds(pl.multiple_of(owner * 24, 8), 24), part * 384 : (part + 1) * 384
                ]
            ref[piece] = piece_rows[...].astype(BF16)
    gain = jnp.zeros((1, 384), F32)
    for crop in range(4):
        rows = pl.ds(crop * SLOTS, SLOTS)
        normal_hat, inv_std = norm_parts(resid[rows, :].astype(F32))
        grad = back[rows, :]
        gain = gain + jnp.sum(grad * normal_hat, axis=0, keepdims=True)
        resid_grad_ref[rows, :] = (
            grad_out[rows, :].astype(F32) + norm_back(grad, normal_hat, inv_std, gain_two[...])
        ).astype(BF16)
    gain_ref[...] = gain


def piece_sides(keep_ref, send_ref):
    core = lax.axis_index("core")
    return (keep_ref, core), (send_ref, 1 - core)


def attention_kernel(
    x_ref, qkv_ref, resid_grad_ref, gain_one, w_qkv, w_proj,
    out_ref, rows_grad, normed_ref, gain_ref, grad_mixed, slots,
):
    grad_mixed[...] = dot(resid_grad_ref[...], w_proj[...]).astype(BF16)
    mask = head_mask((QUAD * ROWS, 128))
    scale = 32.0 ** -0.5

    @pl.loop(0, 2)
    def _(part):
        units = unit_places(part)
        count = range(len(units))
        query = [spread(qkv_ref[rows, pl.ds(lane, 128)], mask) for rows, lane in units]
        grad = [spread(grad_mixed[rows, pl.ds(lane, 128)], mask) for rows, lane in units]
        key = [qkv_ref[rows, pl.ds(384 + lane, 128)] for rows, lane in units]
        probs = [probabilities(key[n], query[n], scale) for n in count]
        grad_probs = [
            dot_nt(qkv_ref[rows, pl.ds(768 + lane, 128)], grad[n])
            for n, (rows, lane) in enumerate(units)
        ]
        grad_scores = []
        for n in count:
            centre = jnp.sum(grad_probs[n] * probs[n], axis=0, keepdims=True)
            grad_scores.append((probs[n] * (grad_probs[n] - centre) * scale).astype(BF16))
        for n, (rows, lane) in enumerate(units):
            rows_grad[rows, pl.ds(768 + lane, 128)] = dot(probs[n].astype(BF16), grad[n]).astype(BF16)
            rows_grad[rows, pl.ds(384 + lane, 128)] = dot(grad_scores[n], query[n]).astype(BF16)
            rows_grad[rows, pl.ds(lane, 128)] = gather_heads(
                dot_tn(grad_scores[n], key[n])
            ).astype(BF16)

    match = one_hot(group_match(iota((SLOTS, SLOTS), 0), iota((SLOTS, SLOTS), 1)))
    gain = jnp.zeros((1, 384), F32)
    for crop in range(4):
        rows = pl.ds(crop * SLOTS, SLOTS)
        grad = dot(rows_grad[rows, :], w_qkv[...]).astype(BF16).astype(F32)
        normal_hat, inv_std = norm_parts(x_ref[rows, :].astype(F32))
        normed_ref[rows, :] = (normal_hat * gain_one[...]).astype(BF16)
        gain = gain + jnp.sum(grad * normal_hat, axis=0, keepdims=True)
        grad_x = resid_grad_ref[rows, :].astype(F32) + norm_back(
            grad, normal_hat, inv_std, gain_one[...]
        )
        returned = dot(match, grad_x.astype(BF16))
        for part in range(3):
            slots[pl.ds(part * 4 + crop, SLOTS, stride=12), :] = returned[
                :, part * 128 : (part + 1) * 128
            ]
    for slot in range(SLOTS):
        for part in range(3):
            start = slot * 12 + part * 4
            out_ref[slot, part] = slots[start : start + 4, :].astype(BF16)
    gain_ref[...] = gain


def weight_kernel(
    rows_grad, normed, resid_grad, mixed, first, second, keep_ref, send_ref,
    qkv_total, proj_total, piece_rows,
):
    for part in range(3):
        cols = pl.ds(part * 384, 384)
        qkv_total[cols, :] = dot_tn(rows_grad[:, cols], normed[...])
    proj_total[...] = dot_tn(resid_grad[...], mixed[...])
    piece_rows[96:, :] = jnp.zeros((16, 384), F32)
    piece_rows[96:97, :] = first[...]
    piece_rows[97:98, :] = second[...]
    for ref, side in piece_sides(keep_ref, send_ref):
        for piece in range(8):
            owner = 2 * piece + side
            piece_rows[:72, :] = qkv_total[pl.ds(pl.multiple_of(owner * 72, 8), 72), :]
            piece_rows[72:96, :] = proj_total[pl.ds(pl.multiple_of(owner * 24, 8), 24), :]
            ref[piece] = piece_rows[...].astype(BF16)


def core_kernel(
    early_keep, early_recv, late_keep, late_recv, own, near, back, far_low, far_high,
):
    row = lax.axis_index("y")

    def put(ref, step, col):
        piece = ((row + step) & 3) * 2 + col
        early = early_keep[piece].astype(F32) + early_recv[piece].astype(F32)
        late = late_keep[piece].astype(F32) + late_recv[piece].astype(F32)
        ref[:192] = early.astype(BF16)
        if step == 2:
            late = jnp.concatenate([late[:96], pltpu.roll(late[96:], 2, 0)], axis=0)
        ref[192:] = late.astype(BF16)

    for ref, step in ((own, 0), (near, 1), (back, 3)):
        for col in range(2):
            put(ref.at[col], step, col)
    put(far_low, 2, 0)
    put(far_high, 2, 1)


def ring_kernel(near, back, far_low, far_high, out_near, out_back):
    out_near[0] = (near[0].astype(F32) + far_low[...].astype(F32)).astype(BF16)
    out_near[1] = near[1]
    out_back[0] = back[0]
    out_back[1] = (back[1].astype(F32) + far_high[...].astype(F32)).astype(BF16)


def row_kernel(own, near, back, keep_ref, send_ref, gains):
    row, col = lax.axis_index("y"), lax.axis_index("xl")
    first, second, third = (ref[0, 288:].astype(F32) for ref in (own, near, back))
    gains[row] = first
    gains[(row + 3) & 3] = second
    gains[(row + 1) & 3] = third
    gains[(row + 2) & 3] = pltpu.roll(second, 14, 0)
    gain = ((gains[0] + gains[1]) + (gains[2] + gains[3])).astype(BF16)
    for ref, side in ((keep_ref, col), (send_ref, 1 - col)):
        total = own[side, :288].astype(F32) + near[side, :288].astype(F32)
        ref[:288] = (total + back[side, :288].astype(F32)).astype(BF16)
        ref[288:] = gain


def pack_columns(rows, col):
    low = pltpu.roll(rows[:48], (384 - 48 * col) % 384, 1)[:, :128]
    high = pltpu.roll(rows[48:96], (384 + 64 - 48 * col) % 384, 1)[:, :128]
    return jnp.where(iota((48, 128), 1) < 64, low, high)


def pack_kernel(keep_ref, recv_ref, out_ref):
    total = keep_ref[...].astype(F32) + recv_ref[...].astype(F32)
    gain_rows = [
        total[288 + which : 289 + which, part * 128 : (part + 1) * 128]
        for which in range(2)
        for part in range(3)
    ]
    gain_rows.append(jnp.zeros((2, 128), F32))
    for col in range(8):
        start = 96 + 24 * (col // 2)
        block = total[start : start + 24]
        if col % 2:
            block = pltpu.roll(block, 192, 1)
        out_ref[col] = jnp.concatenate(
            [pack_columns(total[:96], col), block[:, :128], block[:, 128:256]]
            + [pack_columns(total[192:288], col)] + gain_rows,
            axis=0,
        ).astype(BF16)


def block_sum(recv_ref, out_ref):
    total = recv_ref[0].astype(F32)
    for place in range(1, 8):
        total = total + recv_ref[place].astype(F32)
    out_ref[...] = total.astype(BF16)


def unpack_columns(packed):
    low = packed[:, :48]
    high = pltpu.roll(packed, 64, 1)[:, :48]
    wide = jnp.concatenate([low, high], axis=0)
    wide = jnp.concatenate([wide, jnp.zeros((96, 80), F32)], axis=1)
    wide = jnp.concatenate([wide, jnp.zeros((32, 128), F32)], axis=0)
    return wide.T[:48]


def final_weights(
    own_ref, other_ref,
    qkv_ref, proj_ref, up_ref, down_ref, first_ref, second_ref, factor,
):
    total = (own_ref[...].astype(F32) + other_ref[...].astype(F32)) * factor
    early, late = total[:96], total[96:]
    up_ref[...] = unpack_columns(early[:48])[:, :96]
    down_ref[:, :128] = early[48:72]
    down_ref[:, 128:] = early[72:96, :64]
    qkv_ref[...] = unpack_columns(late[:48])[:, :72]
    proj_ref[...] = pltpu.roll(late[:48], 64, 1)[24:48, :48]
    for part in range(3):
        lane = pl.ds(part * 128, 128)
        first_ref[lane] = late[48 + part]
        second_ref[lane] = late[51 + part]


def call(kernel, outs, scratch=(), flops=0, nbytes=0, space=pltpu.VMEM, limit=16):
    vmem = pl.BlockSpec(memory_space=pltpu.VMEM)
    scratch = [pltpu.VMEM(*item) if isinstance(item, tuple) else item for item in scratch]

    def run(*args):
        return pl.pallas_call(
            kernel,
            out_shape=[jax.ShapeDtypeStruct(shape, dtype) for shape, dtype in outs],
            in_specs=[pl.BlockSpec(memory_space=space)] * len(args),
            out_specs=[vmem] * len(outs),
            scratch_shapes=scratch,
            compiler_params=pltpu.CompilerParams(vmem_limit_bytes=limit << 20),
            cost_estimate=pl.CostEstimate(flops=flops, bytes_accessed=nbytes, transcendentals=0),
        )(*args)

    return run


def exchange(values, axes):
    return lax.all_to_all(values, axes, split_axis=0, concat_axis=0, tiled=True)


def swap(values, axis):
    return lax.ppermute(values, axis, [(0, 1), (1, 0)])


def shift(values, step):
    return lax.ppermute(values, "y", [(place, (place + step) % 4) for place in range(4)])


def body(tokens, grad_out, gain_first, gain_second, w_qkv, w_proj, w_up, w_down):
    gain_one, gain_two = gain_first.reshape(1, 384), gain_second.reshape(1, 384)
    factor = (8 * 224 * 56) ** -0.5
    tile = pltpu.VMEM((LINES, GRID, 4, 384), BF16)
    (sent,) = call(
        send_kernel,
        [((SLOTS, 8, 384), BF16)],
        [tile, tile, pltpu.SemaphoreType.DMA((2,))],
        nbytes=2 * 10**6,
        space=pl.ANY,
        limit=60,
    )(
        tokens.transpose(1, 2, 0, 3), grad_out.transpose(1, 2, 0, 3)
    )
    arrived = exchange(sent, HA + ("wa",)).reshape(SLOTS * 8, 384)
    rows = ((512, 384), BF16)
    x, qkv, mixed, resid, grad_rows = call(
        forward_kernel,
        [rows, ((512, 1152), BF16), rows, rows, rows],
        [((3, 1024, 128), F32), rows],
        flops=10**9, nbytes=4 * 10**6,
    )(arrived, gain_one, w_qkv, w_proj)
    resid_grad, early_keep, early_send, gain_sum_two = call(
        mlp_kernel,
        [rows, ((8, 192, 384), BF16), ((8, 192, 384), BF16), ((1, 384), F32)],
        [
            rows, ((512, 1536), BF16), ((384, 512), BF16), ((1536, 384), F32), ((384, 1536), F32),
            ((512, 384), F32), ((192, 384), F32),
        ],
        flops=3 * 10**9, nbytes=6 * 10**6,
    )(grad_rows, resid, gain_two, w_up, w_down)
    slots, rows_grad, normed, gain_sum_one = call(
        attention_kernel,
        [((SLOTS, 3, 4, 128), BF16), ((512, 1152), BF16), rows, ((1, 384), F32)],
        [rows, ((SLOTS * 12, 128), F32)],
        flops=6 * 10**9, nbytes=20 * 10**6,
    )(x, qkv, resid_grad, gain_one, w_qkv, w_proj)
    returned = exchange(slots, HA + ("wa",))
    late_keep, late_send = call(
        weight_kernel,
        [((8, 112, 384), BF16), ((8, 112, 384), BF16)],
        [((1152, 384), F32), ((384, 384), F32), ((112, 384), F32)],
        flops=10**9, nbytes=5 * 10**6,
    )(rows_grad, normed, resid_grad, mixed, gain_sum_one, gain_sum_two)
    whole, half = ((2, 304, 384), BF16), ((304, 384), BF16)
    own, near, back, low, high = call(core_kernel, [whole, whole, whole, half, half], nbytes=10**7)(
        early_keep, swap(early_send, "core"), late_keep, swap(late_send, "core")
    )
    near, back = call(ring_kernel, [whole, whole], nbytes=4 * 10**6)(
        near, back, shift(low, 1), shift(high, 3)
    )
    keep, send = call(row_kernel, [half, half], [((4, 16, 384), F32)], nbytes=3 * 10**6)(
        own, shift(near, 1), shift(back, 3)
    )
    (blocks,) = call(pack_kernel, [((8, 152, 128), BF16)], nbytes=10**6)(keep, swap(send, "xl"))
    blocks, returned = lax.optimization_barrier((blocks, returned))
    (total,) = call(block_sum, [((152, 128), BF16)], nbytes=10**6)(exchange(blocks, "wa"))
    other = swap(total, "dp")
    grad_qkv, grad_proj, grad_up, grad_down, first, second = call(
        functools.partial(final_weights, factor=factor),
        [
            ((48, 72), F32), ((24, 48), F32), ((48, 96), F32), ((24, 192), F32),
            ((384,), F32), ((384,), F32),
        ],
        nbytes=10**6,
    )(total, other)
    (grad_tile,) = call(return_kernel, [((LINES, GRID, 4, 384), BF16)], nbytes=10**6)(returned)
    return (
        grad_tile.transpose(2, 0, 1, 3), grad_qkv.T, grad_proj, grad_up.T, grad_down, first, second,
    )


def solution(mesh):
    fine = Mesh(mesh.devices.reshape(4, 2, 2, 8, 2), HA + ("wa", "dp"))
    tile = P("dp", HA, "wa", None)
    block = P(HA, "wa")
    return jax.shard_map(
        body,
        mesh=fine,
        in_specs=(tile, tile, P(), P(), P(), P(), P(), P()),
        out_specs=(tile, block, block, block, block, P(), P()),
        check_vma=False,
    )
```

```python
import functools

import jax
import jax.numpy as jnp
from jax import lax
from jax.experimental import pallas as pl
from jax.experimental.pallas import tpu as pltpu
from jax.sharding import Mesh, PartitionSpec as P

HEADS = 12
GRID = 7
EPSILON = 1e-05
SLOTS = 128
ROWS = 64
LINES = 14
QUAD = 4
F32 = jnp.float32
BF16 = jnp.bfloat16
HA = ("y", "xl", "core")


def dot(left, right):
    return jnp.dot(left, right, preferred_element_type=F32)


def dot_nt(left, right):
    return lax.dot_general(left, right, (((1,), (1,)), ((), ())), preferred_element_type=F32)


def dot_tn(left, right):
    return lax.dot_general(left, right, (((0,), (0,)), ((), ())), preferred_element_type=F32)


def iota(shape, dim):
    return lax.broadcasted_iota(jnp.int32, shape, dim)


def position():
    rows = (lax.axis_index("y") * 2 + lax.axis_index("xl")) * 2 + lax.axis_index("core")
    return rows, lax.axis_index("wa")


def group_match(slot, member):
    row, col = position()
    parity, local = member >> 6, member & 63
    band_row = (local * 37) >> 8
    band_col = local - GRID * band_row
    offset_row = row + 16 * parity + 32 * band_row - LINES * (slot >> 3)
    offset_col = col + 8 * band_col - GRID * (slot & 7)
    hit = jnp.logical_and(offset_row >= 0, offset_row < LINES)
    hit = jnp.logical_and(hit, jnp.logical_and(offset_col >= 0, offset_col < GRID))
    return jnp.logical_and(hit, local < GRID * GRID)


def owner_slot(line, column):
    row, col = position()
    return ((LINES * row + line) & 15) * 8 + ((GRID * col + column) & 7)


def one_hot(hit):
    return jnp.where(hit, 1.0, 0.0).astype(BF16)


def norm_parts(values):
    centered = values - jnp.mean(values, axis=-1, keepdims=True)
    inv_std = lax.rsqrt(jnp.mean(centered * centered, axis=-1, keepdims=True) + EPSILON)
    return centered * inv_std, inv_std


def norm_back(grad, normal_hat, inv_std, gain):
    grad_hat = grad * gain
    first = jnp.mean(grad_hat, axis=-1, keepdims=True)
    second = jnp.mean(grad_hat * normal_hat, axis=-1, keepdims=True)
    return inv_std * (grad_hat - first - normal_hat * second)


def head_mask(shape):
    return (iota(shape, 0) >> 6) == (iota(shape, 1) >> 5)


def spread(values, mask):
    tiled = jnp.concatenate([values] * QUAD, axis=0)
    return jnp.where(mask, tiled, jnp.zeros_like(tiled))


def gather_heads(values):
    lanes = iota((ROWS, 128), 1) >> 5
    total = jnp.where(lanes == 0, values[:ROWS], 0.0)
    for head in range(1, QUAD):
        total = total + jnp.where(lanes == head, values[head * ROWS : (head + 1) * ROWS], 0.0)
    return total


def probabilities(key, query_spread, scale):
    scores = dot_nt(key, query_spread) * scale
    expo = jnp.where(iota(scores.shape, 0) < GRID * GRID, jnp.exp(scores), 0.0)
    return expo * (1.0 / jnp.sum(expo, axis=0, keepdims=True))


def load_every(ref, start, step):
    parts = [ref[part, pl.ds(start, SLOTS, stride=step), :] for part in range(3)]
    return jnp.concatenate(parts, axis=1).astype(BF16)


def send_kernel(tokens_hbm, grad_hbm, out_ref, tokens_ref, grad_ref, sems):
    copies = [
        pltpu.make_async_copy(tokens_hbm, tokens_ref, sems.at[0]),
        pltpu.make_async_copy(grad_hbm, grad_ref, sems.at[1]),
    ]
    for copy in copies:
        copy.start()
    for copy in copies:
        copy.wait()
    for line in range(16):
        for column in range(8):
            slot = owner_slot(line, column)
            if line < LINES and column < GRID:
                unit = jnp.concatenate(
                    [tokens_ref[line, column].astype(F32), grad_ref[line, column].astype(F32)], axis=0
                ).astype(BF16)
            else:
                unit = jnp.zeros((8, 384), BF16)
            out_ref[slot] = unit


def return_kernel(recv_ref, out_ref):
    for line in range(LINES):
        for column in range(GRID):
            slot = owner_slot(line, column)
            for part in range(3):
                out_ref[line, column, :, part * 128 : (part + 1) * 128] = recv_ref[slot, part]


def gelu_parts(hidden, grad):
    inner, cubic = 0.7978845608028654, 0.7978845608028654 * 0.044715
    square = hidden * hidden
    part = 0.5 * jnp.tanh(hidden * (inner + cubic * square)) + 0.5
    twice = hidden * (2 * inner + 6 * cubic * square)
    slope = part * (1.0 + (1.0 - part) * twice)
    return hidden * part, grad * slope


def forward_kernel(
    recv_ref, gain_one, w_qkv, w_proj,
    x_ref, qkv_ref, mixed_ref, resid_ref, grad_ref, arrived, normed,
):
    for part in range(3):
        arrived[part] = recv_ref[:, part * 128 : (part + 1) * 128].astype(F32)
    match = one_hot(group_match(iota((SLOTS, SLOTS), 1), iota((SLOTS, SLOTS), 0)))
    for crop in range(4):
        rows = pl.ds(crop * SLOTS, SLOTS)
        x = dot(match, load_every(arrived, crop, 8))
        x_ref[rows, :] = x.astype(BF16)
        normal_hat, _ = norm_parts(x)
        normed[rows, :] = (normal_hat * gain_one[...]).astype(BF16)
        grad_ref[rows, :] = dot(match, load_every(arrived, crop + 4, 8)).astype(BF16)
    for part in range(3):
        cols = pl.ds(part * 384, 384)
        qkv_ref[:, cols] = dot_nt(normed[...], w_qkv[cols, :]).astype(BF16)
    mask = head_mask((QUAD * ROWS, 128))
    scale = 32.0 ** -0.5

    @pl.loop(0, 1)
    def _(part):
        units = unit_places()
        query = [spread(qkv_ref[rows, pl.ds(lane, 128)], mask) for rows, lane in units]
        probs = [
            probabilities(qkv_ref[rows, pl.ds(384 + lane, 128)], query[n], scale).astype(BF16)
            for n, (rows, lane) in enumerate(units)
        ]
        mixed = [
            dot_tn(probs[n], qkv_ref[rows, pl.ds(768 + lane, 128)])
            for n, (rows, lane) in enumerate(units)
        ]
        for n, (rows, lane) in enumerate(units):
            mixed_ref[rows, pl.ds(lane, 128)] = gather_heads(mixed[n]).astype(BF16)

    for crop in range(4):
        rows = pl.ds(crop * SLOTS, SLOTS)
        branch = dot_nt(mixed_ref[rows, :], w_proj[...]).astype(BF16)
        resid_ref[rows, :] = (x_ref[rows, :].astype(F32) + branch.astype(F32)).astype(BF16)


def unit_places():
    return [(pl.ds(group * ROWS, ROWS), quad * 128) for group in range(8) for quad in range(3)]


def mlp_kernel(
    grad_out, resid, gain_two, w_up, w_down,
    resid_grad_ref, keep_ref, send_ref, gain_ref,
    normed, hidden_grad, grad_turned, up_total, down_total, back,
):
    for crop in range(4):
        rows = pl.ds(crop * SLOTS, SLOTS)
        normal_hat, _ = norm_parts(resid[rows, :].astype(F32))
        normed[rows, :] = (normal_hat * gain_two[...]).astype(BF16)
        grad_turned[:, rows] = grad_out[rows, :].astype(F32).T.astype(BF16)
    for chunk in range(4):
        cols = pl.ds(chunk * 384, 384)
        hidden = dot_nt(normed[...], w_up[cols, :])
        grad_act = dot(grad_out[...], w_down[:, cols])
        activated, grad_hidden = gelu_parts(hidden, grad_act)
        hidden_grad[:, cols] = grad_hidden.astype(BF16)
        down_total[:, cols] = dot(grad_turned[...], activated.astype(BF16))
        up_total[cols, :] = dot_tn(hidden_grad[:, cols], normed[...])
    back[...] = dot(hidden_grad[...], w_up[...])

    for ref, side in piece_sides(keep_ref, send_ref):
        for piece in range(8):
            owner = 2 * piece + side
            ref[piece, :96] = up_total[pl.ds(pl.multiple_of(owner * 96, 8), 96), :].astype(BF16)
            rows = pl.ds(pl.multiple_of(owner * 24, 8), 24)
            ref[piece, 96:] = jnp.concatenate(
                [down_total[rows, part * 384 : (part + 1) * 384] for part in range(4)], axis=0
            ).astype(BF16)
    gain = jnp.zeros((1, 384), F32)
    for crop in range(4):
        rows = pl.ds(crop * SLOTS, SLOTS)
        normal_hat, inv_std = norm_parts(resid[rows, :].astype(F32))
        grad = back[rows, :]
        gain = gain + jnp.sum(grad * normal_hat, axis=0, keepdims=True)
        resid_grad_ref[rows, :] = (
            grad_out[rows, :].astype(F32) + norm_back(grad, normal_hat, inv_std, gain_two[...])
        ).astype(BF16)
    gain_ref[...] = gain


def piece_sides(keep_ref, send_ref):
    core = lax.axis_index("core")
    return (keep_ref, core), (send_ref, 1 - core)


def attention_kernel(
    x_ref, qkv_ref, resid_grad_ref, gain_one, w_qkv, w_proj,
    out_ref, rows_grad, normed_ref, gain_ref, grad_mixed, slots,
):
    grad_mixed[...] = dot(resid_grad_ref[...], w_proj[...]).astype(BF16)
    mask = head_mask((QUAD * ROWS, 128))
    scale = 32.0 ** -0.5

    @pl.loop(0, 1)
    def _(part):
        units = unit_places()
        count = range(len(units))
        query = [spread(qkv_ref[rows, pl.ds(lane, 128)], mask) for rows, lane in units]
        grad = [spread(grad_mixed[rows, pl.ds(lane, 128)], mask) for rows, lane in units]
        key = [qkv_ref[rows, pl.ds(384 + lane, 128)] for rows, lane in units]
        probs = [probabilities(key[n], query[n], scale) for n in count]
        grad_probs = [
            dot_nt(qkv_ref[rows, pl.ds(768 + lane, 128)], grad[n])
            for n, (rows, lane) in enumerate(units)
        ]
        grad_scores = []
        for n in count:
            centre = jnp.sum(grad_probs[n] * probs[n], axis=0, keepdims=True)
            grad_scores.append((probs[n] * (grad_probs[n] - centre) * scale).astype(BF16))
        for n, (rows, lane) in enumerate(units):
            rows_grad[rows, pl.ds(768 + lane, 128)] = dot(probs[n].astype(BF16), grad[n]).astype(BF16)
            rows_grad[rows, pl.ds(384 + lane, 128)] = dot(grad_scores[n], query[n]).astype(BF16)
            rows_grad[rows, pl.ds(lane, 128)] = gather_heads(
                dot_tn(grad_scores[n], key[n])
            ).astype(BF16)

    match = one_hot(group_match(iota((SLOTS, SLOTS), 0), iota((SLOTS, SLOTS), 1)))
    gain = jnp.zeros((1, 384), F32)
    for crop in range(4):
        rows = pl.ds(crop * SLOTS, SLOTS)
        grad = dot(rows_grad[rows, :], w_qkv[...]).astype(BF16).astype(F32)
        normal_hat, inv_std = norm_parts(x_ref[rows, :].astype(F32))
        normed_ref[rows, :] = (normal_hat * gain_one[...]).astype(BF16)
        gain = gain + jnp.sum(grad * normal_hat, axis=0, keepdims=True)
        grad_x = resid_grad_ref[rows, :].astype(F32) + norm_back(
            grad, normal_hat, inv_std, gain_one[...]
        )
        returned = dot(match, grad_x.astype(BF16))
        for part in range(3):
            slots[pl.ds(part * 4 + crop, SLOTS, stride=12), :] = returned[
                :, part * 128 : (part + 1) * 128
            ]
    for slot in range(SLOTS):
        for part in range(3):
            start = slot * 12 + part * 4
            out_ref[slot, part] = slots[start : start + 4, :].astype(BF16)
    gain_ref[...] = gain


def weight_kernel(
    rows_grad, normed, resid_grad, mixed, first, second, keep_ref, send_ref,
    qkv_total, proj_total, piece_rows,
):
    for part in range(3):
        cols = pl.ds(part * 384, 384)
        qkv_total[cols, :] = dot_tn(rows_grad[:, cols], normed[...])
    proj_total[...] = dot_tn(resid_grad[...], mixed[...])
    piece_rows[96:, :] = jnp.zeros((16, 384), F32)
    piece_rows[96:97, :] = first[...]
    piece_rows[97:98, :] = second[...]
    for ref, side in piece_sides(keep_ref, send_ref):
        for piece in range(8):
            owner = 2 * piece + side
            piece_rows[:72, :] = qkv_total[pl.ds(pl.multiple_of(owner * 72, 8), 72), :]
            piece_rows[72:96, :] = proj_total[pl.ds(pl.multiple_of(owner * 24, 8), 24), :]
            ref[piece] = piece_rows[...].astype(BF16)


def core_kernel(keep_ref, recv_ref, out_keep, out_send):
    row, col = lax.axis_index("y"), lax.axis_index("xl")
    for ref, side in ((out_keep, col), (out_send, 1 - col)):
        for step in range(4):
            piece = ((row + step) & 3) * 2 + side
            ref[step] = (keep_ref[piece].astype(F32) + recv_ref[piece].astype(F32)).astype(BF16)


def side_kernel(
    early_keep, early_recv, late_keep, late_recv, own, near, back, far_early, far_late,
):
    for step, ref in ((0, own), (1, near), (3, back)):
        early = early_keep[step].astype(F32) + early_recv[step].astype(F32)
        late = late_keep[step].astype(F32) + late_recv[step].astype(F32)
        ref[:192] = early.astype(BF16)
        ref[192:] = late.astype(BF16)
    far_early[...] = (early_keep[2].astype(F32) + early_recv[2].astype(F32)).astype(BF16)
    late = late_keep[2].astype(F32) + late_recv[2].astype(F32)
    far_late[:96] = late[:96].astype(BF16)
    far_late[96:] = pltpu.roll(late[96:], 2, 0).astype(BF16)


def ring_kernel(near, back, far_early, far_late, out_near, out_back):
    out_near[:192] = (near[:192].astype(F32) + far_early[...].astype(F32)).astype(BF16)
    out_near[192:] = near[192:]
    out_back[:192] = back[:192]
    out_back[192:] = (back[192:].astype(F32) + far_late[...].astype(F32)).astype(BF16)


def pack_columns(rows, col):
    low = pltpu.roll(rows[:48], (384 - 48 * col) % 384, 1)[:, :128]
    high = pltpu.roll(rows[48:96], (384 + 64 - 48 * col) % 384, 1)[:, :128]
    return jnp.where(iota((48, 128), 1) < 64, low, high)


def pack_kernel(own, near, back, out_ref, gains):
    row = lax.axis_index("y")
    first, second, third = (ref[288:].astype(F32) for ref in (own, near, back))
    gains[row] = first
    gains[(row + 3) & 3] = second
    gains[(row + 1) & 3] = third
    gains[(row + 2) & 3] = pltpu.roll(third, 14, 0)
    gain = (gains[0] + gains[1]) + (gains[2] + gains[3])
    total = own[:288].astype(F32) + near[:288].astype(F32) + back[:288].astype(F32)
    gain_rows = [
        gain[which : which + 1, part * 128 : (part + 1) * 128]
        for which in range(2)
        for part in range(3)
    ]
    gain_rows.append(jnp.zeros((2, 128), F32))
    for col in range(8):
        start = 96 + 24 * (col // 2)
        block = total[start : start + 24]
        if col % 2:
            block = pltpu.roll(block, 192, 1)
        out_ref[col] = jnp.concatenate(
            [pack_columns(total[:96], col), block[:, :128], block[:, 128:256]]
            + [pack_columns(total[192:288], col)] + gain_rows,
            axis=0,
        ).astype(BF16)


def block_sum(recv_ref, out_ref):
    total = recv_ref[0].astype(F32)
    for place in range(1, 8):
        total = total + recv_ref[place].astype(F32)
    out_ref[...] = total.astype(BF16)


def unpack_columns(packed):
    low = packed[:, :48]
    high = pltpu.roll(packed, 64, 1)[:, :48]
    wide = jnp.concatenate([low, high], axis=0)
    wide = jnp.concatenate([wide, jnp.zeros((96, 80), F32)], axis=1)
    wide = jnp.concatenate([wide, jnp.zeros((32, 128), F32)], axis=0)
    return wide.T[:48]


def final_weights(
    own_ref, other_ref,
    qkv_ref, proj_ref, up_ref, down_ref, first_ref, second_ref, factor,
):
    total = (own_ref[...].astype(F32) + other_ref[...].astype(F32)) * factor
    early, late = total[:96], total[96:]
    up_ref[...] = unpack_columns(early[:48])[:, :96]
    down_ref[:, :128] = early[48:72]
    down_ref[:, 128:] = early[72:96, :64]
    qkv_ref[...] = unpack_columns(late[:48])[:, :72]
    proj_ref[...] = pltpu.roll(late[:48], 64, 1)[24:48, :48]
    for part in range(3):
        lane = pl.ds(part * 128, 128)
        first_ref[lane] = late[48 + part]
        second_ref[lane] = late[51 + part]


def call(kernel, outs, scratch=(), flops=0, nbytes=0, space=pltpu.VMEM, limit=16):
    vmem = pl.BlockSpec(memory_space=pltpu.VMEM)
    scratch = [pltpu.VMEM(*item) if isinstance(item, tuple) else item for item in scratch]

    def run(*args):
        return pl.pallas_call(
            kernel,
            out_shape=[jax.ShapeDtypeStruct(shape, dtype) for shape, dtype in outs],
            in_specs=[pl.BlockSpec(memory_space=space)] * len(args),
            out_specs=[vmem] * len(outs),
            scratch_shapes=scratch,
            compiler_params=pltpu.CompilerParams(vmem_limit_bytes=limit << 20),
            cost_estimate=pl.CostEstimate(flops=flops, bytes_accessed=nbytes, transcendentals=0),
        )(*args)

    return run


def exchange(values, axes):
    return lax.all_to_all(values, axes, split_axis=0, concat_axis=0, tiled=True)


def swap(values, axis):
    return lax.ppermute(values, axis, [(0, 1), (1, 0)])


def side_pieces(keep, recv):
    half = ((4, keep.shape[1], 384), BF16)
    return call(core_kernel, [half, half], nbytes=4 * 10**6)(keep, recv)


def shift(values, step):
    return lax.ppermute(values, "y", [(place, (place + step) % 4) for place in range(4)])


def body(tokens, grad_out, gain_first, gain_second, w_qkv, w_proj, w_up, w_down):
    gain_one, gain_two = gain_first.reshape(1, 384), gain_second.reshape(1, 384)
    factor = (8 * 224 * 56) ** -0.5
    tile = pltpu.VMEM((LINES, GRID, 4, 384), BF16)
    (sent,) = call(
        send_kernel,
        [((SLOTS, 8, 384), BF16)],
        [tile, tile, pltpu.SemaphoreType.DMA((2,))],
        nbytes=2 * 10**6,
        space=pl.ANY,
        limit=60,
    )(
        tokens.transpose(1, 2, 0, 3), grad_out.transpose(1, 2, 0, 3)
    )
    arrived = exchange(sent, HA + ("wa",)).reshape(SLOTS * 8, 384)
    rows = ((512, 384), BF16)
    x, qkv, mixed, resid, grad_rows = call(
        forward_kernel,
        [rows, ((512, 1152), BF16), rows, rows, rows],
        [((3, 1024, 128), F32), rows],
        flops=10**9, nbytes=4 * 10**6,
    )(arrived, gain_one, w_qkv, w_proj)
    resid_grad, early_keep, early_send, gain_sum_two = call(
        mlp_kernel,
        [rows, ((8, 192, 384), BF16), ((8, 192, 384), BF16), ((1, 384), F32)],
        [
            rows, ((512, 1536), BF16), ((384, 512), BF16), ((1536, 384), F32), ((384, 1536), F32),
            ((512, 384), F32),
        ],
        flops=3 * 10**9, nbytes=6 * 10**6,
    )(grad_rows, resid, gain_two, w_up, w_down)
    slots, rows_grad, normed, gain_sum_one = call(
        attention_kernel,
        [((SLOTS, 3, 4, 128), BF16), ((512, 1152), BF16), rows, ((1, 384), F32)],
        [rows, ((SLOTS * 12, 128), F32)],
        flops=6 * 10**9, nbytes=20 * 10**6,
    )(x, qkv, resid_grad, gain_one, w_qkv, w_proj)
    returned = exchange(slots, HA + ("wa",))
    early = side_pieces(early_keep, swap(early_send, "core"))
    rows_grad, *early = lax.optimization_barrier((rows_grad, *early))
    late_keep, late_send = call(
        weight_kernel,
        [((8, 112, 384), BF16), ((8, 112, 384), BF16)],
        [((1152, 384), F32), ((384, 384), F32), ((112, 384), F32)],
        flops=10**9, nbytes=5 * 10**6,
    )(rows_grad, normed, resid_grad, mixed, gain_sum_one, gain_sum_two)
    late = side_pieces(late_keep, swap(late_send, "core"))
    piece = ((304, 384), BF16)
    own, near, back, far_early, far_late = call(
        side_kernel,
        [piece, piece, piece, ((192, 384), BF16), ((112, 384), BF16)],
        nbytes=5 * 10**6,
    )(early[0], swap(early[1], "xl"), late[0], swap(late[1], "xl"))
    near, back = call(ring_kernel, [piece, piece], nbytes=2 * 10**6)(
        near, back, shift(far_early, 1), shift(far_late, 3)
    )
    (blocks,) = call(
        pack_kernel, [((8, 152, 128), BF16)], [((4, 16, 384), F32)], nbytes=10**6
    )(own, shift(near, 1), shift(back, 3))
    blocks, returned = lax.optimization_barrier((blocks, returned))
    (total,) = call(block_sum, [((152, 128), BF16)], nbytes=10**6)(exchange(blocks, "wa"))
    other = swap(total, "dp")
    grad_qkv, grad_proj, grad_up, grad_down, first, second = call(
        functools.partial(final_weights, factor=factor),
        [
            ((48, 72), F32), ((24, 48), F32), ((48, 96), F32), ((24, 192), F32),
            ((384,), F32), ((384,), F32),
        ],
        nbytes=10**6,
    )(total, other)
    (grad_tile,) = call(return_kernel, [((LINES, GRID, 4, 384), BF16)], nbytes=10**6)(returned)
    return (
        grad_tile.transpose(2, 0, 1, 3), grad_qkv.T, grad_proj, grad_up.T, grad_down, first, second,
    )


def solution(mesh):
    fine = Mesh(mesh.devices.reshape(4, 2, 2, 8, 2), HA + ("wa", "dp"))
    tile = P("dp", HA, "wa", None)
    block = P(HA, "wa")
    return jax.shard_map(
        body,
        mesh=fine,
        in_specs=(tile, tile, P(), P(), P(), P(), P(), P()),
        out_specs=(tile, block, block, block, block, P(), P()),
        check_vma=False,
    )
```

```python
import functools

import jax
import jax.numpy as jnp
from jax import lax
from jax.experimental import pallas as pl
from jax.experimental.pallas import tpu as pltpu
from jax.sharding import Mesh, PartitionSpec as P

HEADS = 12
GRID = 7
EPSILON = 1e-05
SLOTS = 128
ROWS = 64
LINES = 14
QUAD = 4
F32 = jnp.float32
BF16 = jnp.bfloat16
HA = ("y", "xl", "core")


def dot(left, right):
    return jnp.dot(left, right, preferred_element_type=F32)


def dot_nt(left, right):
    return lax.dot_general(left, right, (((1,), (1,)), ((), ())), preferred_element_type=F32)


def dot_tn(left, right):
    return lax.dot_general(left, right, (((0,), (0,)), ((), ())), preferred_element_type=F32)


def iota(shape, dim):
    return lax.broadcasted_iota(jnp.int32, shape, dim)


def position():
    rows = (lax.axis_index("y") * 2 + lax.axis_index("xl")) * 2 + lax.axis_index("core")
    return rows, lax.axis_index("wa")


def group_match(slot, member):
    row, col = position()
    parity, local = member >> 6, member & 63
    band_row = (local * 37) >> 8
    band_col = local - GRID * band_row
    offset_row = row + 16 * parity + 32 * band_row - LINES * (slot >> 3)
    offset_col = col + 8 * band_col - GRID * (slot & 7)
    hit = jnp.logical_and(offset_row >= 0, offset_row < LINES)
    hit = jnp.logical_and(hit, jnp.logical_and(offset_col >= 0, offset_col < GRID))
    return jnp.logical_and(hit, local < GRID * GRID)


def owner_slot(line, column):
    row, col = position()
    return ((LINES * row + line) & 15) * 8 + ((GRID * col + column) & 7)


def one_hot(hit):
    return jnp.where(hit, 1.0, 0.0).astype(BF16)


def norm_parts(values):
    centered = values - jnp.mean(values, axis=-1, keepdims=True)
    inv_std = lax.rsqrt(jnp.mean(centered * centered, axis=-1, keepdims=True) + EPSILON)
    return centered * inv_std, inv_std


def norm_back(grad, normal_hat, inv_std, gain):
    grad_hat = grad * gain
    first = jnp.mean(grad_hat, axis=-1, keepdims=True)
    second = jnp.mean(grad_hat * normal_hat, axis=-1, keepdims=True)
    return inv_std * (grad_hat - first - normal_hat * second)


def head_mask(shape):
    return (iota(shape, 0) >> 6) == (iota(shape, 1) >> 5)


def spread(values, mask):
    tiled = jnp.concatenate([values] * QUAD, axis=0)
    return jnp.where(mask, tiled, jnp.zeros_like(tiled))


def gather_heads(values):
    lanes = iota((ROWS, 128), 1) >> 5
    total = jnp.where(lanes == 0, values[:ROWS], 0.0)
    for head in range(1, QUAD):
        total = total + jnp.where(lanes == head, values[head * ROWS : (head + 1) * ROWS], 0.0)
    return total


def probabilities(key, query_spread, scale):
    scores = dot_nt(key, query_spread) * scale
    expo = jnp.where(iota(scores.shape, 0) < GRID * GRID, jnp.exp(scores), 0.0)
    return expo * (1.0 / jnp.sum(expo, axis=0, keepdims=True))


def load_every(ref, start, step):
    parts = [ref[part, pl.ds(start, SLOTS, stride=step), :] for part in range(3)]
    return jnp.concatenate(parts, axis=1).astype(BF16)


def send_kernel(tokens_hbm, grad_hbm, out_ref, tokens_ref, grad_ref, sems):
    copies = [
        pltpu.make_async_copy(tokens_hbm, tokens_ref, sems.at[0]),
        pltpu.make_async_copy(grad_hbm, grad_ref, sems.at[1]),
    ]
    for copy in copies:
        copy.start()
    for copy in copies:
        copy.wait()
    for line in range(16):
        for column in range(8):
            slot = owner_slot(line, column)
            if line < LINES and column < GRID:
                unit = jnp.concatenate(
                    [tokens_ref[line, column].astype(F32), grad_ref[line, column].astype(F32)], axis=0
                ).astype(BF16)
            else:
                unit = jnp.zeros((8, 384), BF16)
            out_ref[slot] = unit


def return_kernel(recv_ref, out_ref):
    for line in range(LINES):
        for column in range(GRID):
            slot = owner_slot(line, column)
            for part in range(3):
                out_ref[line, column, :, part * 128 : (part + 1) * 128] = recv_ref[slot, part]


def gelu_parts(hidden, grad):
    inner, cubic = 0.7978845608028654, 0.7978845608028654 * 0.044715
    square = hidden * hidden
    part = 0.5 * jnp.tanh(hidden * (inner + cubic * square)) + 0.5
    twice = hidden * (2 * inner + 6 * cubic * square)
    slope = part * (1.0 + (1.0 - part) * twice)
    return hidden * part, grad * slope


def forward_kernel(
    recv_ref, gain_one, w_qkv, w_proj,
    x_ref, qkv_ref, mixed_ref, resid_ref, grad_ref, arrived, normed,
):
    for part in range(3):
        arrived[part] = recv_ref[:, part * 128 : (part + 1) * 128].astype(F32)
    match = one_hot(group_match(iota((SLOTS, SLOTS), 1), iota((SLOTS, SLOTS), 0)))
    for crop in range(4):
        rows = pl.ds(crop * SLOTS, SLOTS)
        x = dot(match, load_every(arrived, crop, 8))
        x_ref[rows, :] = x.astype(BF16)
        normal_hat, _ = norm_parts(x)
        normed[rows, :] = (normal_hat * gain_one[...]).astype(BF16)
        grad_ref[rows, :] = dot(match, load_every(arrived, crop + 4, 8)).astype(BF16)
    for part in range(3):
        cols = pl.ds(part * 384, 384)
        qkv_ref[:, cols] = dot_nt(normed[...], w_qkv[cols, :]).astype(BF16)
    mask = head_mask((QUAD * ROWS, 128))
    scale = 32.0 ** -0.5

    @pl.loop(0, 1)
    def _(part):
        units = unit_places()
        query = [spread(qkv_ref[rows, pl.ds(lane, 128)], mask) for rows, lane in units]
        probs = [
            probabilities(qkv_ref[rows, pl.ds(384 + lane, 128)], query[n], scale).astype(BF16)
            for n, (rows, lane) in enumerate(units)
        ]
        mixed = [
            dot_tn(probs[n], qkv_ref[rows, pl.ds(768 + lane, 128)])
            for n, (rows, lane) in enumerate(units)
        ]
        for n, (rows, lane) in enumerate(units):
            mixed_ref[rows, pl.ds(lane, 128)] = gather_heads(mixed[n]).astype(BF16)

    for crop in range(4):
        rows = pl.ds(crop * SLOTS, SLOTS)
        branch = dot_nt(mixed_ref[rows, :], w_proj[...]).astype(BF16)
        resid_ref[rows, :] = (x_ref[rows, :].astype(F32) + branch.astype(F32)).astype(BF16)


def unit_places():
    return [(pl.ds(group * ROWS, ROWS), quad * 128) for group in range(8) for quad in range(3)]


def mlp_kernel(
    grad_out, resid, gain_two, w_up, w_down,
    resid_grad_ref, keep_ref, send_ref, gain_ref,
    normed, hidden_grad, grad_turned, up_total, down_total, back,
):
    for crop in range(4):
        rows = pl.ds(crop * SLOTS, SLOTS)
        normal_hat, _ = norm_parts(resid[rows, :].astype(F32))
        normed[rows, :] = (normal_hat * gain_two[...]).astype(BF16)
        grad_turned[:, rows] = grad_out[rows, :].astype(F32).T.astype(BF16)
    for chunk in range(4):
        cols = pl.ds(chunk * 384, 384)
        hidden = dot_nt(normed[...], w_up[cols, :])
        grad_act = dot(grad_out[...], w_down[:, cols])
        activated, grad_hidden = gelu_parts(hidden, grad_act)
        hidden_grad[:, cols] = grad_hidden.astype(BF16)
        down_total[:, cols] = dot(grad_turned[...], activated.astype(BF16))
        up_total[cols, :] = dot_tn(hidden_grad[:, cols], normed[...])
    back[...] = dot(hidden_grad[...], w_up[...])

    for ref, side in piece_sides(keep_ref, send_ref):
        for piece in range(8):
            owner = 2 * piece + side
            ref[piece, :96] = up_total[pl.ds(pl.multiple_of(owner * 96, 8), 96), :].astype(BF16)
            rows = pl.ds(pl.multiple_of(owner * 24, 8), 24)
            ref[piece, 96:] = jnp.concatenate(
                [down_total[rows, part * 384 : (part + 1) * 384] for part in range(4)], axis=0
            ).astype(BF16)
    gain = jnp.zeros((1, 384), F32)
    for crop in range(4):
        rows = pl.ds(crop * SLOTS, SLOTS)
        normal_hat, inv_std = norm_parts(resid[rows, :].astype(F32))
        grad = back[rows, :]
        gain = gain + jnp.sum(grad * normal_hat, axis=0, keepdims=True)
        resid_grad_ref[rows, :] = (
            grad_out[rows, :].astype(F32) + norm_back(grad, normal_hat, inv_std, gain_two[...])
        ).astype(BF16)
    gain_ref[...] = gain


def piece_sides(keep_ref, send_ref):
    core = lax.axis_index("core")
    return (keep_ref, core), (send_ref, 1 - core)


def attention_kernel(
    x_ref, qkv_ref, resid_grad_ref, gain_one, w_qkv, w_proj,
    out_ref, rows_grad, normed_ref, gain_ref, grad_mixed, slots,
):
    grad_mixed[...] = dot(resid_grad_ref[...], w_proj[...]).astype(BF16)
    mask = head_mask((QUAD * ROWS, 128))
    scale = 32.0 ** -0.5

    @pl.loop(0, 1)
    def _(part):
        units = unit_places()
        count = range(len(units))
        query = [spread(qkv_ref[rows, pl.ds(lane, 128)], mask) for rows, lane in units]
        grad = [spread(grad_mixed[rows, pl.ds(lane, 128)], mask) for rows, lane in units]
        key = [qkv_ref[rows, pl.ds(384 + lane, 128)] for rows, lane in units]
        probs = [probabilities(key[n], query[n], scale) for n in count]
        grad_probs = [
            dot_nt(qkv_ref[rows, pl.ds(768 + lane, 128)], grad[n])
            for n, (rows, lane) in enumerate(units)
        ]
        grad_scores = []
        for n in count:
            centre = jnp.sum(grad_probs[n] * probs[n], axis=0, keepdims=True)
            grad_scores.append((probs[n] * (grad_probs[n] - centre) * scale).astype(BF16))
        for n, (rows, lane) in enumerate(units):
            rows_grad[rows, pl.ds(768 + lane, 128)] = dot(probs[n].astype(BF16), grad[n]).astype(BF16)
            rows_grad[rows, pl.ds(384 + lane, 128)] = dot(grad_scores[n], query[n]).astype(BF16)
            rows_grad[rows, pl.ds(lane, 128)] = gather_heads(
                dot_tn(grad_scores[n], key[n])
            ).astype(BF16)

    match = one_hot(group_match(iota((SLOTS, SLOTS), 0), iota((SLOTS, SLOTS), 1)))
    gain = jnp.zeros((1, 384), F32)
    for crop in range(4):
        rows = pl.ds(crop * SLOTS, SLOTS)
        grad = dot(rows_grad[rows, :], w_qkv[...]).astype(BF16).astype(F32)
        normal_hat, inv_std = norm_parts(x_ref[rows, :].astype(F32))
        normed_ref[rows, :] = (normal_hat * gain_one[...]).astype(BF16)
        gain = gain + jnp.sum(grad * normal_hat, axis=0, keepdims=True)
        grad_x = resid_grad_ref[rows, :].astype(F32) + norm_back(
            grad, normal_hat, inv_std, gain_one[...]
        )
        returned = dot(match, grad_x.astype(BF16))
        for part in range(3):
            slots[pl.ds(part * 4 + crop, SLOTS, stride=12), :] = returned[
                :, part * 128 : (part + 1) * 128
            ]
    for slot in range(SLOTS):
        for part in range(3):
            start = slot * 12 + part * 4
            out_ref[slot, part] = slots[start : start + 4, :].astype(BF16)
    gain_ref[...] = gain


def weight_kernel(
    rows_grad, normed, resid_grad, mixed, first, second, keep_ref, send_ref,
    qkv_total, proj_total, piece_rows,
):
    for part in range(3):
        cols = pl.ds(part * 384, 384)
        qkv_total[cols, :] = dot_tn(rows_grad[:, cols], normed[...])
    proj_total[...] = dot_tn(resid_grad[...], mixed[...])
    piece_rows[96:, :] = jnp.zeros((16, 384), F32)
    piece_rows[96:97, :] = first[...]
    piece_rows[97:98, :] = second[...]
    for ref, side in piece_sides(keep_ref, send_ref):
        for piece in range(8):
            owner = 2 * piece + side
            piece_rows[:72, :] = qkv_total[pl.ds(pl.multiple_of(owner * 72, 8), 72), :]
            piece_rows[72:96, :] = proj_total[pl.ds(pl.multiple_of(owner * 24, 8), 24), :]
            ref[piece] = piece_rows[...].astype(BF16)


def core_total(keep_ref, recv_ref, step, side):
    piece = ((lax.axis_index("y") + step) & 3) * 2 + side
    return (keep_ref[piece].astype(F32) + recv_ref[piece].astype(F32)).astype(BF16)


def early_kernel(keep_ref, recv_ref, out_keep, out_up, out_down):
    col = lax.axis_index("xl")
    for step in range(4):
        out_keep[step] = core_total(keep_ref, recv_ref, step, col)
        other = core_total(keep_ref, recv_ref, step, 1 - col)
        out_up[step] = other[:96]
        out_down[step] = other[96:]


def late_kernel(keep_ref, recv_ref, up_ref, out_keep, out_send):
    col = lax.axis_index("xl")
    for step in range(4):
        out_keep[step] = core_total(keep_ref, recv_ref, step, col)
        out_send[step, :96] = up_ref[step]
        out_send[step, 96:] = core_total(keep_ref, recv_ref, step, 1 - col)


def side_kernel(
    early_keep, down_recv, late_keep, late_recv, own, near, back, far_early, far_late,
):
    def total(step):
        up = early_keep[step, :96].astype(F32) + late_recv[step, :96].astype(F32)
        down = early_keep[step, 96:].astype(F32) + down_recv[step].astype(F32)
        return up, down, late_keep[step].astype(F32) + late_recv[step, 96:].astype(F32)

    for step, ref in ((0, own), (1, near), (3, back)):
        up, down, late = total(step)
        ref[:96] = up.astype(BF16)
        ref[96:192] = down.astype(BF16)
        ref[192:] = late.astype(BF16)
    up, down, late = total(2)
    far_early[:96] = up.astype(BF16)
    far_early[96:] = down.astype(BF16)
    far_late[:96] = late[:96].astype(BF16)
    far_late[96:] = pltpu.roll(late[96:], 2, 0).astype(BF16)


def ring_kernel(near, back, far_early, far_late, out_near, out_back):
    out_near[:192] = (near[:192].astype(F32) + far_early[...].astype(F32)).astype(BF16)
    out_near[192:] = near[192:]
    out_back[:192] = back[:192]
    out_back[192:] = (back[192:].astype(F32) + far_late[...].astype(F32)).astype(BF16)


def pack_columns(rows, col):
    low = pltpu.roll(rows[:48], (384 - 48 * col) % 384, 1)[:, :128]
    high = pltpu.roll(rows[48:96], (384 + 64 - 48 * col) % 384, 1)[:, :128]
    return jnp.where(iota((48, 128), 1) < 64, low, high)


def pack_kernel(own, near, back, out_ref, gains):
    row = lax.axis_index("y")
    first, second, third = (ref[288:].astype(F32) for ref in (own, near, back))
    gains[row] = first
    gains[(row + 3) & 3] = second
    gains[(row + 1) & 3] = third
    gains[(row + 2) & 3] = pltpu.roll(third, 14, 0)
    gain = (gains[0] + gains[1]) + (gains[2] + gains[3])
    total = own[:288].astype(F32) + near[:288].astype(F32) + back[:288].astype(F32)
    gain_rows = [
        gain[which : which + 1, part * 128 : (part + 1) * 128]
        for which in range(2)
        for part in range(3)
    ]
    gain_rows.append(jnp.zeros((2, 128), F32))
    for col in range(8):
        start = 96 + 24 * (col // 2)
        block = total[start : start + 24]
        if col % 2:
            block = pltpu.roll(block, 192, 1)
        out_ref[col] = jnp.concatenate(
            [pack_columns(total[:96], col), block[:, :128], block[:, 128:256]]
            + [pack_columns(total[192:288], col)] + gain_rows,
            axis=0,
        ).astype(BF16)


def block_sum(recv_ref, out_ref):
    total = recv_ref[0].astype(F32)
    for place in range(1, 8):
        total = total + recv_ref[place].astype(F32)
    out_ref[...] = total.astype(BF16)


def unpack_columns(packed):
    low = packed[:, :48]
    high = pltpu.roll(packed, 64, 1)[:, :48]
    wide = jnp.concatenate([low, high], axis=0)
    wide = jnp.concatenate([wide, jnp.zeros((96, 80), F32)], axis=1)
    wide = jnp.concatenate([wide, jnp.zeros((32, 128), F32)], axis=0)
    return wide.T[:48]


def final_weights(
    own_ref, other_ref,
    qkv_ref, proj_ref, up_ref, down_ref, first_ref, second_ref, factor,
):
    total = (own_ref[...].astype(F32) + other_ref[...].astype(F32)) * factor
    early, late = total[:96], total[96:]
    up_ref[...] = unpack_columns(early[:48])[:, :96]
    down_ref[:, :128] = early[48:72]
    down_ref[:, 128:] = early[72:96, :64]
    qkv_ref[...] = unpack_columns(late[:48])[:, :72]
    proj_ref[...] = pltpu.roll(late[:48], 64, 1)[24:48, :48]
    for part in range(3):
        lane = pl.ds(part * 128, 128)
        first_ref[lane] = late[48 + part]
        second_ref[lane] = late[51 + part]


def call(kernel, outs, scratch=(), flops=0, nbytes=0, space=pltpu.VMEM, limit=16):
    vmem = pl.BlockSpec(memory_space=pltpu.VMEM)
    scratch = [pltpu.VMEM(*item) if isinstance(item, tuple) else item for item in scratch]

    def run(*args):
        return pl.pallas_call(
            kernel,
            out_shape=[jax.ShapeDtypeStruct(shape, dtype) for shape, dtype in outs],
            in_specs=[pl.BlockSpec(memory_space=space)] * len(args),
            out_specs=[vmem] * len(outs),
            scratch_shapes=scratch,
            compiler_params=pltpu.CompilerParams(vmem_limit_bytes=limit << 20),
            cost_estimate=pl.CostEstimate(flops=flops, bytes_accessed=nbytes, transcendentals=0),
        )(*args)

    return run


def exchange(values, axes):
    return lax.all_to_all(values, axes, split_axis=0, concat_axis=0, tiled=True)


def swap(values, axis):
    return lax.ppermute(values, axis, [(0, 1), (1, 0)])


def shift(values, step):
    return lax.ppermute(values, "y", [(place, (place + step) % 4) for place in range(4)])


def body(tokens, grad_out, gain_first, gain_second, w_qkv, w_proj, w_up, w_down):
    gain_one, gain_two = gain_first.reshape(1, 384), gain_second.reshape(1, 384)
    factor = (8 * 224 * 56) ** -0.5
    tile = pltpu.VMEM((LINES, GRID, 4, 384), BF16)
    (sent,) = call(
        send_kernel,
        [((SLOTS, 8, 384), BF16)],
        [tile, tile, pltpu.SemaphoreType.DMA((2,))],
        nbytes=2 * 10**6,
        space=pl.ANY,
        limit=60,
    )(
        tokens.transpose(1, 2, 0, 3), grad_out.transpose(1, 2, 0, 3)
    )
    arrived = exchange(sent, HA + ("wa",)).reshape(SLOTS * 8, 384)
    rows = ((512, 384), BF16)
    x, qkv, mixed, resid, grad_rows = call(
        forward_kernel,
        [rows, ((512, 1152), BF16), rows, rows, rows],
        [((3, 1024, 128), F32), rows],
        flops=10**9, nbytes=4 * 10**6,
    )(arrived, gain_one, w_qkv, w_proj)
    resid_grad, early_keep, early_send, gain_sum_two = call(
        mlp_kernel,
        [rows, ((8, 192, 384), BF16), ((8, 192, 384), BF16), ((1, 384), F32)],
        [
            rows, ((512, 1536), BF16), ((384, 512), BF16), ((1536, 384), F32), ((384, 1536), F32),
            ((512, 384), F32),
        ],
        flops=3 * 10**9, nbytes=6 * 10**6,
    )(grad_rows, resid, gain_two, w_up, w_down)
    slots, rows_grad, normed, gain_sum_one = call(
        attention_kernel,
        [((SLOTS, 3, 4, 128), BF16), ((512, 1152), BF16), rows, ((1, 384), F32)],
        [rows, ((SLOTS * 12, 128), F32)],
        flops=6 * 10**9, nbytes=20 * 10**6,
    )(x, qkv, resid_grad, gain_one, w_qkv, w_proj)
    returned = exchange(slots, HA + ("wa",))
    part = ((4, 96, 384), BF16)
    early = call(early_kernel, [((4, 192, 384), BF16), part, part], nbytes=4 * 10**6)(
        early_keep, swap(early_send, "core")
    )
    rows_grad, early_keep, up_send, down_send = lax.optimization_barrier((rows_grad, *early))
    late_keep, late_send = call(
        weight_kernel,
        [((8, 112, 384), BF16), ((8, 112, 384), BF16)],
        [((1152, 384), F32), ((384, 384), F32), ((112, 384), F32)],
        flops=10**9, nbytes=5 * 10**6,
    )(rows_grad, normed, resid_grad, mixed, gain_sum_one, gain_sum_two)
    late_keep, late_send = call(
        late_kernel, [((4, 112, 384), BF16), ((4, 208, 384), BF16)], nbytes=4 * 10**6
    )(late_keep, swap(late_send, "core"), up_send)
    piece = ((304, 384), BF16)
    own, near, back, far_early, far_late = call(
        side_kernel,
        [piece, piece, piece, ((192, 384), BF16), ((112, 384), BF16)],
        nbytes=5 * 10**6,
    )(early_keep, swap(down_send, "xl"), late_keep, swap(late_send, "xl"))
    near, back = call(ring_kernel, [piece, piece], nbytes=2 * 10**6)(
        near, back, shift(far_early, 1), shift(far_late, 3)
    )
    (blocks,) = call(
        pack_kernel, [((8, 152, 128), BF16)], [((4, 16, 384), F32)], nbytes=10**6
    )(own, shift(near, 1), shift(back, 3))
    blocks, returned = lax.optimization_barrier((blocks, returned))
    (total,) = call(block_sum, [((152, 128), BF16)], nbytes=10**6)(exchange(blocks, "wa"))
    other = swap(total, "dp")
    grad_qkv, grad_proj, grad_up, grad_down, first, second = call(
        functools.partial(final_weights, factor=factor),
        [
            ((48, 72), F32), ((24, 48), F32), ((48, 96), F32), ((24, 192), F32),
            ((384,), F32), ((384,), F32),
        ],
        nbytes=10**6,
    )(total, other)
    (grad_tile,) = call(return_kernel, [((LINES, GRID, 4, 384), BF16)], nbytes=10**6)(returned)
    return (
        grad_tile.transpose(2, 0, 1, 3), grad_qkv.T, grad_proj, grad_up.T, grad_down, first, second,
    )


def solution(mesh):
    fine = Mesh(mesh.devices.reshape(4, 2, 2, 8, 2), HA + ("wa", "dp"))
    tile = P("dp", HA, "wa", None)
    block = P(HA, "wa")
    return jax.shard_map(
        body,
        mesh=fine,
        in_specs=(tile, tile, P(), P(), P(), P(), P(), P()),
        out_specs=(tile, block, block, block, block, P(), P()),
        check_vma=False,
    )
```

```python
import functools

import jax
import jax.numpy as jnp
from jax import lax
from jax.experimental import pallas as pl
from jax.experimental.pallas import tpu as pltpu
from jax.sharding import Mesh, PartitionSpec as P

HEADS = 12
GRID = 7
EPSILON = 1e-05
SLOTS = 128
ROWS = 64
LINES = 14
QUAD = 4
F32 = jnp.float32
BF16 = jnp.bfloat16
HA = ("y", "xl", "core")


def dot(left, right):
    return jnp.dot(left, right, preferred_element_type=F32)


def dot_nt(left, right):
    return lax.dot_general(left, right, (((1,), (1,)), ((), ())), preferred_element_type=F32)


def dot_tn(left, right):
    return lax.dot_general(left, right, (((0,), (0,)), ((), ())), preferred_element_type=F32)


def iota(shape, dim):
    return lax.broadcasted_iota(jnp.int32, shape, dim)


def position():
    rows = (lax.axis_index("y") * 2 + lax.axis_index("xl")) * 2 + lax.axis_index("core")
    return rows, lax.axis_index("wa")


def group_match(slot, member):
    row, col = position()
    parity, local = member >> 6, member & 63
    band_row = (local * 37) >> 8
    band_col = local - GRID * band_row
    offset_row = row + 16 * parity + 32 * band_row - LINES * (slot >> 3)
    offset_col = col + 8 * band_col - GRID * (slot & 7)
    hit = jnp.logical_and(offset_row >= 0, offset_row < LINES)
    hit = jnp.logical_and(hit, jnp.logical_and(offset_col >= 0, offset_col < GRID))
    return jnp.logical_and(hit, local < GRID * GRID)


def owner_slot(line, column):
    row, col = position()
    return ((LINES * row + line) & 15) * 8 + ((GRID * col + column) & 7)


def one_hot(hit):
    return jnp.where(hit, 1.0, 0.0).astype(BF16)


def norm_parts(values):
    centered = values - jnp.mean(values, axis=-1, keepdims=True)
    inv_std = lax.rsqrt(jnp.mean(centered * centered, axis=-1, keepdims=True) + EPSILON)
    return centered * inv_std, inv_std


def norm_back(grad, normal_hat, inv_std, gain):
    grad_hat = grad * gain
    first = jnp.mean(grad_hat, axis=-1, keepdims=True)
    second = jnp.mean(grad_hat * normal_hat, axis=-1, keepdims=True)
    return inv_std * (grad_hat - first - normal_hat * second)


def head_mask(shape):
    return (iota(shape, 0) >> 6) == (iota(shape, 1) >> 5)


def spread(values, mask):
    tiled = jnp.concatenate([values] * QUAD, axis=0)
    return jnp.where(mask, tiled, jnp.zeros_like(tiled))


def gather_heads(values):
    lanes = iota((ROWS, 128), 1) >> 5
    total = jnp.where(lanes == 0, values[:ROWS], 0.0)
    for head in range(1, QUAD):
        total = total + jnp.where(lanes == head, values[head * ROWS : (head + 1) * ROWS], 0.0)
    return total


def probabilities(key, query_spread, scale):
    scores = dot_nt(key, query_spread) * scale
    expo = jnp.where(iota(scores.shape, 0) < GRID * GRID, jnp.exp(scores), 0.0)
    return expo * (1.0 / jnp.sum(expo, axis=0, keepdims=True))


def load_every(ref, start, step):
    parts = [ref[part, pl.ds(start, SLOTS, stride=step), :] for part in range(3)]
    return jnp.concatenate(parts, axis=1).astype(BF16)


def send_kernel(tokens_hbm, grad_hbm, out_ref, tokens_ref, grad_ref, sems):
    copies = [
        pltpu.make_async_copy(tokens_hbm, tokens_ref, sems.at[0]),
        pltpu.make_async_copy(grad_hbm, grad_ref, sems.at[1]),
    ]
    for copy in copies:
        copy.start()
    for copy in copies:
        copy.wait()
    for line in range(16):
        for column in range(8):
            slot = owner_slot(line, column)
            if line < LINES and column < GRID:
                unit = jnp.concatenate(
                    [tokens_ref[line, column].astype(F32), grad_ref[line, column].astype(F32)], axis=0
                ).astype(BF16)
            else:
                unit = jnp.zeros((8, 384), BF16)
            out_ref[slot] = unit


def return_kernel(recv_ref, out_ref):
    for line in range(LINES):
        for column in range(GRID):
            slot = owner_slot(line, column)
            for part in range(3):
                out_ref[line, column, :, part * 128 : (part + 1) * 128] = recv_ref[slot, part]


def gelu_parts(hidden, grad):
    inner, cubic = 0.7978845608028654, 0.7978845608028654 * 0.044715
    square = hidden * hidden
    part = 0.5 * jnp.tanh(hidden * (inner + cubic * square)) + 0.5
    twice = hidden * (2 * inner + 6 * cubic * square)
    slope = part * (1.0 + (1.0 - part) * twice)
    return hidden * part, grad * slope


def forward_kernel(
    recv_ref, gain_one, w_qkv, w_proj,
    x_ref, qkv_ref, mixed_ref, resid_ref, grad_ref, arrived, normed,
):
    for part in range(3):
        arrived[part] = recv_ref[:, part * 128 : (part + 1) * 128].astype(F32)
    match = one_hot(group_match(iota((SLOTS, SLOTS), 1), iota((SLOTS, SLOTS), 0)))
    for crop in range(4):
        rows = pl.ds(crop * SLOTS, SLOTS)
        x = dot(match, load_every(arrived, crop, 8))
        x_ref[rows, :] = x.astype(BF16)
        normal_hat, _ = norm_parts(x)
        normed[rows, :] = (normal_hat * gain_one[...]).astype(BF16)
        grad_ref[rows, :] = dot(match, load_every(arrived, crop + 4, 8)).astype(BF16)
    for part in range(3):
        cols = pl.ds(part * 384, 384)
        qkv_ref[:, cols] = dot_nt(normed[...], w_qkv[cols, :]).astype(BF16)
    mask = head_mask((QUAD * ROWS, 128))
    scale = 32.0 ** -0.5

    @pl.loop(0, 1)
    def _(part):
        units = unit_places()
        query = [spread(qkv_ref[rows, pl.ds(lane, 128)], mask) for rows, lane in units]
        probs = [
            probabilities(qkv_ref[rows, pl.ds(384 + lane, 128)], query[n], scale).astype(BF16)
            for n, (rows, lane) in enumerate(units)
        ]
        mixed = [
            dot_tn(probs[n], qkv_ref[rows, pl.ds(768 + lane, 128)])
            for n, (rows, lane) in enumerate(units)
        ]
        for n, (rows, lane) in enumerate(units):
            mixed_ref[rows, pl.ds(lane, 128)] = gather_heads(mixed[n]).astype(BF16)

    for crop in range(4):
        rows = pl.ds(crop * SLOTS, SLOTS)
        branch = dot_nt(mixed_ref[rows, :], w_proj[...]).astype(BF16)
        resid_ref[rows, :] = (x_ref[rows, :].astype(F32) + branch.astype(F32)).astype(BF16)


def unit_places():
    return [(pl.ds(group * ROWS, ROWS), quad * 128) for group in range(8) for quad in range(3)]


def mlp_kernel(
    grad_out, resid, gain_two, w_up, w_down,
    resid_grad_ref, keep_ref, send_ref, gain_ref,
    normed, hidden_grad, grad_turned, up_total, down_total, back,
):
    for crop in range(4):
        rows = pl.ds(crop * SLOTS, SLOTS)
        normal_hat, _ = norm_parts(resid[rows, :].astype(F32))
        normed[rows, :] = (normal_hat * gain_two[...]).astype(BF16)
        grad_turned[:, rows] = grad_out[rows, :].astype(F32).T.astype(BF16)
    for chunk in range(4):
        cols = pl.ds(chunk * 384, 384)
        hidden = dot_nt(normed[...], w_up[cols, :])
        grad_act = dot(grad_out[...], w_down[:, cols])
        activated, grad_hidden = gelu_parts(hidden, grad_act)
        hidden_grad[:, cols] = grad_hidden.astype(BF16)
        down_total[:, cols] = dot(grad_turned[...], activated.astype(BF16))
        up_total[cols, :] = dot_tn(hidden_grad[:, cols], normed[...])
    back[...] = dot(hidden_grad[...], w_up[...])

    for ref, side in piece_sides(keep_ref, send_ref):
        for piece in range(8):
            owner = 2 * piece + side
            ref[piece, :96] = up_total[pl.ds(pl.multiple_of(owner * 96, 8), 96), :].astype(BF16)
            rows = pl.ds(pl.multiple_of(owner * 24, 8), 24)
            ref[piece, 96:] = jnp.concatenate(
                [down_total[rows, part * 384 : (part + 1) * 384] for part in range(4)], axis=0
            ).astype(BF16)
    gain = jnp.zeros((1, 384), F32)
    for crop in range(4):
        rows = pl.ds(crop * SLOTS, SLOTS)
        normal_hat, inv_std = norm_parts(resid[rows, :].astype(F32))
        grad = back[rows, :]
        gain = gain + jnp.sum(grad * normal_hat, axis=0, keepdims=True)
        resid_grad_ref[rows, :] = (
            grad_out[rows, :].astype(F32) + norm_back(grad, normal_hat, inv_std, gain_two[...])
        ).astype(BF16)
    gain_ref[...] = gain


def piece_sides(keep_ref, send_ref):
    core = lax.axis_index("core")
    return (keep_ref, core), (send_ref, 1 - core)


def attention_kernel(
    x_ref, qkv_ref, resid_grad_ref, gain_one, w_qkv, w_proj,
    out_ref, rows_grad, normed_ref, gain_ref, grad_mixed, slots,
):
    grad_mixed[...] = dot(resid_grad_ref[...], w_proj[...]).astype(BF16)
    mask = head_mask((QUAD * ROWS, 128))
    scale = 32.0 ** -0.5

    @pl.loop(0, 1)
    def _(part):
        units = unit_places()
        count = range(len(units))
        query = [spread(qkv_ref[rows, pl.ds(lane, 128)], mask) for rows, lane in units]
        grad = [spread(grad_mixed[rows, pl.ds(lane, 128)], mask) for rows, lane in units]
        key = [qkv_ref[rows, pl.ds(384 + lane, 128)] for rows, lane in units]
        probs = [probabilities(key[n], query[n], scale) for n in count]
        grad_probs = [
            dot_nt(qkv_ref[rows, pl.ds(768 + lane, 128)], grad[n])
            for n, (rows, lane) in enumerate(units)
        ]
        grad_scores = []
        for n in count:
            centre = jnp.sum(grad_probs[n] * probs[n], axis=0, keepdims=True)
            grad_scores.append((probs[n] * (grad_probs[n] - centre) * scale).astype(BF16))
        for n, (rows, lane) in enumerate(units):
            rows_grad[rows, pl.ds(768 + lane, 128)] = dot(probs[n].astype(BF16), grad[n]).astype(BF16)
            rows_grad[rows, pl.ds(384 + lane, 128)] = dot(grad_scores[n], query[n]).astype(BF16)
            rows_grad[rows, pl.ds(lane, 128)] = gather_heads(
                dot_tn(grad_scores[n], key[n])
            ).astype(BF16)

    match = one_hot(group_match(iota((SLOTS, SLOTS), 0), iota((SLOTS, SLOTS), 1)))
    gain = jnp.zeros((1, 384), F32)
    for crop in range(4):
        rows = pl.ds(crop * SLOTS, SLOTS)
        grad = dot(rows_grad[rows, :], w_qkv[...]).astype(BF16).astype(F32)
        normal_hat, inv_std = norm_parts(x_ref[rows, :].astype(F32))
        normed_ref[rows, :] = (normal_hat * gain_one[...]).astype(BF16)
        gain = gain + jnp.sum(grad * normal_hat, axis=0, keepdims=True)
        grad_x = resid_grad_ref[rows, :].astype(F32) + norm_back(
            grad, normal_hat, inv_std, gain_one[...]
        )
        returned = dot(match, grad_x.astype(BF16))
        for part in range(3):
            slots[pl.ds(part * 4 + crop, SLOTS, stride=12), :] = returned[
                :, part * 128 : (part + 1) * 128
            ]
    for slot in range(SLOTS):
        for part in range(3):
            start = slot * 12 + part * 4
            out_ref[slot, part] = slots[start : start + 4, :].astype(BF16)
    gain_ref[...] = gain


def weight_kernel(
    rows_grad, normed, resid_grad, mixed, first, second, keep_ref, send_ref,
    qkv_total, proj_total, piece_rows,
):
    for part in range(3):
        cols = pl.ds(part * 384, 384)
        qkv_total[cols, :] = dot_tn(rows_grad[:, cols], normed[...])
    proj_total[...] = dot_tn(resid_grad[...], mixed[...])
    piece_rows[96:, :] = jnp.zeros((16, 384), F32)
    piece_rows[96:97, :] = first[...]
    piece_rows[97:98, :] = second[...]
    for ref, side in piece_sides(keep_ref, send_ref):
        for piece in range(8):
            owner = 2 * piece + side
            piece_rows[:72, :] = qkv_total[pl.ds(pl.multiple_of(owner * 72, 8), 72), :]
            piece_rows[72:96, :] = proj_total[pl.ds(pl.multiple_of(owner * 24, 8), 24), :]
            ref[piece] = piece_rows[...].astype(BF16)


def core_kernel(early_keep, early_recv, late_keep, late_recv, out_keep, out_send):
    row, col = lax.axis_index("y"), lax.axis_index("xl")
    for ref, side in ((out_keep, col), (out_send, 1 - col)):
        for step in range(4):
            piece = ((row + step) & 3) * 2 + side
            early = early_keep[piece].astype(F32) + early_recv[piece].astype(F32)
            late = late_keep[piece].astype(F32) + late_recv[piece].astype(F32)
            ref[step, :192] = early.astype(BF16)
            ref[step, 192:] = late.astype(BF16)


def side_kernel(keep_ref, recv_ref, own, near, back, far_early, far_late):
    for step, ref in ((0, own), (1, near), (3, back)):
        ref[...] = (keep_ref[step].astype(F32) + recv_ref[step].astype(F32)).astype(BF16)
    total = keep_ref[2].astype(F32) + recv_ref[2].astype(F32)
    far_early[...] = total[:192].astype(BF16)
    far_late[:96] = total[192:288].astype(BF16)
    far_late[96:] = pltpu.roll(total[288:], 2, 0).astype(BF16)


def ring_kernel(near, back, far_early, far_late, out_near, out_back):
    out_near[:192] = (near[:192].astype(F32) + far_early[...].astype(F32)).astype(BF16)
    out_near[192:] = near[192:]
    out_back[:192] = back[:192]
    out_back[192:] = (back[192:].astype(F32) + far_late[...].astype(F32)).astype(BF16)


def pack_columns(rows, col):
    low = pltpu.roll(rows[:48], (384 - 48 * col) % 384, 1)[:, :128]
    high = pltpu.roll(rows[48:96], (384 + 64 - 48 * col) % 384, 1)[:, :128]
    return jnp.where(iota((48, 128), 1) < 64, low, high)


def pack_kernel(own, near, back, out_ref, gains):
    row = lax.axis_index("y")
    first, second, third = (ref[288:].astype(F32) for ref in (own, near, back))
    gains[row] = first
    gains[(row + 3) & 3] = second
    gains[(row + 1) & 3] = third
    gains[(row + 2) & 3] = pltpu.roll(third, 14, 0)
    gain = (gains[0] + gains[1]) + (gains[2] + gains[3])
    total = own[:288].astype(F32) + near[:288].astype(F32) + back[:288].astype(F32)
    gain_rows = [
        gain[which : which + 1, part * 128 : (part + 1) * 128]
        for which in range(2)
        for part in range(3)
    ]
    gain_rows.append(jnp.zeros((2, 128), F32))
    for col in range(8):
        start = 96 + 24 * (col // 2)
        block = total[start : start + 24]
        if col % 2:
            block = pltpu.roll(block, 192, 1)
        out_ref[col] = jnp.concatenate(
            [pack_columns(total[:96], col), block[:, :128], block[:, 128:256]]
            + [pack_columns(total[192:288], col)] + gain_rows,
            axis=0,
        ).astype(BF16)


def block_sum(recv_ref, out_ref):
    total = recv_ref[0].astype(F32)
    for place in range(1, 8):
        total = total + recv_ref[place].astype(F32)
    out_ref[...] = total.astype(BF16)


def unpack_columns(packed):
    low = packed[:, :48]
    high = pltpu.roll(packed, 64, 1)[:, :48]
    wide = jnp.concatenate([low, high], axis=0)
    wide = jnp.concatenate([wide, jnp.zeros((96, 80), F32)], axis=1)
    wide = jnp.concatenate([wide, jnp.zeros((32, 128), F32)], axis=0)
    return wide.T[:48]


def final_weights(
    own_ref, other_ref,
    qkv_ref, proj_ref, up_ref, down_ref, first_ref, second_ref, factor,
):
    total = (own_ref[...].astype(F32) + other_ref[...].astype(F32)) * factor
    early, late = total[:96], total[96:]
    up_ref[...] = unpack_columns(early[:48])[:, :96]
    down_ref[:, :128] = early[48:72]
    down_ref[:, 128:] = early[72:96, :64]
    qkv_ref[...] = unpack_columns(late[:48])[:, :72]
    proj_ref[...] = pltpu.roll(late[:48], 64, 1)[24:48, :48]
    for part in range(3):
        lane = pl.ds(part * 128, 128)
        first_ref[lane] = late[48 + part]
        second_ref[lane] = late[51 + part]


def call(kernel, outs, scratch=(), flops=0, nbytes=0, space=pltpu.VMEM, limit=16):
    vmem = pl.BlockSpec(memory_space=pltpu.VMEM)
    scratch = [pltpu.VMEM(*item) if isinstance(item, tuple) else item for item in scratch]

    def run(*args):
        return pl.pallas_call(
            kernel,
            out_shape=[jax.ShapeDtypeStruct(shape, dtype) for shape, dtype in outs],
            in_specs=[pl.BlockSpec(memory_space=space)] * len(args),
            out_specs=[vmem] * len(outs),
            scratch_shapes=scratch,
            compiler_params=pltpu.CompilerParams(vmem_limit_bytes=limit << 20),
            cost_estimate=pl.CostEstimate(flops=flops, bytes_accessed=nbytes, transcendentals=0),
        )(*args)

    return run


def exchange(values, axes):
    return lax.all_to_all(values, axes, split_axis=0, concat_axis=0, tiled=True)


def swap(values, axis):
    return lax.ppermute(values, axis, [(0, 1), (1, 0)])


def shift(values, step):
    return lax.ppermute(values, "y", [(place, (place + step) % 4) for place in range(4)])


def body(tokens, grad_out, gain_first, gain_second, w_qkv, w_proj, w_up, w_down):
    gain_one, gain_two = gain_first.reshape(1, 384), gain_second.reshape(1, 384)
    factor = (8 * 224 * 56) ** -0.5
    tile = pltpu.VMEM((LINES, GRID, 4, 384), BF16)
    (sent,) = call(
        send_kernel,
        [((SLOTS, 8, 384), BF16)],
        [tile, tile, pltpu.SemaphoreType.DMA((2,))],
        nbytes=2 * 10**6,
        space=pl.ANY,
        limit=60,
    )(
        tokens.transpose(1, 2, 0, 3), grad_out.transpose(1, 2, 0, 3)
    )
    arrived = exchange(sent, HA + ("wa",)).reshape(SLOTS * 8, 384)
    rows = ((512, 384), BF16)
    x, qkv, mixed, resid, grad_rows = call(
        forward_kernel,
        [rows, ((512, 1152), BF16), rows, rows, rows],
        [((3, 1024, 128), F32), rows],
        flops=10**9, nbytes=4 * 10**6,
    )(arrived, gain_one, w_qkv, w_proj)
    resid_grad, early_keep, early_send, gain_sum_two = call(
        mlp_kernel,
        [rows, ((8, 192, 384), BF16), ((8, 192, 384), BF16), ((1, 384), F32)],
        [
            rows, ((512, 1536), BF16), ((384, 512), BF16), ((1536, 384), F32), ((384, 1536), F32),
            ((512, 384), F32),
        ],
        flops=3 * 10**9, nbytes=6 * 10**6,
    )(grad_rows, resid, gain_two, w_up, w_down)
    slots, rows_grad, normed, gain_sum_one = call(
        attention_kernel,
        [((SLOTS, 3, 4, 128), BF16), ((512, 1152), BF16), rows, ((1, 384), F32)],
        [rows, ((SLOTS * 12, 128), F32)],
        flops=6 * 10**9, nbytes=20 * 10**6,
    )(x, qkv, resid_grad, gain_one, w_qkv, w_proj)
    returned = exchange(slots, HA + ("wa",))
    late_keep, late_send = call(
        weight_kernel,
        [((8, 112, 384), BF16), ((8, 112, 384), BF16)],
        [((1152, 384), F32), ((384, 384), F32), ((112, 384), F32)],
        flops=10**9, nbytes=5 * 10**6,
    )(rows_grad, normed, resid_grad, mixed, gain_sum_one, gain_sum_two)
    half = ((4, 304, 384), BF16)
    keep, send = call(core_kernel, [half, half], nbytes=10**7)(
        early_keep, swap(early_send, "core"), late_keep, swap(late_send, "core")
    )
    piece = ((304, 384), BF16)
    own, near, back, far_early, far_late = call(
        side_kernel,
        [piece, piece, piece, ((192, 384), BF16), ((112, 384), BF16)],
        nbytes=5 * 10**6,
    )(keep, swap(send, "xl"))
    near, back = call(ring_kernel, [piece, piece], nbytes=2 * 10**6)(
        near, back, shift(far_early, 1), shift(far_late, 3)
    )
    (blocks,) = call(
        pack_kernel, [((8, 152, 128), BF16)], [((4, 16, 384), F32)], nbytes=10**6
    )(own, shift(near, 1), shift(back, 3))
    blocks, returned = lax.optimization_barrier((blocks, returned))
    (total,) = call(block_sum, [((152, 128), BF16)], nbytes=10**6)(exchange(blocks, "wa"))
    other = swap(total, "dp")
    grad_qkv, grad_proj, grad_up, grad_down, first, second = call(
        functools.partial(final_weights, factor=factor),
        [
            ((48, 72), F32), ((24, 48), F32), ((48, 96), F32), ((24, 192), F32),
            ((384,), F32), ((384,), F32),
        ],
        nbytes=10**6,
    )(total, other)
    (grad_tile,) = call(return_kernel, [((LINES, GRID, 4, 384), BF16)], nbytes=10**6)(returned)
    return (
        grad_tile.transpose(2, 0, 1, 3), grad_qkv.T, grad_proj, grad_up.T, grad_down, first, second,
    )


def solution(mesh):
    fine = Mesh(mesh.devices.reshape(4, 2, 2, 8, 2), HA + ("wa", "dp"))
    tile = P("dp", HA, "wa", None)
    block = P(HA, "wa")
    return jax.shard_map(
        body,
        mesh=fine,
        in_specs=(tile, tile, P(), P(), P(), P(), P(), P()),
        out_specs=(tile, block, block, block, block, P(), P()),
        check_vma=False,
    )
```

```python
import functools

import jax
import jax.numpy as jnp
from jax import lax
from jax.experimental import pallas as pl
from jax.experimental.pallas import tpu as pltpu
from jax.sharding import Mesh, PartitionSpec as P

HEADS = 12
GRID = 7
EPSILON = 1e-05
SLOTS = 128
ROWS = 64
LINES = 14
QUAD = 4
F32 = jnp.float32
BF16 = jnp.bfloat16
HA = ("y", "xl", "core")


def dot(left, right):
    return jnp.dot(left, right, preferred_element_type=F32)


def dot_nt(left, right):
    return lax.dot_general(left, right, (((1,), (1,)), ((), ())), preferred_element_type=F32)


def dot_tn(left, right):
    return lax.dot_general(left, right, (((0,), (0,)), ((), ())), preferred_element_type=F32)


def iota(shape, dim):
    return lax.broadcasted_iota(jnp.int32, shape, dim)


def position():
    rows = (lax.axis_index("y") * 2 + lax.axis_index("xl")) * 2 + lax.axis_index("core")
    return rows, lax.axis_index("wa")


def group_match(slot, member):
    row, col = position()
    parity, local = member >> 6, member & 63
    band_row = (local * 37) >> 8
    band_col = local - GRID * band_row
    offset_row = row + 16 * parity + 32 * band_row - LINES * (slot >> 3)
    offset_col = col + 8 * band_col - GRID * (slot & 7)
    hit = jnp.logical_and(offset_row >= 0, offset_row < LINES)
    hit = jnp.logical_and(hit, jnp.logical_and(offset_col >= 0, offset_col < GRID))
    return jnp.logical_and(hit, local < GRID * GRID)


def owner_slot(line, column):
    row, col = position()
    return ((LINES * row + line) & 15) * 8 + ((GRID * col + column) & 7)


def one_hot(hit):
    return jnp.where(hit, 1.0, 0.0).astype(BF16)


def norm_parts(values):
    centered = values - jnp.mean(values, axis=-1, keepdims=True)
    inv_std = lax.rsqrt(jnp.mean(centered * centered, axis=-1, keepdims=True) + EPSILON)
    return centered * inv_std, inv_std


def norm_back(grad, normal_hat, inv_std, gain):
    grad_hat = grad * gain
    first = jnp.mean(grad_hat, axis=-1, keepdims=True)
    second = jnp.mean(grad_hat * normal_hat, axis=-1, keepdims=True)
    return inv_std * (grad_hat - first - normal_hat * second)


def head_mask(shape):
    return (iota(shape, 0) >> 6) == (iota(shape, 1) >> 5)


def spread(values, mask):
    tiled = jnp.concatenate([values] * QUAD, axis=0)
    return jnp.where(mask, tiled, jnp.zeros_like(tiled))


def gather_heads(values):
    lanes = iota((ROWS, 128), 1) >> 5
    total = jnp.where(lanes == 0, values[:ROWS], 0.0)
    for head in range(1, QUAD):
        total = total + jnp.where(lanes == head, values[head * ROWS : (head + 1) * ROWS], 0.0)
    return total


def probabilities(key, query_spread, scale):
    scores = dot_nt(key, query_spread) * scale
    expo = jnp.where(iota(scores.shape, 0) < GRID * GRID, jnp.exp(scores), 0.0)
    return expo * (1.0 / jnp.sum(expo, axis=0, keepdims=True))


def load_every(ref, start, step):
    parts = [ref[part, pl.ds(start, SLOTS, stride=step), :] for part in range(3)]
    return jnp.concatenate(parts, axis=1).astype(BF16)


def send_kernel(tokens_hbm, grad_hbm, out_ref, tokens_ref, grad_ref, sems):
    copies = [
        pltpu.make_async_copy(tokens_hbm, tokens_ref, sems.at[0]),
        pltpu.make_async_copy(grad_hbm, grad_ref, sems.at[1]),
    ]
    for copy in copies:
        copy.start()
    for copy in copies:
        copy.wait()
    for line in range(16):
        for column in range(8):
            slot = owner_slot(line, column)
            if line < LINES and column < GRID:
                unit = jnp.concatenate(
                    [tokens_ref[line, column].astype(F32), grad_ref[line, column].astype(F32)], axis=0
                ).astype(BF16)
            else:
                unit = jnp.zeros((8, 384), BF16)
            out_ref[slot] = unit


def return_kernel(recv_ref, out_ref):
    for line in range(LINES):
        for column in range(GRID):
            slot = owner_slot(line, column)
            for part in range(3):
                out_ref[line, column, :, part * 128 : (part + 1) * 128] = recv_ref[slot, part]


def gelu_parts(hidden, grad):
    inner, cubic = 0.7978845608028654, 0.7978845608028654 * 0.044715
    square = hidden * hidden
    part = 0.5 * jnp.tanh(hidden * (inner + cubic * square)) + 0.5
    twice = hidden * (2 * inner + 6 * cubic * square)
    slope = part * (1.0 + (1.0 - part) * twice)
    return hidden * part, grad * slope


def forward_kernel(
    recv_ref, gain_one, w_qkv, w_proj,
    x_ref, qkv_ref, mixed_ref, resid_ref, grad_ref, arrived, normed,
):
    for part in range(3):
        arrived[part] = recv_ref[:, part * 128 : (part + 1) * 128].astype(F32)
    match = one_hot(group_match(iota((SLOTS, SLOTS), 1), iota((SLOTS, SLOTS), 0)))
    for crop in range(4):
        rows = pl.ds(crop * SLOTS, SLOTS)
        x = dot(match, load_every(arrived, crop, 8))
        x_ref[rows, :] = x.astype(BF16)
        normal_hat, _ = norm_parts(x)
        normed[rows, :] = (normal_hat * gain_one[...]).astype(BF16)
        grad_ref[rows, :] = dot(match, load_every(arrived, crop + 4, 8)).astype(BF16)
    for part in range(3):
        cols = pl.ds(part * 384, 384)
        qkv_ref[:, cols] = dot_nt(normed[...], w_qkv[cols, :]).astype(BF16)
    mask = head_mask((QUAD * ROWS, 128))
    scale = 32.0 ** -0.5

    @pl.loop(0, 1)
    def _(part):
        units = unit_places()
        query = [spread(qkv_ref[rows, pl.ds(lane, 128)], mask) for rows, lane in units]
        probs = [
            probabilities(qkv_ref[rows, pl.ds(384 + lane, 128)], query[n], scale).astype(BF16)
            for n, (rows, lane) in enumerate(units)
        ]
        mixed = [
            dot_tn(probs[n], qkv_ref[rows, pl.ds(768 + lane, 128)])
            for n, (rows, lane) in enumerate(units)
        ]
        for n, (rows, lane) in enumerate(units):
            mixed_ref[rows, pl.ds(lane, 128)] = gather_heads(mixed[n]).astype(BF16)

    for crop in range(4):
        rows = pl.ds(crop * SLOTS, SLOTS)
        branch = dot_nt(mixed_ref[rows, :], w_proj[...]).astype(BF16)
        resid_ref[rows, :] = (x_ref[rows, :].astype(F32) + branch.astype(F32)).astype(BF16)


def unit_places():
    return [(pl.ds(group * ROWS, ROWS), quad * 128) for group in range(8) for quad in range(3)]


def mlp_kernel(
    grad_out, resid, gain_two, w_up, w_down,
    resid_grad_ref, keep_ref, send_ref, gain_ref,
    normed, hidden_grad, grad_turned, up_total, down_total, back,
):
    for crop in range(4):
        rows = pl.ds(crop * SLOTS, SLOTS)
        normal_hat, _ = norm_parts(resid[rows, :].astype(F32))
        normed[rows, :] = (normal_hat * gain_two[...]).astype(BF16)
        grad_turned[:, rows] = grad_out[rows, :].astype(F32).T.astype(BF16)
    for chunk in range(4):
        cols = pl.ds(chunk * 384, 384)
        hidden = dot_nt(normed[...], w_up[cols, :])
        grad_act = dot(grad_out[...], w_down[:, cols])
        activated, grad_hidden = gelu_parts(hidden, grad_act)
        hidden_grad[:, cols] = grad_hidden.astype(BF16)
        down_total[:, cols] = dot(grad_turned[...], activated.astype(BF16))
        up_total[cols, :] = dot_tn(hidden_grad[:, cols], normed[...])
    back[...] = dot(hidden_grad[...], w_up[...])

    for ref, side in piece_sides(keep_ref, send_ref):
        for piece in range(8):
            owner = 2 * piece + side
            ref[piece, :96] = up_total[pl.ds(pl.multiple_of(owner * 96, 8), 96), :].astype(BF16)
            rows = pl.ds(pl.multiple_of(owner * 24, 8), 24)
            ref[piece, 96:] = jnp.concatenate(
                [down_total[rows, part * 384 : (part + 1) * 384] for part in range(4)], axis=0
            ).astype(BF16)
    gain = jnp.zeros((1, 384), F32)
    for crop in range(4):
        rows = pl.ds(crop * SLOTS, SLOTS)
        normal_hat, inv_std = norm_parts(resid[rows, :].astype(F32))
        grad = back[rows, :]
        gain = gain + jnp.sum(grad * normal_hat, axis=0, keepdims=True)
        resid_grad_ref[rows, :] = (
            grad_out[rows, :].astype(F32) + norm_back(grad, normal_hat, inv_std, gain_two[...])
        ).astype(BF16)
    gain_ref[...] = gain


def piece_sides(keep_ref, send_ref):
    core = lax.axis_index("core")
    return (keep_ref, core), (send_ref, 1 - core)


def attention_kernel(
    x_ref, qkv_ref, resid_grad_ref, gain_one, w_qkv, w_proj,
    out_ref, rows_grad, normed_ref, gain_ref, grad_mixed, slots,
):
    grad_mixed[...] = dot(resid_grad_ref[...], w_proj[...]).astype(BF16)
    mask = head_mask((QUAD * ROWS, 128))
    scale = 32.0 ** -0.5

    @pl.loop(0, 1)
    def _(part):
        units = unit_places()
        count = range(len(units))
        query = [spread(qkv_ref[rows, pl.ds(lane, 128)], mask) for rows, lane in units]
        grad = [spread(grad_mixed[rows, pl.ds(lane, 128)], mask) for rows, lane in units]
        key = [qkv_ref[rows, pl.ds(384 + lane, 128)] for rows, lane in units]
        probs = [probabilities(key[n], query[n], scale) for n in count]
        grad_probs = [
            dot_nt(qkv_ref[rows, pl.ds(768 + lane, 128)], grad[n])
            for n, (rows, lane) in enumerate(units)
        ]
        grad_scores = []
        for n in count:
            centre = jnp.sum(grad_probs[n] * probs[n], axis=0, keepdims=True)
            grad_scores.append((probs[n] * (grad_probs[n] - centre) * scale).astype(BF16))
        for n, (rows, lane) in enumerate(units):
            rows_grad[rows, pl.ds(768 + lane, 128)] = dot(probs[n].astype(BF16), grad[n]).astype(BF16)
            rows_grad[rows, pl.ds(384 + lane, 128)] = dot(grad_scores[n], query[n]).astype(BF16)
            rows_grad[rows, pl.ds(lane, 128)] = gather_heads(
                dot_tn(grad_scores[n], key[n])
            ).astype(BF16)

    match = one_hot(group_match(iota((SLOTS, SLOTS), 0), iota((SLOTS, SLOTS), 1)))
    gain = jnp.zeros((1, 384), F32)
    for crop in range(4):
        rows = pl.ds(crop * SLOTS, SLOTS)
        grad = dot(rows_grad[rows, :], w_qkv[...]).astype(BF16).astype(F32)
        normal_hat, inv_std = norm_parts(x_ref[rows, :].astype(F32))
        normed_ref[rows, :] = (normal_hat * gain_one[...]).astype(BF16)
        gain = gain + jnp.sum(grad * normal_hat, axis=0, keepdims=True)
        grad_x = resid_grad_ref[rows, :].astype(F32) + norm_back(
            grad, normal_hat, inv_std, gain_one[...]
        )
        returned = dot(match, grad_x.astype(BF16))
        for part in range(3):
            slots[pl.ds(part * 4 + crop, SLOTS, stride=12), :] = returned[
                :, part * 128 : (part + 1) * 128
            ]
    for slot in range(SLOTS):
        for part in range(3):
            start = slot * 12 + part * 4
            out_ref[slot, part] = slots[start : start + 4, :].astype(BF16)
    gain_ref[...] = gain


def weight_kernel(
    rows_grad, normed, resid_grad, mixed, first, second, keep_ref, send_ref,
    qkv_total, proj_total, piece_rows,
):
    for part in range(3):
        cols = pl.ds(part * 384, 384)
        qkv_total[cols, :] = dot_tn(rows_grad[:, cols], normed[...])
    proj_total[...] = dot_tn(resid_grad[...], mixed[...])
    piece_rows[96:, :] = jnp.zeros((16, 384), F32)
    piece_rows[96:97, :] = first[...]
    piece_rows[97:98, :] = second[...]
    for ref, side in piece_sides(keep_ref, send_ref):
        for piece in range(8):
            owner = 2 * piece + side
            piece_rows[:72, :] = qkv_total[pl.ds(pl.multiple_of(owner * 72, 8), 72), :]
            piece_rows[72:96, :] = proj_total[pl.ds(pl.multiple_of(owner * 24, 8), 24), :]
            ref[piece] = piece_rows[...].astype(BF16)


def core_kernel(keep_ref, recv_ref, out_keep, out_send):
    row, col = lax.axis_index("y"), lax.axis_index("xl")
    for ref, side in ((out_keep, col), (out_send, 1 - col)):
        for step in range(4):
            piece = ((row + step) & 3) * 2 + side
            ref[step] = (keep_ref[piece].astype(F32) + recv_ref[piece].astype(F32)).astype(BF16)


def side_kernel(
    early_keep, early_recv, late_keep, late_recv, own, near, back, far_early, far_late,
):
    for step, ref in ((0, own), (1, near), (3, back)):
        early = early_keep[step].astype(F32) + early_recv[step].astype(F32)
        late = late_keep[step].astype(F32) + late_recv[step].astype(F32)
        ref[:192] = early.astype(BF16)
        ref[192:] = late.astype(BF16)
    far_early[...] = (early_keep[2].astype(F32) + early_recv[2].astype(F32)).astype(BF16)
    late = late_keep[2].astype(F32) + late_recv[2].astype(F32)
    far_late[:96] = late[:96].astype(BF16)
    far_late[96:] = pltpu.roll(late[96:], 2, 0).astype(BF16)


def ring_kernel(near, back, far_early, far_late, out_near, out_back):
    out_near[:192] = (near[:192].astype(F32) + far_early[...].astype(F32)).astype(BF16)
    out_near[192:] = near[192:]
    out_back[:192] = back[:192]
    out_back[192:] = (back[192:].astype(F32) + far_late[...].astype(F32)).astype(BF16)


def pack_columns(rows, col):
    low = pltpu.roll(rows[:48], (384 - 48 * col) % 384, 1)[:, :128]
    high = pltpu.roll(rows[48:96], (384 + 64 - 48 * col) % 384, 1)[:, :128]
    return jnp.where(iota((48, 128), 1) < 64, low, high)


def pack_kernel(own, near, back, out_ref, gains):
    row = lax.axis_index("y")
    first, second, third = (ref[288:].astype(F32) for ref in (own, near, back))
    gains[row] = first
    gains[(row + 3) & 3] = second
    gains[(row + 1) & 3] = third
    gains[(row + 2) & 3] = pltpu.roll(third, 14, 0)
    gain = (gains[0] + gains[1]) + (gains[2] + gains[3])
    total = own[:288].astype(F32) + near[:288].astype(F32) + back[:288].astype(F32)
    gain_rows = [
        gain[which : which + 1, part * 128 : (part + 1) * 128]
        for which in range(2)
        for part in range(3)
    ]
    gain_rows.append(jnp.zeros((2, 128), F32))
    for col in range(8):
        start = 96 + 24 * (col // 2)
        block = total[start : start + 24]
        if col % 2:
            block = pltpu.roll(block, 192, 1)
        out_ref[col] = jnp.concatenate(
            [pack_columns(total[:96], col), block[:, :128], block[:, 128:256]]
            + [pack_columns(total[192:288], col)] + gain_rows,
            axis=0,
        ).astype(BF16)


def block_sum(recv_ref, out_ref):
    total = recv_ref[0].astype(F32)
    for place in range(1, 8):
        total = total + recv_ref[place].astype(F32)
    out_ref[...] = total.astype(BF16)


def unpack_columns(packed):
    low = packed[:, :48]
    high = pltpu.roll(packed, 64, 1)[:, :48]
    wide = jnp.concatenate([low, high], axis=0)
    wide = jnp.concatenate([wide, jnp.zeros((96, 80), F32)], axis=1)
    wide = jnp.concatenate([wide, jnp.zeros((32, 128), F32)], axis=0)
    return wide.T[:48]


def final_weights(
    own_ref, other_ref,
    qkv_ref, proj_ref, up_ref, down_ref, first_ref, second_ref, factor,
):
    total = (own_ref[...].astype(F32) + other_ref[...].astype(F32)) * factor
    early, late = total[:96], total[96:]
    up_ref[...] = unpack_columns(early[:48])[:, :96]
    down_ref[:, :128] = early[48:72]
    down_ref[:, 128:] = early[72:96, :64]
    qkv_ref[...] = unpack_columns(late[:48])[:, :72]
    proj_ref[...] = pltpu.roll(late[:48], 64, 1)[24:48, :48]
    for part in range(3):
        lane = pl.ds(part * 128, 128)
        first_ref[lane] = late[48 + part]
        second_ref[lane] = late[51 + part]


def call(kernel, outs, scratch=(), flops=0, nbytes=0, space=pltpu.VMEM, limit=16):
    vmem = pl.BlockSpec(memory_space=pltpu.VMEM)
    scratch = [pltpu.VMEM(*item) if isinstance(item, tuple) else item for item in scratch]

    def run(*args):
        return pl.pallas_call(
            kernel,
            out_shape=[jax.ShapeDtypeStruct(shape, dtype) for shape, dtype in outs],
            in_specs=[pl.BlockSpec(memory_space=space)] * len(args),
            out_specs=[vmem] * len(outs),
            scratch_shapes=scratch,
            compiler_params=pltpu.CompilerParams(vmem_limit_bytes=limit << 20),
            cost_estimate=pl.CostEstimate(flops=flops, bytes_accessed=nbytes, transcendentals=0),
        )(*args)

    return run


def exchange(values, axes):
    return lax.all_to_all(values, axes, split_axis=0, concat_axis=0, tiled=True)


def swap(values, axis):
    return lax.ppermute(values, axis, [(0, 1), (1, 0)])


def side_pieces(keep, recv):
    half = ((4, keep.shape[1], 384), BF16)
    return call(core_kernel, [half, half], nbytes=4 * 10**6)(keep, recv)


def shift(values, step):
    return lax.ppermute(values, "y", [(place, (place + step) % 4) for place in range(4)])


def body(tokens, grad_out, gain_first, gain_second, w_qkv, w_proj, w_up, w_down):
    gain_one, gain_two = gain_first.reshape(1, 384), gain_second.reshape(1, 384)
    factor = (8 * 224 * 56) ** -0.5
    tile = pltpu.VMEM((LINES, GRID, 4, 384), BF16)
    (sent,) = call(
        send_kernel,
        [((SLOTS, 8, 384), BF16)],
        [tile, tile, pltpu.SemaphoreType.DMA((2,))],
        nbytes=2 * 10**6,
        space=pl.ANY,
        limit=60,
    )(
        tokens.transpose(1, 2, 0, 3), grad_out.transpose(1, 2, 0, 3)
    )
    arrived = exchange(sent, HA + ("wa",)).reshape(SLOTS * 8, 384)
    rows = ((512, 384), BF16)
    x, qkv, mixed, resid, grad_rows = call(
        forward_kernel,
        [rows, ((512, 1152), BF16), rows, rows, rows],
        [((3, 1024, 128), F32), rows],
        flops=10**9, nbytes=4 * 10**6,
    )(arrived, gain_one, w_qkv, w_proj)
    resid_grad, early_keep, early_send, gain_sum_two = call(
        mlp_kernel,
        [rows, ((8, 192, 384), BF16), ((8, 192, 384), BF16), ((1, 384), F32)],
        [
            rows, ((512, 1536), BF16), ((384, 512), BF16), ((1536, 384), F32), ((384, 1536), F32),
            ((512, 384), F32),
        ],
        flops=3 * 10**9, nbytes=6 * 10**6,
    )(grad_rows, resid, gain_two, w_up, w_down)
    slots, rows_grad, normed, gain_sum_one = call(
        attention_kernel,
        [((SLOTS, 3, 4, 128), BF16), ((512, 1152), BF16), rows, ((1, 384), F32)],
        [rows, ((SLOTS * 12, 128), F32)],
        flops=6 * 10**9, nbytes=20 * 10**6,
    )(x, qkv, resid_grad, gain_one, w_qkv, w_proj)
    returned = exchange(slots, HA + ("wa",))
    early = side_pieces(early_keep, swap(early_send, "core"))
    rows_grad, *early = lax.optimization_barrier((rows_grad, *early))
    late_keep, late_send = call(
        weight_kernel,
        [((8, 112, 384), BF16), ((8, 112, 384), BF16)],
        [((1152, 384), F32), ((384, 384), F32), ((112, 384), F32)],
        flops=10**9, nbytes=5 * 10**6, limit=8,
    )(rows_grad, normed, resid_grad, mixed, gain_sum_one, gain_sum_two)
    late = side_pieces(late_keep, swap(late_send, "core"))
    piece = ((304, 384), BF16)
    own, near, back, far_early, far_late = call(
        side_kernel,
        [piece, piece, piece, ((192, 384), BF16), ((112, 384), BF16)],
        nbytes=5 * 10**6,
    )(early[0], swap(early[1], "xl"), late[0], swap(late[1], "xl"))
    near, back = call(ring_kernel, [piece, piece], nbytes=2 * 10**6)(
        near, back, shift(far_early, 1), shift(far_late, 3)
    )
    (blocks,) = call(
        pack_kernel, [((8, 152, 128), BF16)], [((4, 16, 384), F32)], nbytes=10**6
    )(own, shift(near, 1), shift(back, 3))
    blocks, returned = lax.optimization_barrier((blocks, returned))
    (total,) = call(block_sum, [((152, 128), BF16)], nbytes=10**6)(exchange(blocks, "wa"))
    other = swap(total, "dp")
    grad_qkv, grad_proj, grad_up, grad_down, first, second = call(
        functools.partial(final_weights, factor=factor),
        [
            ((48, 72), F32), ((24, 48), F32), ((48, 96), F32), ((24, 192), F32),
            ((384,), F32), ((384,), F32),
        ],
        nbytes=10**6,
    )(total, other)
    (grad_tile,) = call(return_kernel, [((LINES, GRID, 4, 384), BF16)], nbytes=10**6)(returned)
    return (
        grad_tile.transpose(2, 0, 1, 3), grad_qkv.T, grad_proj, grad_up.T, grad_down, first, second,
    )


def solution(mesh):
    fine = Mesh(mesh.devices.reshape(4, 2, 2, 8, 2), HA + ("wa", "dp"))
    tile = P("dp", HA, "wa", None)
    block = P(HA, "wa")
    return jax.shard_map(
        body,
        mesh=fine,
        in_specs=(tile, tile, P(), P(), P(), P(), P(), P()),
        out_specs=(tile, block, block, block, block, P(), P()),
        check_vma=False,
    )
```
